128 devices in a mesh: wide: 32 (over x_hi, y, z), narrow: 4 (over x_lo, core).
Axes of the slice: x: 4 (x_hi: 2, x_lo: 2; x = x_hi * 2 + x_lo), y: 4, z: 4, core: 2. Of those that a mesh axis runs over, the one named last changes fastest.
Arguments:
- tokens: bfloat16 [128, 257, 1664], P(('wide', 'narrow')), may hold values from -6 to 6
- cotangent: bfloat16 [128, 257, 1664], P(('wide', 'narrow')), may hold values from -24 to 24
- ln_gain: float32 [1664], replicated, may hold values from 0.1 to 1.9
- w_qkv: bfloat16 [4992, 1664], replicated, may hold values from -6 to 6, as said below
- w_out: bfloat16 [1664, 1664], replicated, may hold values from -0.15625 to 0.15625
Outputs:
- grad_input: bfloat16 [128, 257, 1664], P(('wide', 'narrow'))
- grad_qkv: float32 [4992, 1664], P('wide')
- grad_out: float32 [1664, 1664], P('wide')
- grad_gain: float32 [1664], replicated
The draws below stay inside these ranges and needn't reach their ends.
Inputs may be any that keep to these rules, and one draw needn't show every extreme that they name: `w_qkv`: rows [0, 1664) project to queries, [1664, 3328) to keys, the rest to values.
All inputs are finite; a program needn't handle non-finite values.
Results may differ from the reference program's by a relative error of at most 0.03.
Values may be sent and summed in bfloat16 or wider, within the bound.
A program may use at most 128 MiB of HBM per device.

```python
import jax
import jax.numpy as jnp
from jax import lax

D = 1664
HEADS = 16
TOK = 257
IMAGES = 128


def draw_w_qkv(key, part):
    key = jax.random.fold_in(key, 11)
    key_base = jax.random.fold_in(key, 1)
    scale_base = D ** (-0.5)
    base = jnp.clip(jax.random.normal(key_base, (3 * D, D), jnp.float32), -6.0, 6.0) * scale_base
    return base.astype(jnp.bfloat16)


def spiked(drawn, stream_key, source, target, blocks, factor):
    owner, partner = [(jnp.arange(drawn.shape[position]) // (drawn.shape[position] // blocks)).reshape([-1 if axis == position else 1 for axis in range(drawn.ndim)]) for position in (source, target)]
    chosen = jax.random.permutation(stream_key, blocks)[partner]
    strong = (owner == chosen) | (owner == (partner + blocks // 2) % blocks)
    return jnp.where(strong, factor * drawn, drawn)


def levels(stream_key, extent, pieces, smallest, largest):
    gain, own = 1.0, jax.random.fold_in(stream_key, 6)
    for dim, shards_of in pieces:
        heights = jnp.exp(jax.random.uniform(jax.random.fold_in(own, dim), (shards_of,), jnp.float32, smallest / len(pieces), largest / len(pieces)))
        gain = gain * jnp.repeat(heights, extent[dim] // shards_of).reshape([-1 if axis == dim else 1 for axis in range(len(extent))])
    return gain


def normal_values(own_key, dims, scale, limit, cuts=(), dtype=jnp.bfloat16):
    drawn = scale * jax.random.normal(own_key, dims, jnp.float32)
    if cuts:
        drawn = drawn * levels(own_key, dims, cuts, -0.22, 0.18)
    return jnp.clip(drawn, -limit, limit).astype(dtype)


def noise_with(stream_key, dims, scale, reach, pieces, heavy, held_as=jnp.bfloat16):
    array = scale * jax.random.normal(stream_key, dims, jnp.float32)
    if pieces:
        array = array * levels(stream_key, dims, pieces, -0.22, 0.18)
    return jnp.clip(spiked(array, jax.random.fold_in(stream_key, 3), *heavy), -reach, reach).astype(held_as)


def setup_inputs(seed: int = 0) -> dict:
    keys = jax.random.split(jax.random.key(seed), 6)
    return {
        "tokens": normal_values(keys[0], (IMAGES, TOK, D), 1.0, 6.0, ((0, 128),)),
        "cotangent": noise_with(keys[1], (IMAGES, TOK, D), 1.0, 24.0, ((0, 128),), (0, 2, 128, 5.5)),
        "ln_gain": jnp.clip(1.0 + 0.18 * jax.random.normal(keys[2], (D,), jnp.float32), 0.1, 1.9),
        "w_qkv": draw_w_qkv(jax.random.fold_in(keys[5], 71), 0),
        "w_out": normal_values(keys[4], (D, D), D ** -0.5, 0.15625),
    }


ln_epsilon = 1e-06

def block_backward(x_in, grad_y, ln_gain, w_qkv, w_out):
    seq_len = x_in.shape[0]
    model_width = x_in.shape[1]
    head_dim = model_width // HEADS
    factor = 1.0 / jnp.sqrt(jnp.float32(head_dim))
    x_float = x_in.astype(jnp.float32)
    x_mean = lax.optimization_barrier(jnp.mean(x_float, axis=-1, keepdims=True))
    centered = x_float - x_mean
    variance = lax.optimization_barrier(jnp.mean(centered * centered, axis=-1, keepdims=True))
    inv_sigma = lax.rsqrt(variance + ln_epsilon)
    normed = centered * inv_sigma
    ln_out = (normed * ln_gain).astype(jnp.bfloat16)
    qkv_proj = lax.dot_general(ln_out, w_qkv, (((1,), (1,)), ((), ())), preferred_element_type=jnp.float32).astype(jnp.bfloat16)
    queries = qkv_proj[:, :model_width].reshape(seq_len, HEADS, head_dim).astype(jnp.float32)
    keys_all = qkv_proj[:, model_width:2 * model_width].reshape(seq_len, HEADS, head_dim).astype(jnp.float32)
    values_all = qkv_proj[:, 2 * model_width:].reshape(seq_len, HEADS, head_dim).astype(jnp.float32)
    scores = jnp.einsum('qhd,khd->hqk', queries, keys_all) * factor
    row_max = lax.optimization_barrier(jnp.max(scores, axis=-1, keepdims=True))
    expo = jnp.exp(scores - row_max)
    prob = expo / lax.optimization_barrier(jnp.sum(expo, axis=-1, keepdims=True))
    prob_low = prob.astype(jnp.bfloat16)
    attn_out = jnp.einsum('hqk,khd->qhd', prob_low.astype(jnp.float32), values_all).reshape(seq_len, model_width).astype(jnp.bfloat16)
    grad_attn = jnp.dot(grad_y, w_out, preferred_element_type=jnp.float32).astype(jnp.bfloat16)
    grad_heads = grad_attn.reshape(seq_len, HEADS, head_dim).astype(jnp.float32)
    grad_prob = jnp.einsum('qhd,khd->hqk', grad_heads, values_all)
    inner_sum = lax.optimization_barrier(jnp.sum(grad_prob * prob, axis=-1, keepdims=True))
    grad_score = (prob * (grad_prob - inner_sum) * factor).astype(jnp.bfloat16).astype(jnp.float32)
    grad_query = jnp.einsum('hqk,khd->qhd', grad_score, keys_all).astype(jnp.bfloat16)
    grad_key = jnp.einsum('hqk,qhd->khd', grad_score, queries).astype(jnp.bfloat16)
    grad_value = jnp.einsum('hqk,qhd->khd', prob_low.astype(jnp.float32), grad_heads).astype(jnp.bfloat16)
    grad_proj = jnp.concatenate([grad_query.reshape(seq_len, model_width), grad_key.reshape(seq_len, model_width), grad_value.reshape(seq_len, model_width)], axis=1)
    grad_ln = jnp.dot(grad_proj, w_qkv, preferred_element_type=jnp.float32)
    grad_gain = lax.optimization_barrier(jnp.sum(grad_ln * normed, axis=0))
    scaled = grad_ln * ln_gain
    grad_x = inv_sigma * (scaled - lax.optimization_barrier(jnp.mean(scaled, axis=-1, keepdims=True)) - normed * lax.optimization_barrier(jnp.mean(scaled * normed, axis=-1, keepdims=True)))
    grad_input = (grad_y.astype(jnp.float32) + grad_x).astype(jnp.bfloat16)
    return (grad_input, ln_out, attn_out, grad_proj, grad_gain)

def reference(tokens, cotangent, ln_gain, w_qkv, w_out):
    images = tokens.shape[0]
    factor = 1.0 / images

    def one_image(carry, pair):
        sum_qkv, sum_out, sum_gain = carry
        x_in, grad_y = pair
        grad_input, ln_out, attn_out, grad_proj, grad_gain = block_backward(x_in, grad_y, ln_gain, w_qkv, w_out)
        part_qkv = lax.dot_general(grad_proj, ln_out, (((0,), (0,)), ((), ())), preferred_element_type=jnp.float32)
        part_out = lax.dot_general(grad_y, attn_out, (((0,), (0,)), ((), ())), preferred_element_type=jnp.float32)
        low_qkv = lax.optimization_barrier((part_qkv * factor).astype(jnp.bfloat16))
        low_out = lax.optimization_barrier((part_out * factor).astype(jnp.bfloat16))
        return ((sum_qkv + low_qkv.astype(jnp.float32), sum_out + low_out.astype(jnp.float32), sum_gain + grad_gain), grad_input)
    width = tokens.shape[2]
    start = (jnp.zeros((3 * width, width), jnp.float32), jnp.zeros((width, width), jnp.float32), jnp.zeros((width,), jnp.float32))
    totals, grad_input = lax.scan(one_image, start, (tokens, cotangent))
    return (grad_input, totals[0], totals[1], totals[2] * factor)
```

```python
import functools

import jax
import jax.numpy as jnp
from jax import lax
from jax.experimental import pallas as pl
from jax.experimental.pallas import tpu as pltpu
from jax.sharding import PartitionSpec as P

HEADS = 16


ln_epsilon = 1e-06


def block_backward(x_in, grad_y, ln_gain, w_qkv, w_out):
    seq_len = x_in.shape[0]
    model_width = x_in.shape[1]
    head_dim = model_width // HEADS
    factor = 1.0 / jnp.sqrt(jnp.float32(head_dim))
    x_float = x_in.astype(jnp.float32)
    x_mean = jnp.mean(x_float, axis=-1, keepdims=True)
    centered = x_float - x_mean
    variance = jnp.mean(centered * centered, axis=-1, keepdims=True)
    inv_sigma = lax.rsqrt(variance + ln_epsilon)
    normed = centered * inv_sigma
    ln_out = (normed * ln_gain).astype(jnp.bfloat16)
    qkv_proj = lax.dot_general(
        ln_out, w_qkv, (((1,), (1,)), ((), ())), preferred_element_type=jnp.float32
    ).astype(jnp.bfloat16)
    queries = qkv_proj[:, :model_width].reshape(seq_len, HEADS, head_dim)
    keys_all = qkv_proj[:, model_width : 2 * model_width].reshape(seq_len, HEADS, head_dim)
    values_all = qkv_proj[:, 2 * model_width :].reshape(seq_len, HEADS, head_dim)
    scores = (
        jnp.einsum("qhd,khd->hqk", queries, keys_all, preferred_element_type=jnp.float32) * factor
    )
    row_max = jnp.max(scores, axis=-1, keepdims=True)
    expo = jnp.exp(scores - row_max)
    prob = expo / jnp.sum(expo, axis=-1, keepdims=True)
    prob_low = prob.astype(jnp.bfloat16)
    attn_out = (
        jnp.einsum("hqk,khd->qhd", prob_low, values_all, preferred_element_type=jnp.float32)
        .reshape(seq_len, model_width)
        .astype(jnp.bfloat16)
    )
    grad_attn = jnp.dot(grad_y, w_out, preferred_element_type=jnp.float32).astype(jnp.bfloat16)
    grad_heads = grad_attn.reshape(seq_len, HEADS, head_dim)
    grad_prob = jnp.einsum(
        "qhd,khd->hqk", grad_heads, values_all, preferred_element_type=jnp.float32
    )
    inner_sum = jnp.sum(grad_prob * prob, axis=-1, keepdims=True)
    grad_score = (prob * (grad_prob - inner_sum) * factor).astype(jnp.bfloat16)
    grad_query = jnp.einsum(
        "hqk,khd->qhd", grad_score, keys_all, preferred_element_type=jnp.float32
    ).astype(jnp.bfloat16)
    grad_key = jnp.einsum(
        "hqk,qhd->khd", grad_score, queries, preferred_element_type=jnp.float32
    ).astype(jnp.bfloat16)
    grad_value = jnp.einsum(
        "hqk,qhd->khd", prob_low, grad_heads, preferred_element_type=jnp.float32
    ).astype(jnp.bfloat16)
    grad_proj = jnp.concatenate(
        [
            grad_query.reshape(seq_len, model_width),
            grad_key.reshape(seq_len, model_width),
            grad_value.reshape(seq_len, model_width),
        ],
        axis=1,
    )
    grad_ln = jnp.dot(grad_proj, w_qkv, preferred_element_type=jnp.float32)
    grad_gain = jnp.sum(grad_ln * normed, axis=0)
    scaled = grad_ln * ln_gain
    grad_x = inv_sigma * (
        scaled
        - jnp.mean(scaled, axis=-1, keepdims=True)
        - normed * jnp.mean(scaled * normed, axis=-1, keepdims=True)
    )
    grad_input = (grad_y.astype(jnp.float32) + grad_x).astype(jnp.bfloat16)
    return (grad_input, ln_out, attn_out, grad_proj, grad_gain)


BLOCKS = 32
ROWS = 208
Q_ROWS = 156
PARTS = ((0, 80), (80, 64), (144, 64))
CUTS = (48, 32, 32)


def rem(a, b):
    return lax.rem(a, jnp.int32(b))


def div(a, b):
    return lax.div(a, jnp.int32(b))


def reduce_kernel(factor, lt, lno, ao, gain_in, out, gain_out,
                  S, R0, T0, A1, A2, A3, B1, B2, B3, E1, E2, E3, C1, C2, C3, T1, F, G,
                  s0, r0, s1, r1, s2, r2, s3, r3, s4, r4, sg, rg):
    cols = lno.shape[1]
    wide, narrow = lax.axis_index("wide"), lax.axis_index("narrow")
    xh, y, z = div(wide, 16), rem(div(wide, 4), 4), rem(wide, 4)
    xl, c = div(narrow, 2), rem(narrow, 2)
    x = 2 * xh + xl

    def device(x_, y_, z_, c_):
        return (div(x_, 2) * 16 + y_ * 4 + z_, rem(x_, 2) * 2 + c_)

    def shift(dim, by):
        at = [x, y, z]
        at[dim] = rem(at[dim] + by, 4)
        return device(*at, c)

    place = (x, y, z)
    mate = device(x, y, z, 1 - c)
    peers = [mate] + [shift(d, by) for d in range(3) for by in (1, 2, 3)]
    barrier = pltpu.get_barrier_semaphore()
    for peer in peers:
        pl.semaphore_signal(barrier, inc=1, device_id=peer, device_id_type=pl.DeviceIdType.MESH)
    pl.semaphore_wait(barrier, len(peers))

    sent = []

    def send(src, dst, ssem, rsem, to):
        copy = pltpu.make_async_remote_copy(src_ref=src, dst_ref=dst, send_sem=ssem, recv_sem=rsem,
                                            device_id=to, device_id_type=pl.DeviceIdType.MESH)
        copy.start()
        return copy

    def gain_stage(k, n, m, to):
        G[k, m] = gain_out[...] if k else gain_in[...]
        copies = [send(G.at[k, m], G.at[k, m], sg.at[k, r], rg.at[k, r], to(r + 1)) for r in range(n - 1)]
        for copy in copies:
            copy.wait()
        total = G[k, 0]
        for other in range(1, n):
            total = total + G[k, other]
        gain_out[...] = total

    def block_of(b, core):
        bx, by, bz = div(b, 8), rem(div(b, 2), 4), rem(b, 2)
        return bx * 16 + by * 4 + 2 * bz + rem(core + bx + by, 2)

    def fill(dst, b, w):
        top = pl.multiple_of(w * ROWS, 16)
        first = lt[pl.ds(top, 160), :]
        last = lt[pl.ds(pl.multiple_of(top + 144, 16), 64), :]
        row = lax.broadcasted_iota(jnp.int32, (16, 1), 0)
        for lo, hi in ((0, 512), (512, 1024), (1024, cols)):
            p = jnp.dot(first, lno[:, lo:hi], preferred_element_type=jnp.float32) * factor
            q = jnp.dot(last, ao[:, lo:hi], preferred_element_type=jnp.float32) * factor
            dst[b, 0:144, lo:hi] = p[0:144].astype(jnp.bfloat16)
            dst[b, 144:160, lo:hi] = jnp.where(row < Q_ROWS - 144, p[144:160], q[0:16]).astype(jnp.bfloat16)
            dst[b, 160:208, lo:hi] = q[16:64].astype(jnp.bfloat16)

    def core_copy(b):
        return pltpu.make_async_remote_copy(src_ref=T0.at[b], dst_ref=R0.at[b], send_sem=s0.at[b], recv_sem=r0.at[b],
                                            device_id=mate, device_id_type=pl.DeviceIdType.MESH)

    @pl.loop(0, 16)
    def _(b):
        fill(T0, b, block_of(b, 1 - c))
        core_copy(b).start()
        fill(S, b, block_of(b, c))

    def accumulate(dst, *more):
        total = dst[...].astype(jnp.float32)
        for term in more:
            total = total + term[...].astype(jnp.float32)
        dst[...] = total.astype(jnp.bfloat16)

    @pl.loop(0, 16)
    def _(b):
        core_copy(b).wait()
        accumulate(S.at[b], R0.at[b])

    def y_block(t, i):
        return (i // 2) * 8 + t * 2 + i % 2

    def z_block(t, i):
        return (i // 2) * 8 + (2 * (i % 2) + rem(c + t + i // 2, 2)) * 2 + div(t, 2)

    def x_block(t, i):
        return div(t, 2) * 8 + i * 2 + rem(t, 2)

    def yz_block(t):
        return rem(c + y + t, 2) * 8 + y * 2 + div(t, 2)

    def zx_block(t):
        return div(t, 2) * 8 + (2 * rem(t, 2) + rem(c + z + div(t, 2), 2)) * 2 + div(z, 2)

    def xy_block(t):
        return div(x, 2) * 8 + t * 2 + rem(x, 2)

    orders = ((1, 2, 0), (2, 0, 1), (0, 1, 2))
    firsts = (y_block, z_block, x_block)
    seconds = (yz_block, zx_block, xy_block)
    halves1, wholes1 = (A1, B1, E1), (A2, B2, E2)
    later = (A3, B3, E3)

    def part(p, b):
        return S.at[b, pl.ds(*PARTS[p]), :]

    for p in range(3):
        d = orders[p][0]
        m = place[d]
        t = rem(m + 2, 4)
        for i in range(2):
            sent.append(send(part(p, firsts[p](t, i)), halves1[p].at[0, i], s1.at[p, 0, i], r1.at[p, 0, i], shift(d, 1)))
            sent.append(send(part(p, firsts[p](t, 2 + i)), halves1[p].at[1, i], s1.at[p, 1, i], r1.at[p, 1, i], shift(d, 3)))
    step1 = list(sent)

    def pass_on(p, side, i):
        d = orders[p][0]
        t = rem(place[d] + (1 if side == 0 else 3), 4)
        copy = send(part(p, firsts[p](t, i)), wholes1[p].at[side, i], s2.at[p, side, i], r2.at[p, side, i],
                    shift(d, 1 if side == 0 else 3))
        sent.append(copy)
        return copy

    step2 = {}
    for p in range(3):
        for i in range(2):
            step2[p, 0, 2 + i] = pass_on(p, 0, 2 + i)
            step2[p, 1, i] = pass_on(p, 1, i)
    n = 0
    for p in range(3):
        d = orders[p][0]
        for i in range(2):
            for side in range(2):
                step1[n].wait_recv()
                n += 1
                t = rem(place[d] + (1 if side == 0 else 3), 4)
                index = i if side == 0 else 2 + i
                accumulate(part(p, firsts[p](t, index)), halves1[p].at[side, i])
                step2[p, side, index] = pass_on(p, side, index)

    gain_stage(0, 2, c, lambda r: mate)
    gain_stage(1, 4, x, lambda r: shift(0, r))
    gain_stage(2, 4, y, lambda r: shift(1, r))
    gain_stage(3, 4, z, lambda r: shift(2, r))

    step3 = {}
    for p in range(3):
        d, e = orders[p][0], orders[p][1]
        cut, size = CUTS[p], PARTS[p][1]
        low, high = pl.ds(0, cut), pl.ds(cut, size - cut)
        for i in range(4):
            step2[p, 0, i].wait_recv()
            step2[p, 1, i].wait_recv()
            accumulate(part(p, firsts[p](place[d], i)), wholes1[p].at[0, i], wholes1[p].at[1, i])
        m = place[e]
        opposite = part(p, seconds[p](rem(m + 2, 4)))
        right, left = part(p, seconds[p](rem(m + 1, 4))), part(p, seconds[p](rem(m + 3, 4)))
        inbox = later[p]
        for k, (what, rows, slot, by) in enumerate((
                (opposite, low, 0, 1), (opposite, high, 0, 3), (right, high, 1, 1), (left, low, 2, 3))):
            step3[p, k] = send(what.at[rows], inbox.at[slot, rows], s3.at[p, k], r3.at[p, k], shift(e, by))
            sent.append(step3[p, k])
    for p in range(3):
        e = orders[p][1]
        cut, size = CUTS[p], PARTS[p][1]
        low, high = pl.ds(0, cut), pl.ds(cut, size - cut)
        m = place[e]
        right, left = part(p, seconds[p](rem(m + 1, 4))), part(p, seconds[p](rem(m + 3, 4)))
        inbox = later[p]
        for k, (what, rows, slot, by) in enumerate(((right, low, 1, 1), (left, high, 2, 3))):
            step3[p, k].wait_recv()
            accumulate(what.at[rows], inbox.at[0, rows])
            step3[p, 4 + k] = send(what.at[rows], inbox.at[slot, rows], s3.at[p, 4 + k], r3.at[p, 4 + k], shift(e, by))
            sent.append(step3[p, 4 + k])
    mine = []
    for p in range(3):
        e = orders[p][1]
        for k in range(2, 6):
            step3[p, k].wait_recv()
        own = part(p, seconds[p](place[e]))
        accumulate(own, later[p].at[1], later[p].at[2])
        mine.append(own)

    chosen = c == rem(xh + y + z, 2)
    partner = device(2 * xh + 1 - xl, y, z, c)

    def final(p):
        return F.at[pl.ds(*PARTS[p]), :]

    def third(copy_of, slot, p, to):
        return pltpu.make_async_remote_copy(src_ref=copy_of, dst_ref=slot, send_sem=s4.at[p], recv_sem=r4.at[p],
                                            device_id=to, device_id_type=pl.DeviceIdType.MESH)

    outward = device(rem(x + 3 + 2 * xl, 4), y, z, c)
    to_pair = third(mine[0], C1.at[0], 0, outward)
    swap = third(T1, C1.at[1], 1, partner)

    y_to = 2 * xl + rem(c + z + xh, 2)
    z_to = 2 * xl + rem(c + y + xh, 2)
    reach = ((1, 2, C2, y_to, y, lambda: device(x, y_to, z, c)), (2, 5, C3, z_to, z, lambda: device(x, y, z_to, c)))

    @pl.when(jnp.logical_not(chosen))
    def _():
        to_pair.start()

    for p, base, slots, to, at, where in reach:
        for r in range(3):
            @pl.when(rem(at - to + 4, 4) == r + 1)
            def _():
                third(mine[p], slots.at[r], base + r, where()).start()

    @pl.when(chosen)
    def _():
        to_pair.wait_recv()
        T1[...] = (mine[0][...].astype(jnp.float32) + C1[0].astype(jnp.float32)).astype(jnp.bfloat16)
        swap.start()

    share = {1: third(final(1), final(1), 8, partner), 2: third(final(2), final(2), 9, partner)}
    for p, base, slots, to, at, where in reach:
        @pl.when(at == to)
        def _():
            for r in range(3):
                third(mine[p], slots.at[r], base + r, mate).wait_recv()
            total = mine[p][...].astype(jnp.float32)
            for r in range(3):
                total = total + slots[r].astype(jnp.float32)
            F[pl.ds(*PARTS[p]), :] = total.astype(jnp.bfloat16)
            share[p].start()

    give = third(F, F, 10, mate)

    @pl.when(chosen)
    def _():
        swap.wait_recv()
        F[pl.ds(*PARTS[0]), :] = (T1[...].astype(jnp.float32) + C1[1].astype(jnp.float32)).astype(jnp.bfloat16)

    for p, base, slots, to, at, where in reach:
        @pl.when(jnp.logical_and(chosen, at != to))
        def _():
            share[p].wait_recv()

    @pl.when(chosen)
    def _():
        give.start()

    @pl.when(jnp.logical_not(chosen))
    def _():
        give.wait_recv()

    out[...] = F[...].astype(jnp.float32)

    for copy in sent:
        copy.wait_send()

    @pl.when(chosen)
    def _():
        swap.wait_send()
        give.wait_send()

    @pl.when(jnp.logical_not(chosen))
    def _():
        to_pair.wait_send()

    for p, base, slots, to, at, where in reach:
        @pl.when(at == to)
        def _():
            share[p].wait_send()

        for r in range(3):
            @pl.when(rem(at - to + 4, 4) == r + 1)
            def _():
                third(mine[p], slots.at[r], base + r, where()).wait_send()


def reduce_call(lt, lno, ao, gain, factor):
    cols = lno.shape[1]
    bf = lambda *shape: pltpu.VMEM(shape, jnp.bfloat16)
    sizes = [size for _, size in PARTS]
    dma = pltpu.SemaphoreType.DMA
    vm = pl.BlockSpec(memory_space=pltpu.VMEM)
    return pl.pallas_call(
        functools.partial(reduce_kernel, factor),
        out_shape=(jax.ShapeDtypeStruct((ROWS, cols), jnp.float32), jax.ShapeDtypeStruct((8, cols), jnp.float32)),
        in_specs=[vm] * 4,
        out_specs=[vm] * 2,
        scratch_shapes=(
            [bf(16, ROWS, cols)] * 3
            + [x for s in sizes for x in (bf(2, 2, s, cols), bf(2, 4, s, cols), bf(3, s, cols))]
            + [bf(2, sizes[0], cols), bf(3, sizes[1], cols), bf(3, sizes[2], cols), bf(sizes[0], cols), bf(ROWS, cols),
               pltpu.VMEM((4, 4, 8, cols), jnp.float32)]
            + [dma((16,))] * 2 + [dma((3, 2, 2))] * 2 + [dma((3, 2, 4))] * 2 + [dma((3, 6))] * 2 + [dma((11,))] * 2
            + [dma((4, 3))] * 2
        ),
        compiler_params=pltpu.CompilerParams(collective_id=0, has_side_effects=True, vmem_limit_bytes=62 * 2**20),
        cost_estimate=pl.CostEstimate(flops=2 * BLOCKS * ROWS * lno.shape[0] * cols, bytes_accessed=2**24, transcendentals=0),
    )(lt, lno, ao, gain)


def local(tokens, cotangent, ln_gain, w_qkv, w_out):
    local_images = tokens.shape[0]
    images = local_images * lax.axis_size("wide") * lax.axis_size("narrow")
    factor = 1.0 / images
    grad_input, ln_out, attn_out, grad_proj, grad_gain = block_backward(
        tokens[0], cotangent[0], ln_gain, w_qkv, w_out
    )
    width = tokens.shape[2]
    left = jnp.concatenate(
        [grad_proj.T.reshape(BLOCKS, Q_ROWS, -1), cotangent[0].T.reshape(BLOCKS, ROWS - Q_ROWS, -1)], axis=1
    ).reshape(BLOCKS * ROWS, -1)
    gain = jnp.zeros((8, width), jnp.float32).at[0].set(grad_gain)
    total, gain = reduce_call(left, ln_out, attn_out, gain, factor)
    return (grad_input[None], total[:Q_ROWS], total[Q_ROWS:], gain[0] * factor)


def solution(mesh):
    return jax.shard_map(
        local,
        mesh=mesh,
        in_specs=(
            P(("wide", "narrow"), None, None),
            P(("wide", "narrow"), None, None),
            P(),
            P(),
            P(),
        ),
        out_specs=(P(("wide", "narrow"), None, None), P("wide", None), P("wide", None), P()),
        check_vma=False,
    )
```

```python
import functools

import jax
import jax.numpy as jnp
from jax import lax
from jax.experimental import pallas as pl
from jax.experimental.pallas import tpu as pltpu
from jax.sharding import PartitionSpec as P

HEADS = 16


ln_epsilon = 1e-06


LANES = 128
WINDOW = 256


def dot(a, b, over=((1,), (0,))):
    return lax.dot_general(a, b, (over, ((), ())), preferred_element_type=jnp.float32)


def low(a):
    return a.astype(jnp.bfloat16)


def normalise(x_ref):
    x = x_ref[...].astype(jnp.float32)
    centered = x - jnp.mean(x, axis=-1, keepdims=True)
    inv_sigma = lax.rsqrt(jnp.mean(centered * centered, axis=-1, keepdims=True) + ln_epsilon)
    return centered * inv_sigma, inv_sigma


def front_kernel(scale, x_ref, cot_ref, gain_ref, w_ref, wo_ref,
                 lno_ref, ao_ref, gt_ref, gx_ref, gg_ref, wpad, gln):
    h = pl.program_id(0)
    dim = w_ref.shape[2]

    @pl.when(h == 0)
    def _():
        normed, _ = normalise(x_ref)
        lno_ref[...] = low(normed * gain_ref[...])
        wpad[...] = jnp.zeros_like(wpad)
        gln[...] = jnp.zeros_like(gln)

    for s in range(3):
        wpad[s * LANES : s * LANES + dim, :] = w_ref[s, 0]
    qkv = low(dot(lno_ref[...], wpad[...], ((1,), (1,))))
    q, k, v = (qkv[:, s * LANES : (s + 1) * LANES] for s in range(3))
    scores = dot(q, k, ((1,), (1,))) * scale
    expo = jnp.exp(scores - jnp.max(scores, axis=-1, keepdims=True))
    prob = expo / jnp.sum(expo, axis=-1, keepdims=True)
    prob_low = low(prob)

    start = jnp.minimum(lax.div(h * dim, LANES) * LANES, wo_ref.shape[1] - WINDOW)
    start = pl.multiple_of(start, LANES)
    offset = h * dim - start
    lane = lax.broadcasted_iota(jnp.int32, (1, WINDOW), 1)
    attn = dot(prob_low, v)
    attn = jnp.concatenate([attn, jnp.zeros_like(attn)], axis=1)
    attn = pltpu.roll(attn, offset, 1)
    window = ao_ref[:, pl.ds(start, WINDOW)].astype(jnp.float32)
    inside = jnp.logical_and(lane >= offset, lane < offset + dim)
    ao_ref[:, pl.ds(start, WINDOW)] = low(jnp.where(inside, attn, window))

    grad = dot(cot_ref[...], wo_ref[:, pl.ds(start, WINDOW)])
    grad = pltpu.roll(grad, lax.rem(WINDOW - offset, WINDOW), 1)[:, :LANES]
    grad = low(jnp.where(lane[:, :LANES] < dim, grad, 0.0))
    grad_prob = dot(grad, v, ((1,), (1,)))
    inner = jnp.sum(grad_prob * prob, axis=-1, keepdims=True)
    grad_score = low(prob * (grad_prob - inner) * scale)

    gq = low(dot(grad_score, k)).astype(jnp.float32)
    gkt = low(dot(q, grad_score, ((0,), (0,)))).astype(jnp.float32)
    gvt = low(dot(grad, prob_low, ((0,), (0,)))).astype(jnp.float32)
    gt_ref[0, 0] = low(gq.T[:dim])
    gt_ref[1, 0] = low(gkt[:dim])
    gt_ref[2, 0] = low(gvt[:dim])
    gcat = low(jnp.concatenate([gq, gkt.T, gvt.T], axis=1))
    gln[...] += dot(gcat, wpad[...])

    @pl.when(h == pl.num_programs(0) - 1)
    def _():
        normed, inv_sigma = normalise(x_ref)
        grad_ln = gln[...]
        total = jnp.sum(grad_ln * normed, axis=0, keepdims=True)
        row = lax.broadcasted_iota(jnp.int32, gg_ref.shape, 0)
        gg_ref[...] = jnp.where(row == 0, total, 0.0)
        g = grad_ln * gain_ref[...]
        grad_x = inv_sigma * (
            g - jnp.mean(g, axis=-1, keepdims=True) - normed * jnp.mean(g * normed, axis=-1, keepdims=True)
        )
        gx_ref[...] = low(cot_ref[...].astype(jnp.float32) + grad_x)


def front_call(x, cot, gain, w_qkv, w_out):
    tok, width = x.shape
    dim = width // HEADS
    whole = lambda a: pl.BlockSpec(a.shape, lambda h: (0,) * len(a.shape))
    w = w_qkv.reshape(3, HEADS, dim, width)
    gain = gain.reshape(1, width)
    outs = (
        jax.ShapeDtypeStruct((tok, width), jnp.bfloat16),
        jax.ShapeDtypeStruct((tok, width), jnp.bfloat16),
        jax.ShapeDtypeStruct((3, HEADS, dim, tok), jnp.bfloat16),
        jax.ShapeDtypeStruct((tok, width), jnp.bfloat16),
        jax.ShapeDtypeStruct((8, width), jnp.float32),
    )
    return pl.pallas_call(
        functools.partial(front_kernel, dim**-0.5),
        grid=(HEADS,),
        out_shape=outs,
        in_specs=[whole(x), whole(cot), whole(gain), pl.BlockSpec((3, 1, dim, width), lambda h: (0, h, 0, 0)), whole(w_out)],
        out_specs=[whole(outs[0]), whole(outs[1]), pl.BlockSpec((3, 1, dim, tok), lambda h: (0, h, 0, 0)), whole(outs[3]), whole(outs[4])],
        scratch_shapes=[pltpu.VMEM((3 * LANES, width), jnp.bfloat16), pltpu.VMEM((tok, width), jnp.float32)],
        compiler_params=pltpu.CompilerParams(vmem_limit_bytes=56 * 2**20, dimension_semantics=("arbitrary",)),
        cost_estimate=pl.CostEstimate(flops=12 * 10**9, bytes_accessed=26 * 2**20, transcendentals=HEADS * tok * tok),
    )(x, cot, gain, w, w_out)


BLOCKS = 32
ROWS = 208
Q_ROWS = 156
PARTS = ((0, 80), (80, 64), (144, 64))
CUTS = (48, 32, 32)


def rem(a, b):
    return lax.rem(a, jnp.int32(b))


def div(a, b):
    return lax.div(a, jnp.int32(b))


def reduce_kernel(factor, gt, ct, lno, ao, gain_in, out, gain_out,
                  S, R0, T0, A1, A2, A3, B1, B2, B3, E1, E2, E3, C1, C2, C3, T1, F, G,
                  s0, r0, s1, r1, s2, r2, s3, r3, s4, r4, sg, rg):
    cols = lno.shape[1]
    wide, narrow = lax.axis_index("wide"), lax.axis_index("narrow")
    xh, y, z = div(wide, 16), rem(div(wide, 4), 4), rem(wide, 4)
    xl, c = div(narrow, 2), rem(narrow, 2)
    x = 2 * xh + xl

    def device(x_, y_, z_, c_):
        return (div(x_, 2) * 16 + y_ * 4 + z_, rem(x_, 2) * 2 + c_)

    def shift(dim, by):
        at = [x, y, z]
        at[dim] = rem(at[dim] + by, 4)
        return device(*at, c)

    place = (x, y, z)
    mate = device(x, y, z, 1 - c)
    peers = [mate] + [shift(d, by) for d in range(3) for by in (1, 2, 3)]
    barrier = pltpu.get_barrier_semaphore()
    for peer in peers:
        pl.semaphore_signal(barrier, inc=1, device_id=peer, device_id_type=pl.DeviceIdType.MESH)
    pl.semaphore_wait(barrier, len(peers))

    sent = []

    def send(src, dst, ssem, rsem, to):
        copy = pltpu.make_async_remote_copy(src_ref=src, dst_ref=dst, send_sem=ssem, recv_sem=rsem,
                                            device_id=to, device_id_type=pl.DeviceIdType.MESH)
        copy.start()
        return copy

    def gain_stage(k, n, m, to):
        G[k, m] = gain_out[...] if k else gain_in[...]
        copies = [send(G.at[k, m], G.at[k, m], sg.at[k, r], rg.at[k, r], to(r + 1)) for r in range(n - 1)]
        for copy in copies:
            copy.wait()
        total = G[k, 0]
        for other in range(1, n):
            total = total + G[k, other]
        gain_out[...] = total

    def fill(dst, b, left):
        first, last = left[0:160], left[144:208]
        row = lax.broadcasted_iota(jnp.int32, (16, 1), 0)
        for lo, hi in ((0, 512), (512, 1024), (1024, cols)):
            p = jnp.dot(first, lno[:, lo:hi], preferred_element_type=jnp.float32) * factor
            q = jnp.dot(last, ao[:, lo:hi], preferred_element_type=jnp.float32) * factor
            dst[b, 0:144, lo:hi] = p[0:144].astype(jnp.bfloat16)
            dst[b, 144:160, lo:hi] = jnp.where(row < Q_ROWS - 144, p[144:160], q[0:16]).astype(jnp.bfloat16)
            dst[b, 160:208, lo:hi] = q[16:64].astype(jnp.bfloat16)

    def rows_of_pair(b):
        g = jnp.concatenate([gt[3 * b + i].astype(jnp.float32) for i in range(3)], axis=0)
        d = ct[b].astype(jnp.float32)
        out_rows = ROWS - Q_ROWS
        return tuple(
            jnp.concatenate([g[i * Q_ROWS : (i + 1) * Q_ROWS], d[i * out_rows : (i + 1) * out_rows]], axis=0)
            for i in range(2)
        )

    def core_copy(b):
        return pltpu.make_async_remote_copy(src_ref=T0.at[b], dst_ref=R0.at[b], send_sem=s0.at[b], recv_sem=r0.at[b],
                                            device_id=mate, device_id_type=pl.DeviceIdType.MESH)

    @pl.loop(0, 16)
    def _(b):
        even, odd = rows_of_pair(b)
        mine_odd = rem(c + div(b, 8) + rem(div(b, 2), 4), 2) == 1
        fill(T0, b, jnp.where(mine_odd, even, odd).astype(jnp.bfloat16))
        core_copy(b).start()
        fill(S, b, jnp.where(mine_odd, odd, even).astype(jnp.bfloat16))

    def accumulate(dst, *more):
        total = dst[...].astype(jnp.float32)
        for term in more:
            total = total + term[...].astype(jnp.float32)
        dst[...] = total.astype(jnp.bfloat16)

    @pl.loop(0, 16)
    def _(b):
        core_copy(b).wait()
        accumulate(S.at[b], R0.at[b])

    def y_block(t, i):
        return (i // 2) * 8 + t * 2 + i % 2

    def z_block(t, i):
        return (i // 2) * 8 + (2 * (i % 2) + rem(c + t + i // 2, 2)) * 2 + div(t, 2)

    def x_block(t, i):
        return div(t, 2) * 8 + i * 2 + rem(t, 2)

    def yz_block(t):
        return rem(c + y + t, 2) * 8 + y * 2 + div(t, 2)

    def zx_block(t):
        return div(t, 2) * 8 + (2 * rem(t, 2) + rem(c + z + div(t, 2), 2)) * 2 + div(z, 2)

    def xy_block(t):
        return div(x, 2) * 8 + t * 2 + rem(x, 2)

    orders = ((1, 2, 0), (2, 0, 1), (0, 1, 2))
    firsts = (y_block, z_block, x_block)
    seconds = (yz_block, zx_block, xy_block)
    halves1, wholes1 = (A1, B1, E1), (A2, B2, E2)
    later = (A3, B3, E3)

    def part(p, b):
        return S.at[b, pl.ds(*PARTS[p]), :]

    for p in range(3):
        d = orders[p][0]
        m = place[d]
        t = rem(m + 2, 4)
        for i in range(2):
            sent.append(send(part(p, firsts[p](t, i)), halves1[p].at[0, i], s1.at[p, 0, i], r1.at[p, 0, i], shift(d, 1)))
            sent.append(send(part(p, firsts[p](t, 2 + i)), halves1[p].at[1, i], s1.at[p, 1, i], r1.at[p, 1, i], shift(d, 3)))
    step1 = list(sent)

    def pass_on(p, side, i):
        d = orders[p][0]
        t = rem(place[d] + (1 if side == 0 else 3), 4)
        copy = send(part(p, firsts[p](t, i)), wholes1[p].at[side, i], s2.at[p, side, i], r2.at[p, side, i],
                    shift(d, 1 if side == 0 else 3))
        sent.append(copy)
        return copy

    step2 = {}
    for p in range(3):
        for i in range(2):
            step2[p, 0, 2 + i] = pass_on(p, 0, 2 + i)
            step2[p, 1, i] = pass_on(p, 1, i)
    n = 0
    for p in range(3):
        d = orders[p][0]
        for i in range(2):
            for side in range(2):
                step1[n].wait_recv()
                n += 1
                t = rem(place[d] + (1 if side == 0 else 3), 4)
                index = i if side == 0 else 2 + i
                accumulate(part(p, firsts[p](t, index)), halves1[p].at[side, i])
                step2[p, side, index] = pass_on(p, side, index)

    gain_stage(0, 2, c, lambda r: mate)
    gain_stage(1, 4, x, lambda r: shift(0, r))
    gain_stage(2, 4, y, lambda r: shift(1, r))
    gain_stage(3, 4, z, lambda r: shift(2, r))

    step3 = {}
    for p in range(3):
        d, e = orders[p][0], orders[p][1]
        cut, size = CUTS[p], PARTS[p][1]
        low, high = pl.ds(0, cut), pl.ds(cut, size - cut)
        for i in range(4):
            step2[p, 0, i].wait_recv()
            step2[p, 1, i].wait_recv()
            accumulate(part(p, firsts[p](place[d], i)), wholes1[p].at[0, i], wholes1[p].at[1, i])
        m = place[e]
        opposite = part(p, seconds[p](rem(m + 2, 4)))
        right, left = part(p, seconds[p](rem(m + 1, 4))), part(p, seconds[p](rem(m + 3, 4)))
        inbox = later[p]
        for k, (what, rows, slot, by) in enumerate((
                (opposite, low, 0, 1), (opposite, high, 0, 3), (right, high, 1, 1), (left, low, 2, 3))):
            step3[p, k] = send(what.at[rows], inbox.at[slot, rows], s3.at[p, k], r3.at[p, k], shift(e, by))
            sent.append(step3[p, k])
    for p in range(3):
        e = orders[p][1]
        cut, size = CUTS[p], PARTS[p][1]
        low, high = pl.ds(0, cut), pl.ds(cut, size - cut)
        m = place[e]
        right, left = part(p, seconds[p](rem(m + 1, 4))), part(p, seconds[p](rem(m + 3, 4)))
        inbox = later[p]
        for k, (what, rows, slot, by) in enumerate(((right, low, 1, 1), (left, high, 2, 3))):
            step3[p, k].wait_recv()
            accumulate(what.at[rows], inbox.at[0, rows])
            step3[p, 4 + k] = send(what.at[rows], inbox.at[slot, rows], s3.at[p, 4 + k], r3.at[p, 4 + k], shift(e, by))
            sent.append(step3[p, 4 + k])
    mine = []
    for p in range(3):
        e = orders[p][1]
        for k in range(2, 6):
            step3[p, k].wait_recv()
        own = part(p, seconds[p](place[e]))
        accumulate(own, later[p].at[1], later[p].at[2])
        mine.append(own)

    chosen = c == rem(xh + y + z, 2)
    partner = device(2 * xh + 1 - xl, y, z, c)

    def final(p):
        return F.at[pl.ds(*PARTS[p]), :]

    def third(copy_of, slot, p, to):
        return pltpu.make_async_remote_copy(src_ref=copy_of, dst_ref=slot, send_sem=s4.at[p], recv_sem=r4.at[p],
                                            device_id=to, device_id_type=pl.DeviceIdType.MESH)

    outward = device(rem(x + 3 + 2 * xl, 4), y, z, c)
    to_pair = third(mine[0], C1.at[0], 0, outward)
    swap = third(T1, C1.at[1], 1, partner)

    y_to = 2 * xl + rem(c + z + xh, 2)
    z_to = 2 * xl + rem(c + y + xh, 2)
    reach = ((1, 2, C2, y_to, y, lambda: device(x, y_to, z, c)), (2, 5, C3, z_to, z, lambda: device(x, y, z_to, c)))

    @pl.when(jnp.logical_not(chosen))
    def _():
        to_pair.start()

    for p, base, slots, to, at, where in reach:
        for r in range(3):
            @pl.when(rem(at - to + 4, 4) == r + 1)
            def _():
                third(mine[p], slots.at[r], base + r, where()).start()

    @pl.when(chosen)
    def _():
        to_pair.wait_recv()
        T1[...] = (mine[0][...].astype(jnp.float32) + C1[0].astype(jnp.float32)).astype(jnp.bfloat16)
        swap.start()

    share = {1: third(final(1), final(1), 8, partner), 2: third(final(2), final(2), 9, partner)}
    for p, base, slots, to, at, where in reach:
        @pl.when(at == to)
        def _():
            for r in range(3):
                third(mine[p], slots.at[r], base + r, mate).wait_recv()
            total = mine[p][...].astype(jnp.float32)
            for r in range(3):
                total = total + slots[r].astype(jnp.float32)
            F[pl.ds(*PARTS[p]), :] = total.astype(jnp.bfloat16)
            share[p].start()

    give = third(F, F, 10, mate)

    @pl.when(chosen)
    def _():
        swap.wait_recv()
        F[pl.ds(*PARTS[0]), :] = (T1[...].astype(jnp.float32) + C1[1].astype(jnp.float32)).astype(jnp.bfloat16)

    for p, base, slots, to, at, where in reach:
        @pl.when(jnp.logical_and(chosen, at != to))
        def _():
            share[p].wait_recv()

    @pl.when(chosen)
    def _():
        give.start()

    @pl.when(jnp.logical_not(chosen))
    def _():
        give.wait_recv()

    out[...] = F[...].astype(jnp.float32)

    for copy in sent:
        copy.wait_send()

    @pl.when(chosen)
    def _():
        swap.wait_send()
        give.wait_send()

    @pl.when(jnp.logical_not(chosen))
    def _():
        to_pair.wait_send()

    for p, base, slots, to, at, where in reach:
        @pl.when(at == to)
        def _():
            share[p].wait_send()

        for r in range(3):
            @pl.when(rem(at - to + 4, 4) == r + 1)
            def _():
                third(mine[p], slots.at[r], base + r, where()).wait_send()


def reduce_call(gt, ct, lno, ao, gain, factor):
    cols = lno.shape[1]
    bf = lambda *shape: pltpu.VMEM(shape, jnp.bfloat16)
    sizes = [size for _, size in PARTS]
    dma = pltpu.SemaphoreType.DMA
    vm = pl.BlockSpec(memory_space=pltpu.VMEM)
    return pl.pallas_call(
        functools.partial(reduce_kernel, factor),
        out_shape=(jax.ShapeDtypeStruct((ROWS, cols), jnp.float32), jax.ShapeDtypeStruct((8, cols), jnp.float32)),
        in_specs=[vm] * 5,
        out_specs=[vm] * 2,
        scratch_shapes=(
            [bf(16, ROWS, cols)] * 3
            + [x for s in sizes for x in (bf(2, 2, s, cols), bf(2, 4, s, cols), bf(3, s, cols))]
            + [bf(2, sizes[0], cols), bf(3, sizes[1], cols), bf(3, sizes[2], cols), bf(sizes[0], cols), bf(ROWS, cols),
               pltpu.VMEM((4, 4, 8, cols), jnp.float32)]
            + [dma((16,))] * 2 + [dma((3, 2, 2))] * 2 + [dma((3, 2, 4))] * 2 + [dma((3, 6))] * 2 + [dma((11,))] * 2
            + [dma((4, 3))] * 2
        ),
        compiler_params=pltpu.CompilerParams(collective_id=0, has_side_effects=True, vmem_limit_bytes=62 * 2**20),
        cost_estimate=pl.CostEstimate(flops=2 * BLOCKS * ROWS * lno.shape[0] * cols, bytes_accessed=2**24, transcendentals=0),
    )(gt, ct, lno, ao, gain)


def local(tokens, cotangent, ln_gain, w_qkv, w_out):
    images = tokens.shape[0] * lax.axis_size("wide") * lax.axis_size("narrow")
    factor = 1.0 / images
    x, cot = tokens[0], cotangent[0]
    ln_out, attn_out, grad_t, grad_input, gain = front_call(x, cot, ln_gain, w_qkv, w_out)
    cot_t = cot.T.reshape(BLOCKS // 2, -1, cot.shape[0])
    grad_t = grad_t.reshape(BLOCKS * 3 // 2, -1, cot.shape[0])
    total, gain = reduce_call(grad_t, cot_t, ln_out, attn_out, gain, factor)
    return (grad_input[None], total[:Q_ROWS], total[Q_ROWS:], gain[0] * factor)


def solution(mesh):
    return jax.shard_map(
        local,
        mesh=mesh,
        in_specs=(
            P(("wide", "narrow"), None, None),
            P(("wide", "narrow"), None, None),
            P(),
            P(),
            P(),
        ),
        out_specs=(P(("wide", "narrow"), None, None), P("wide", None), P("wide", None), P()),
        check_vma=False,
    )
```

```python
import functools

import jax
import jax.numpy as jnp
from jax import lax
from jax.experimental import pallas as pl
from jax.experimental.pallas import tpu as pltpu
from jax.sharding import PartitionSpec as P

HEADS = 16


ln_epsilon = 1e-06


LANES = 128
WINDOW = 256


def dot(a, b, over=((1,), (0,))):
    return lax.dot_general(a, b, (over, ((), ())), preferred_element_type=jnp.float32)


def low(a):
    return a.astype(jnp.bfloat16)


def normalise(x_ref):
    x = x_ref[...].astype(jnp.float32)
    centered = x - jnp.mean(x, axis=-1, keepdims=True)
    inv_sigma = lax.rsqrt(jnp.mean(centered * centered, axis=-1, keepdims=True) + ln_epsilon)
    return centered * inv_sigma, inv_sigma


def front_kernel(scale, x_ref, cot_ref, gain_ref, w_ref, wo_ref,
                 lno_ref, ao_ref, gt_ref, gx_ref, gg_ref, wpad, gln):
    h = pl.program_id(0)
    dim = w_ref.shape[2]

    @pl.when(h == 0)
    def _():
        normed, _ = normalise(x_ref)
        lno_ref[...] = low(normed * gain_ref[...])
        wpad[...] = jnp.zeros_like(wpad)
        gln[...] = jnp.zeros_like(gln)

    for s in range(3):
        wpad[s * LANES : s * LANES + dim, :] = w_ref[s, 0]
    qkv = low(dot(lno_ref[...], wpad[...], ((1,), (1,))))
    q, k, v = (qkv[:, s * LANES : (s + 1) * LANES] for s in range(3))
    scores = dot(q, k, ((1,), (1,))) * scale
    expo = jnp.exp(scores - jnp.max(scores, axis=-1, keepdims=True))
    prob = expo / jnp.sum(expo, axis=-1, keepdims=True)
    prob_low = low(prob)

    start = jnp.minimum(lax.div(h * dim, LANES) * LANES, wo_ref.shape[1] - WINDOW)
    start = pl.multiple_of(start, LANES)
    offset = h * dim - start
    lane = lax.broadcasted_iota(jnp.int32, (1, WINDOW), 1)
    attn = dot(prob_low, v)
    attn = jnp.concatenate([attn, jnp.zeros_like(attn)], axis=1)
    attn = pltpu.roll(attn, offset, 1)
    window = ao_ref[:, pl.ds(start, WINDOW)].astype(jnp.float32)
    inside = jnp.logical_and(lane >= offset, lane < offset + dim)
    ao_ref[:, pl.ds(start, WINDOW)] = low(jnp.where(inside, attn, window))

    grad = dot(cot_ref[...], wo_ref[:, pl.ds(start, WINDOW)])
    grad = pltpu.roll(grad, lax.rem(WINDOW - offset, WINDOW), 1)[:, :LANES]
    grad = low(jnp.where(lane[:, :LANES] < dim, grad, 0.0))
    grad_prob = dot(grad, v, ((1,), (1,)))
    inner = jnp.sum(grad_prob * prob, axis=-1, keepdims=True)
    grad_score = low(prob * (grad_prob - inner) * scale)

    gq = low(dot(grad_score, k)).astype(jnp.float32)
    gkt = low(dot(q, grad_score, ((0,), (0,)))).astype(jnp.float32)
    gvt = low(dot(grad, prob_low, ((0,), (0,)))).astype(jnp.float32)
    gt_ref[0, 0] = low(gq.T[:dim])
    gt_ref[1, 0] = low(gkt[:dim])
    gt_ref[2, 0] = low(gvt[:dim])
    gcat = low(jnp.concatenate([gq, gkt.T, gvt.T], axis=1))
    gln[...] += dot(gcat, wpad[...])

    @pl.when(h == pl.num_programs(0) - 1)
    def _():
        normed, inv_sigma = normalise(x_ref)
        grad_ln = gln[...]
        total = jnp.sum(grad_ln * normed, axis=0, keepdims=True)
        row = lax.broadcasted_iota(jnp.int32, gg_ref.shape, 0)
        gg_ref[...] = jnp.where(row == 0, total, 0.0)
        g = grad_ln * gain_ref[...]
        grad_x = inv_sigma * (
            g - jnp.mean(g, axis=-1, keepdims=True) - normed * jnp.mean(g * normed, axis=-1, keepdims=True)
        )
        gx_ref[...] = low(cot_ref[...].astype(jnp.float32) + grad_x)


def front_call(x, cot, gain, w_qkv, w_out):
    tok, width = x.shape
    dim = width // HEADS
    whole = lambda a: pl.BlockSpec(a.shape, lambda h: (0,) * len(a.shape))
    w = w_qkv.reshape(3, HEADS, dim, width)
    gain = gain.reshape(1, width)
    outs = (
        jax.ShapeDtypeStruct((tok, width), jnp.bfloat16),
        jax.ShapeDtypeStruct((tok, width), jnp.bfloat16),
        jax.ShapeDtypeStruct((3, HEADS, dim, tok), jnp.bfloat16),
        jax.ShapeDtypeStruct((tok, width), jnp.bfloat16),
        jax.ShapeDtypeStruct((8, width), jnp.float32),
    )
    return pl.pallas_call(
        functools.partial(front_kernel, dim**-0.5),
        grid=(HEADS,),
        out_shape=outs,
        in_specs=[whole(x), whole(cot), whole(gain), pl.BlockSpec((3, 1, dim, width), lambda h: (0, h, 0, 0)), whole(w_out)],
        out_specs=[whole(outs[0]), whole(outs[1]), pl.BlockSpec((3, 1, dim, tok), lambda h: (0, h, 0, 0)), whole(outs[3]), whole(outs[4])],
        scratch_shapes=[pltpu.VMEM((3 * LANES, width), jnp.bfloat16), pltpu.VMEM((tok, width), jnp.float32)],
        compiler_params=pltpu.CompilerParams(vmem_limit_bytes=56 * 2**20, dimension_semantics=("arbitrary",)),
        cost_estimate=pl.CostEstimate(flops=12 * 10**9, bytes_accessed=26 * 2**20, transcendentals=HEADS * tok * tok),
    )(x, cot, gain, w, w_out)


BLOCKS = 32
ROWS = 208
Q_ROWS = 156
PARTS = ((0, 80), (80, 64), (144, 64))
CUTS = (48, 32, 32)
RING = 4
LAG = 2
MESH = pl.DeviceIdType.MESH


def rem(a, b):
    return lax.rem(a, jnp.int32(b))


def div(a, b):
    return lax.div(a, jnp.int32(b))


def column_halves(cols):
    edge = (cols // LANES + 1) // 2 * LANES
    return ((0, edge), (edge, cols))


def reduce_kernel(factor, gt, ct, lno, ao, gain_in, out, gain_out, G, sg, rg, *scratch):
    cols = lno.shape[1]
    spans = column_halves(cols)
    per = len(scratch) // 2
    sides = []
    for h in range(2):
        s = scratch[h * per : (h + 1) * per]
        sides.append(dict(S=s[0], R0=s[1], T0=s[2], halves=(s[3], s[6], s[9]), wholes=(s[4], s[7], s[10]),
                          later=(s[5], s[8], s[11]), C=s[12:15], T1=s[15], F=s[16], sems=s[17:27]))

    wide, narrow = lax.axis_index("wide"), lax.axis_index("narrow")
    xh, y, z = div(wide, 16), rem(div(wide, 4), 4), rem(wide, 4)
    xl, c = div(narrow, 2), rem(narrow, 2)
    x = 2 * xh + xl
    place = (x, y, z)

    def device(x_, y_, z_, c_):
        return (div(x_, 2) * 16 + y_ * 4 + z_, rem(x_, 2) * 2 + c_)

    def shift(dim, by):
        at = [x, y, z]
        at[dim] = rem(at[dim] + by, 4)
        return device(*at, c)

    mate = device(x, y, z, 1 - c)
    peers = [mate] + [shift(d, by) for d in range(3) for by in (1, 2, 3)]
    barrier = pltpu.get_barrier_semaphore()
    for peer in peers:
        pl.semaphore_signal(barrier, inc=1, device_id=peer, device_id_type=MESH)
    pl.semaphore_wait(barrier, len(peers))

    def remote(src, dst, ssem, rsem, to):
        return pltpu.make_async_remote_copy(src_ref=src, dst_ref=dst, send_sem=ssem, recv_sem=rsem,
                                            device_id=to, device_id_type=MESH)

    def accumulate(dst, *more):
        total = dst[...].astype(jnp.float32)
        for term in more:
            total = total + term[...].astype(jnp.float32)
        dst[...] = total.astype(jnp.bfloat16)

    rings = ((2, c, lambda r: mate), (4, x, lambda r: shift(0, r)), (4, y, lambda r: shift(1, r)), (4, z, lambda r: shift(2, r)))
    gain_copies = []

    def gain_start(k):
        n, m, to = rings[k]
        G[k, m] = gain_out[...] if k else gain_in[...]
        for r in range(n - 1):
            copy = remote(G.at[k, m], G.at[k, m], sg.at[k, r], rg.at[k, r], to(r + 1))
            copy.start()
            gain_copies.append(copy)

    def gain_end(k):
        while gain_copies:
            gain_copies.pop().wait()
        total = G[k, 0]
        for other in range(1, rings[k][0]):
            total = total + G[k, other]
        gain_out[...] = total

    def rows_of_pair(b):
        g = jnp.concatenate([gt[3 * b + i].astype(jnp.float32) for i in range(3)], axis=0)
        d = ct[b].astype(jnp.float32)
        out_rows = ROWS - Q_ROWS
        return tuple(
            jnp.concatenate([g[i * Q_ROWS : (i + 1) * Q_ROWS], d[i * out_rows : (i + 1) * out_rows]], axis=0)
            for i in range(2)
        )

    def product(left, right, lo, hi):
        full = right.shape[0] // 256 * 256
        total = dot(low(left[:, :full]), right[0:full, lo:hi])
        for k in range(full, right.shape[0]):
            total = total + left[:, k : k + 1] * right[k : k + 1, lo:hi].astype(jnp.float32)
        return total * factor

    def fill(side, span, b, slot):
        even, odd = rows_of_pair(b)
        mine_odd = rem(c + div(b, 8) + rem(div(b, 2), 4), 2) == 1
        give, keep = jnp.where(mine_odd, even, odd), jnp.where(mine_odd, odd, even)
        first = jnp.concatenate([give[0:160], keep[0:160]], axis=0)
        last = jnp.concatenate([give[144:208], keep[144:208]], axis=0)
        row = lax.broadcasted_iota(jnp.int32, (16, 1), 0)
        width = span[1] - span[0]
        for lo in range(0, width, 512):
            hi = min(width, lo + 512)
            p = product(first, lno, span[0] + lo, span[0] + hi)
            q = product(last, ao, span[0] + lo, span[0] + hi)
            for k, dst, at in ((0, side["T0"], slot), (1, side["S"], b)):
                u, v = p[160 * k : 160 * k + 160], q[64 * k : 64 * k + 64]
                dst[at, 0:144, lo:hi] = low(u[0:144])
                dst[at, 144:160, lo:hi] = low(jnp.where(row < Q_ROWS - 144, u[144:160], v[0:16]))
                dst[at, 160:208, lo:hi] = low(v[16:64])

    def core_copy(side, b, slot):
        return remote(side["T0"].at[slot], side["R0"].at[b], side["sems"][0].at[b], side["sems"][1].at[b], mate)

    def produce(h):
        side = sides[h]

        @pl.loop(0, 16 + LAG)
        def _(n):
            @pl.when(n < 16)
            def _():
                slot = rem(n, RING)

                @pl.when(n >= RING)
                def _():
                    core_copy(side, n - RING, slot).wait_send()

                fill(side, spans[h], n, slot)
                core_copy(side, n, slot).start()

            @pl.when(n >= LAG)
            def _():
                b = n - LAG
                core_copy(side, b, 0).wait_recv()
                accumulate(side["S"].at[b], side["R0"].at[b])

        for n in range(16 - RING, 16):
            core_copy(side, n, n % RING).wait_send()

    orders = ((1, 2, 0), (2, 0, 1), (0, 1, 2))
    firsts = (
        lambda t, i: (i // 2) * 8 + t * 2 + i % 2,
        lambda t, i: (i // 2) * 8 + (2 * (i % 2) + rem(c + t + i // 2, 2)) * 2 + div(t, 2),
        lambda t, i: div(t, 2) * 8 + i * 2 + rem(t, 2),
    )
    seconds = (
        lambda t: (rem(c + y + t, 2) * 8 + y * 2 + div(t, 2), rem(c + y + t, 2) * 2 + div(t, 2)),
        lambda t: (div(t, 2) * 8 + (2 * rem(t, 2) + rem(c + z + div(t, 2), 2)) * 2 + div(z, 2), t),
        lambda t: (div(x, 2) * 8 + t * 2 + rem(x, 2), t),
    )

    def part(h, p, b):
        return sides[h]["S"].at[b, pl.ds(*PARTS[p]), :]

    def half_copy(h, p, to, i, src):
        sems = sides[h]["sems"]
        return remote(src, sides[h]["halves"][p].at[to, i], sems[2].at[p, to, i], sems[3].at[p, to, i],
                      shift(orders[p][0], 1 + 2 * to))

    def whole_copy(h, p, to, i, src):
        sems = sides[h]["sems"]
        return remote(src, sides[h]["wholes"][p].at[to, i], sems[4].at[p, to, i], sems[5].at[p, to, i],
                      shift(orders[p][0], 1 + 2 * to))

    six = [(p, to) for to in range(2) for p in range(3)]

    def first_sends(h):
        for i in range(2):
            for p, to in six:
                t = rem(place[orders[p][0]] + 2, 4)
                half_copy(h, p, to, i, part(h, p, firsts[p](t, i + 2 * to))).start()
        for i in range(2):
            for p, to in six:
                t = rem(place[orders[p][0]] + 1 + 2 * to, 4)
                index = i + 2 - 2 * to
                whole_copy(h, p, to, index, part(h, p, firsts[p](t, index))).start()

    def first_relays(h):
        for i in range(2):
            for p, to in six:
                halves = sides[h]["halves"][p]
                half_copy(h, p, to, i, halves.at[to, i]).wait_recv()
                t = rem(place[orders[p][0]] + 1 + 2 * to, 4)
                index = i + 2 * to
                block = part(h, p, firsts[p](t, index))
                accumulate(block, halves.at[to, i])
                whole_copy(h, p, to, index, block).start()

    def ready(h, p, t):
        b, i = seconds[p](t)
        wholes = sides[h]["wholes"][p]
        for to in range(2):
            whole_copy(h, p, to, i, wholes.at[to, i]).wait_recv()
        accumulate(part(h, p, b), wholes.at[0, i], wholes.at[1, i])
        return part(h, p, b)

    def second_copy(h, p, k, what):
        edge = CUTS[p]
        lower, upper = pl.ds(0, edge), pl.ds(edge, PARTS[p][1] - edge)
        rows, slot, by = ((lower, 0, 1), (upper, 0, 3), (upper, 1, 1), (lower, 2, 3), (lower, 1, 1), (upper, 2, 3))[k]
        sems = sides[h]["sems"]
        return remote(what.at[rows], sides[h]["later"][p].at[slot, rows], sems[6].at[p, k], sems[7].at[p, k],
                      shift(orders[p][1], by))

    def block2(h, p, by):
        return part(h, p, seconds[p](rem(place[orders[p][1]] + by, 4))[0])

    def second_sends(h):
        for p in range(3):
            opposite = ready(h, p, rem(place[orders[p][1]] + 2, 4))
            second_copy(h, p, 0, opposite).start()
            second_copy(h, p, 1, opposite).start()
        for p in range(3):
            second_copy(h, p, 2, ready(h, p, rem(place[orders[p][1]] + 1, 4))).start()
            second_copy(h, p, 3, ready(h, p, rem(place[orders[p][1]] + 3, 4))).start()

    def second_relays(h):
        for p in range(3):
            edge = CUTS[p]
            inbox = sides[h]["later"][p]
            for k, by, rows in ((0, 1, pl.ds(0, edge)), (1, 3, pl.ds(edge, PARTS[p][1] - edge))):
                what = block2(h, p, by)
                second_copy(h, p, k, what).wait_recv()
                accumulate(what.at[rows], inbox.at[0, rows])
                second_copy(h, p, 4 + k, what).start()
        for p in range(3):
            ready(h, p, place[orders[p][1]])

    chosen = c == rem(xh + y + z, 2)
    partner = device(2 * xh + 1 - xl, y, z, c)
    outward = device(rem(x + 3 + 2 * xl, 4), y, z, c)
    y_to = 2 * xl + rem(c + z + xh, 2)
    z_to = 2 * xl + rem(c + y + xh, 2)
    reach = ((1, 2, y_to, y, lambda: device(x, y_to, z, c)), (2, 5, z_to, z, lambda: device(x, y, z_to, c)))

    def third(h, src, dst, k, to):
        sems = sides[h]["sems"]
        return remote(src, dst, sems[8].at[k], sems[9].at[k], to)

    def mine(h, p):
        return block2(h, p, 0)

    def final(h, p):
        return sides[h]["F"].at[pl.ds(*PARTS[p]), :]

    def to_pair(h):
        return third(h, mine(h, 0), sides[h]["C"][0].at[0], 0, outward)

    def swap(h):
        return third(h, sides[h]["T1"], sides[h]["C"][0].at[1], 1, partner)

    def share(h, p):
        return third(h, final(h, p), final(h, p), 7 + p, partner)

    def hand(h):
        return third(h, sides[h]["F"], sides[h]["F"], 10, mate)

    def third_sends(h):
        for p in range(3):
            for k in range(2, 6):
                second_copy(h, p, k, mine(h, p)).wait_recv()
            accumulate(mine(h, p), sides[h]["later"][p].at[1], sides[h]["later"][p].at[2])
            if p == 0:
                @pl.when(jnp.logical_not(chosen))
                def _():
                    to_pair(h).start()
            else:
                _, base, to, at, where = reach[p - 1]
                for r in range(3):
                    @pl.when(rem(at - to + 4, 4) == r + 1)
                    def _():
                        third(h, mine(h, p), sides[h]["C"][p].at[r], base + r, where()).start()

    def third_sums(h):
        side = sides[h]

        @pl.when(chosen)
        def _():
            to_pair(h).wait_recv()
            side["T1"][...] = low(mine(h, 0)[...].astype(jnp.float32) + side["C"][0][0].astype(jnp.float32))
            swap(h).start()

        for p, base, to, at, where in reach:
            @pl.when(at == to)
            def _():
                total = mine(h, p)[...].astype(jnp.float32)
                for r in range(3):
                    third(h, mine(h, p), side["C"][p].at[r], base + r, mate).wait_recv()
                    total = total + side["C"][p][r].astype(jnp.float32)
                final(h, p)[...] = low(total)
                share(h, p).start()

    def finish(h):
        side = sides[h]

        @pl.when(chosen)
        def _():
            swap(h).wait_recv()
            final(h, 0)[...] = low(side["T1"][...].astype(jnp.float32) + side["C"][0][1].astype(jnp.float32))

        for p, base, to, at, where in reach:
            @pl.when(jnp.logical_and(chosen, at != to))
            def _():
                share(h, p).wait_recv()

        @pl.when(chosen)
        def _():
            hand(h).start()

    def write(h):
        @pl.when(jnp.logical_not(chosen))
        def _():
            hand(h).wait_recv()

        out[:, spans[h][0] : spans[h][1]] = sides[h]["F"][...].astype(jnp.float32)

    def drain(h):
        for p in range(3):
            for to in range(2):
                for i in range(4):
                    whole_copy(h, p, to, i, sides[h]["wholes"][p].at[to, i]).wait_send()
                for i in range(2):
                    half_copy(h, p, to, i, sides[h]["halves"][p].at[to, i]).wait_send()
            for k in range(6):
                second_copy(h, p, k, mine(h, p)).wait_send()

        @pl.when(chosen)
        def _():
            swap(h).wait_send()
            hand(h).wait_send()

        @pl.when(jnp.logical_not(chosen))
        def _():
            to_pair(h).wait_send()

        for p, base, to, at, where in reach:
            @pl.when(at == to)
            def _():
                share(h, p).wait_send()

            for r in range(3):
                @pl.when(rem(at - to + 4, 4) == r + 1)
                def _():
                    third(h, mine(h, p), sides[h]["C"][p].at[r], base + r, where()).wait_send()

    produce(0)
    first_sends(0)
    produce(1)
    first_relays(0)
    first_sends(1)
    gain_start(0)
    second_sends(0)
    gain_end(0)
    gain_start(1)
    first_relays(1)
    gain_end(1)
    gain_start(2)
    second_relays(0)
    second_sends(1)
    third_sends(0)
    gain_end(2)
    gain_start(3)
    second_relays(1)
    third_sums(0)
    third_sends(1)
    finish(0)
    gain_end(3)
    third_sums(1)
    write(0)
    finish(1)
    write(1)
    drain(0)
    drain(1)


def reduce_call(gt, ct, lno, ao, gain, factor):
    cols = lno.shape[1]
    dma = pltpu.SemaphoreType.DMA
    vm = pl.BlockSpec(memory_space=pltpu.VMEM)
    scratch = [pltpu.VMEM((4, 4) + gain.shape, jnp.float32), dma((4, 3)), dma((4, 3))]
    for lo, hi in column_halves(cols):
        bf = lambda *shape: pltpu.VMEM(shape + (hi - lo,), jnp.bfloat16)
        sizes = [size for _, size in PARTS]
        scratch += [bf(16, ROWS), bf(16, ROWS), bf(RING, ROWS)]
        scratch += [x for s in sizes for x in (bf(2, 2, s), bf(2, 4, s), bf(3, s))]
        scratch += [bf(2, sizes[0]), bf(3, sizes[1]), bf(3, sizes[2]), bf(sizes[0]), bf(ROWS)]
        scratch += [dma((16,))] * 2 + [dma((3, 2, 2))] * 2 + [dma((3, 2, 4))] * 2 + [dma((3, 6))] * 2 + [dma((11,))] * 2
    return pl.pallas_call(
        functools.partial(reduce_kernel, factor),
        out_shape=(jax.ShapeDtypeStruct((ROWS, cols), jnp.float32), jax.ShapeDtypeStruct(gain.shape, jnp.float32)),
        in_specs=[vm] * 5,
        out_specs=[vm] * 2,
        scratch_shapes=scratch,
        compiler_params=pltpu.CompilerParams(collective_id=0, has_side_effects=True, vmem_limit_bytes=62 * 2**20),
        cost_estimate=pl.CostEstimate(flops=2 * BLOCKS * ROWS * lno.shape[0] * cols, bytes_accessed=2**24, transcendentals=0),
    )(gt, ct, lno, ao, gain)


def local(tokens, cotangent, ln_gain, w_qkv, w_out):
    images = tokens.shape[0] * lax.axis_size("wide") * lax.axis_size("narrow")
    factor = 1.0 / images
    x, cot = tokens[0], cotangent[0]
    ln_out, attn_out, grad_t, grad_input, gain = front_call(x, cot, ln_gain, w_qkv, w_out)
    cot_t = cot.T.reshape(BLOCKS // 2, -1, cot.shape[0])
    width = cot.shape[1]
    gain = jnp.zeros((16, LANES), jnp.float32).at[: width // LANES].set(gain[0].reshape(-1, LANES))
    grad_t = grad_t.reshape(BLOCKS * 3 // 2, -1, cot.shape[0])
    total, gain = reduce_call(grad_t, cot_t, ln_out, attn_out, gain, factor)
    return (grad_input[None], total[:Q_ROWS], total[Q_ROWS:], gain[: width // LANES].reshape(width) * factor)


def solution(mesh):
    return jax.shard_map(
        local,
        mesh=mesh,
        in_specs=(
            P(("wide", "narrow"), None, None),
            P(("wide", "narrow"), None, None),
            P(),
            P(),
            P(),
        ),
        out_specs=(P(("wide", "narrow"), None, None), P("wide", None), P("wide", None), P()),
        check_vma=False,
    )
```

```python
import functools

import jax
import jax.numpy as jnp
from jax import lax
from jax.experimental import pallas as pl
from jax.experimental.pallas import tpu as pltpu
from jax.sharding import PartitionSpec as P

HEADS = 16


ln_epsilon = 1e-06


LANES = 128
WINDOW = 256


def dot(a, b, over=((1,), (0,))):
    return lax.dot_general(a, b, (over, ((), ())), preferred_element_type=jnp.float32)


def low(a):
    return a.astype(jnp.bfloat16)


def normalise(x_ref):
    x = x_ref[...].astype(jnp.float32)
    centered = x - jnp.mean(x, axis=-1, keepdims=True)
    inv_sigma = lax.rsqrt(jnp.mean(centered * centered, axis=-1, keepdims=True) + ln_epsilon)
    return centered * inv_sigma, inv_sigma


def front_kernel(scale, x_ref, cot_ref, gain_ref, w_ref, wo_ref,
                 lno_ref, ao_ref, gt_ref, wpad):
    h = pl.program_id(0)
    dim = w_ref.shape[2]

    @pl.when(h == 0)
    def _():
        normed, _ = normalise(x_ref)
        lno_ref[...] = low(normed * gain_ref[...].reshape(1, -1))
        wpad[...] = jnp.zeros_like(wpad)

    for s in range(3):
        wpad[s * LANES : s * LANES + dim, :] = w_ref[s, 0]
    qkv = low(dot(lno_ref[...], wpad[...], ((1,), (1,))))
    q, k, v = (qkv[:, s * LANES : (s + 1) * LANES] for s in range(3))
    scores = dot(q, k, ((1,), (1,))) * scale
    expo = jnp.exp(scores - jnp.max(scores, axis=-1, keepdims=True))
    prob = expo / jnp.sum(expo, axis=-1, keepdims=True)
    prob_low = low(prob)

    start = jnp.minimum(lax.div(h * dim, LANES) * LANES, wo_ref.shape[1] - WINDOW)
    start = pl.multiple_of(start, LANES)
    offset = h * dim - start
    lane = lax.broadcasted_iota(jnp.int32, (1, WINDOW), 1)
    attn = dot(prob_low, v)
    attn = jnp.concatenate([attn, jnp.zeros_like(attn)], axis=1)
    attn = pltpu.roll(attn, offset, 1)
    window = ao_ref[:, pl.ds(start, WINDOW)].astype(jnp.float32)
    inside = jnp.logical_and(lane >= offset, lane < offset + dim)
    ao_ref[:, pl.ds(start, WINDOW)] = low(jnp.where(inside, attn, window))

    grad = dot(cot_ref[...], wo_ref[:, pl.ds(start, WINDOW)])
    grad = pltpu.roll(grad, lax.rem(WINDOW - offset, WINDOW), 1)[:, :LANES]
    grad = low(jnp.where(lane[:, :LANES] < dim, grad, 0.0))
    grad_prob = dot(grad, v, ((1,), (1,)))
    inner = jnp.sum(grad_prob * prob, axis=-1, keepdims=True)
    grad_score = low(prob * (grad_prob - inner) * scale)

    gt_ref[0, 0] = low(dot(grad_score, k).T[:dim])
    gt_ref[1, 0] = low(dot(q, grad_score, ((0,), (0,)))[:dim])
    gt_ref[2, 0] = low(dot(grad, prob_low, ((0,), (0,)))[:dim])


def front_call(x, cot, gain, w_qkv, w_out):
    tok, width = x.shape
    dim = width // HEADS
    whole = lambda a: pl.BlockSpec(a.shape, lambda h: (0,) * len(a.shape))
    w = w_qkv.reshape(3, HEADS, dim, width)
    outs = (
        jax.ShapeDtypeStruct((tok, width), jnp.bfloat16),
        jax.ShapeDtypeStruct((tok, width), jnp.bfloat16),
        jax.ShapeDtypeStruct((3, HEADS, dim, tok), jnp.bfloat16),
    )
    return pl.pallas_call(
        functools.partial(front_kernel, dim**-0.5),
        grid=(HEADS,),
        out_shape=outs,
        in_specs=[whole(x), whole(cot), whole(gain), pl.BlockSpec((3, 1, dim, width), lambda h: (0, h, 0, 0)), whole(w_out)],
        out_specs=[whole(outs[0]), whole(outs[1]), pl.BlockSpec((3, 1, dim, tok), lambda h: (0, h, 0, 0))],
        scratch_shapes=[pltpu.VMEM((3 * LANES, width), jnp.bfloat16)],
        compiler_params=pltpu.CompilerParams(vmem_limit_bytes=56 * 2**20, dimension_semantics=("arbitrary",)),
        cost_estimate=pl.CostEstimate(flops=12 * 10**9, bytes_accessed=26 * 2**20, transcendentals=HEADS * tok * tok),
    )(x, cot, gain, w, w_out)


BLOCKS = 32
ROWS = 208
Q_ROWS = 156
PARTS = ((0, 80), (80, 64), (144, 64))
CUTS = (48, 32, 32)
RING = 4
LAG = 2
MESH = pl.DeviceIdType.MESH


def rem(a, b):
    return lax.rem(a, jnp.int32(b))


def div(a, b):
    return lax.div(a, jnp.int32(b))


def column_halves(cols):
    edge = (cols // LANES + 1) // 2 * LANES
    return ((0, edge), (edge, cols))


def reduce_kernel(factor, gt, ct, lno, ao, x_ref, cot_ref, gain_ref, w_hbm, qkv_out, out_out, gain_out, gx_ref,
                  G, sg, rg, wbuf, wpad, gln, row, wsem, *scratch):
    cols = lno.shape[1]
    spans = column_halves(cols)
    per = len(scratch) // 2
    sides = []
    for h in range(2):
        s = scratch[h * per : (h + 1) * per]
        sides.append(dict(S=s[0], R0=s[1], T0=s[2], halves=(s[3], s[6], s[9]), wholes=(s[4], s[7], s[10]),
                          later=(s[5], s[8], s[11]), C=s[12:15], T1=s[15], F=s[16], sems=s[17:27]))

    wide, narrow = lax.axis_index("wide"), lax.axis_index("narrow")
    xh, y, z = div(wide, 16), rem(div(wide, 4), 4), rem(wide, 4)
    xl, c = div(narrow, 2), rem(narrow, 2)
    x = 2 * xh + xl
    place = (x, y, z)

    def device(x_, y_, z_, c_):
        return (div(x_, 2) * 16 + y_ * 4 + z_, rem(x_, 2) * 2 + c_)

    def shift(dim, by):
        at = [x, y, z]
        at[dim] = rem(at[dim] + by, 4)
        return device(*at, c)

    mate = device(x, y, z, 1 - c)
    peers = [mate] + [shift(d, by) for d in range(3) for by in (1, 2, 3)]
    barrier = pltpu.get_barrier_semaphore()
    for peer in peers:
        pl.semaphore_signal(barrier, inc=1, device_id=peer, device_id_type=MESH)
    pl.semaphore_wait(barrier, len(peers))

    def remote(src, dst, ssem, rsem, to):
        return pltpu.make_async_remote_copy(src_ref=src, dst_ref=dst, send_sem=ssem, recv_sem=rsem,
                                            device_id=to, device_id_type=MESH)

    def accumulate(dst, *more):
        total = dst[...].astype(jnp.float32)
        for term in more:
            total = total + term[...].astype(jnp.float32)
        dst[...] = total.astype(jnp.bfloat16)

    rings = ((2, c, lambda r: mate), (4, x, lambda r: shift(0, r)), (4, y, lambda r: shift(1, r)), (4, z, lambda r: shift(2, r)))
    gain_copies = []

    def gain_start(k):
        n, m, to = rings[k]
        if k == 0:
            G[k, m] = jnp.zeros(G.shape[2:], jnp.float32)
            for i in range(cols // LANES):
                G[k, m, i : i + 1, :] = row[:, i * LANES : (i + 1) * LANES]
        else:
            G[k, m] = gain_total(k - 1)
        for r in range(n - 1):
            copy = remote(G.at[k, m], G.at[k, m], sg.at[k, r], rg.at[k, r], to(r + 1))
            copy.start()
            gain_copies.append(copy)

    def gain_total(k):
        total = G[k, 0]
        for other in range(1, rings[k][0]):
            total = total + G[k, other]
        return total

    def gain_end(k):
        while gain_copies:
            gain_copies.pop().wait()
        if k == 3:
            total = gain_total(k) * factor
            for i in range(cols // LANES):
                gain_out[:, i * LANES : (i + 1) * LANES] = total[i : i + 1]

    def weights(h, slot):
        return pltpu.make_async_copy(w_hbm.at[:, h], wbuf.at[slot], wsem.at[slot])

    def input_gradient():
        dim = gt.shape[1]
        gln[...] = jnp.zeros_like(gln)
        wpad[...] = jnp.zeros_like(wpad)

        @pl.loop(0, HEADS)
        def _(h):
            slot = rem(h, 2)
            weights(h, slot).wait()

            @pl.when(h < HEADS - 1)
            def _():
                weights(h + 1, 1 - slot).start()

            pad = jnp.zeros((LANES - dim, gt.shape[2]), jnp.float32)
            stack = []
            for s in range(3):
                wpad[s * LANES : s * LANES + dim, :] = wbuf[slot, s]
                stack += [gt[s * HEADS + h].astype(jnp.float32), pad]
            gln[...] += dot(low(jnp.concatenate(stack, axis=0).T), wpad[...])

        normed, inv_sigma = normalise(x_ref)
        grad_ln = gln[...]
        row[...] = jnp.sum(grad_ln * normed, axis=0, keepdims=True)
        g = grad_ln * gain_ref[...].reshape(1, -1)
        grad_x = inv_sigma * (
            g - jnp.mean(g, axis=-1, keepdims=True) - normed * jnp.mean(g * normed, axis=-1, keepdims=True)
        )
        gx_ref[...] = low(cot_ref[...].astype(jnp.float32) + grad_x)

    def rows_of_pair(b):
        g = jnp.concatenate([gt[3 * b + i].astype(jnp.float32) for i in range(3)], axis=0)
        d = ct[b].astype(jnp.float32)
        out_rows = ROWS - Q_ROWS
        return tuple(
            jnp.concatenate([g[i * Q_ROWS : (i + 1) * Q_ROWS], d[i * out_rows : (i + 1) * out_rows]], axis=0)
            for i in range(2)
        )

    def product(left, right, lo, hi):
        full = right.shape[0] // 256 * 256
        total = dot(low(left[:, :full]), right[0:full, lo:hi])
        for k in range(full, right.shape[0]):
            total = total + left[:, k : k + 1] * right[k : k + 1, lo:hi].astype(jnp.float32)
        return total * factor

    def fill(side, span, b, slot):
        even, odd = rows_of_pair(b)
        mine_odd = rem(c + div(b, 8) + rem(div(b, 2), 4), 2) == 1
        give, keep = jnp.where(mine_odd, even, odd), jnp.where(mine_odd, odd, even)
        first = jnp.concatenate([give[0:160], keep[0:160]], axis=0)
        last = jnp.concatenate([give[144:208], keep[144:208]], axis=0)
        line = lax.broadcasted_iota(jnp.int32, (16, 1), 0)
        width = span[1] - span[0]
        for lo in range(0, width, 512):
            hi = min(width, lo + 512)
            p = product(first, lno, span[0] + lo, span[0] + hi)
            q = product(last, ao, span[0] + lo, span[0] + hi)
            for k, dst, at in ((0, side["T0"], slot), (1, side["S"], b)):
                u, v = p[160 * k : 160 * k + 160], q[64 * k : 64 * k + 64]
                dst[at, 0:144, lo:hi] = low(u[0:144])
                dst[at, 144:160, lo:hi] = low(jnp.where(line < Q_ROWS - 144, u[144:160], v[0:16]))
                dst[at, 160:208, lo:hi] = low(v[16:64])

    def core_copy(side, b, slot):
        return remote(side["T0"].at[slot], side["R0"].at[b], side["sems"][0].at[b], side["sems"][1].at[b], mate)

    def produce(h):
        side = sides[h]

        @pl.loop(0, 16 + LAG)
        def _(n):
            @pl.when(n < 16)
            def _():
                slot = rem(n, RING)

                @pl.when(n >= RING)
                def _():
                    core_copy(side, n - RING, slot).wait_send()

                fill(side, spans[h], n, slot)
                core_copy(side, n, slot).start()

            @pl.when(n >= LAG)
            def _():
                b = n - LAG
                core_copy(side, b, 0).wait_recv()
                accumulate(side["S"].at[b], side["R0"].at[b])

        for n in range(16 - RING, 16):
            core_copy(side, n, n % RING).wait_send()

    orders = ((1, 2, 0), (2, 0, 1), (0, 1, 2))
    firsts = (
        lambda t, i: (i // 2) * 8 + t * 2 + i % 2,
        lambda t, i: (i // 2) * 8 + (2 * (i % 2) + rem(c + t + i // 2, 2)) * 2 + div(t, 2),
        lambda t, i: div(t, 2) * 8 + i * 2 + rem(t, 2),
    )
    seconds = (
        lambda t: (rem(c + y + t, 2) * 8 + y * 2 + div(t, 2), rem(c + y + t, 2) * 2 + div(t, 2)),
        lambda t: (div(t, 2) * 8 + (2 * rem(t, 2) + rem(c + z + div(t, 2), 2)) * 2 + div(z, 2), t),
        lambda t: (div(x, 2) * 8 + t * 2 + rem(x, 2), t),
    )

    def part(h, p, b):
        return sides[h]["S"].at[b, pl.ds(*PARTS[p]), :]

    def half_copy(h, p, to, i, src):
        sems = sides[h]["sems"]
        return remote(src, sides[h]["halves"][p].at[to, i], sems[2].at[p, to, i], sems[3].at[p, to, i],
                      shift(orders[p][0], 1 + 2 * to))

    def whole_copy(h, p, to, i, src):
        sems = sides[h]["sems"]
        return remote(src, sides[h]["wholes"][p].at[to, i], sems[4].at[p, to, i], sems[5].at[p, to, i],
                      shift(orders[p][0], 1 + 2 * to))

    six = [(p, to) for to in range(2) for p in range(3)]

    def first_sends(h):
        for i in range(2):
            for p, to in six:
                t = rem(place[orders[p][0]] + 2, 4)
                half_copy(h, p, to, i, part(h, p, firsts[p](t, i + 2 * to))).start()
        for i in range(2):
            for p, to in six:
                t = rem(place[orders[p][0]] + 1 + 2 * to, 4)
                index = i + 2 - 2 * to
                whole_copy(h, p, to, index, part(h, p, firsts[p](t, index))).start()

    def first_relays(h):
        for i in range(2):
            for p, to in six:
                halves = sides[h]["halves"][p]
                half_copy(h, p, to, i, halves.at[to, i]).wait_recv()
                t = rem(place[orders[p][0]] + 1 + 2 * to, 4)
                index = i + 2 * to
                block = part(h, p, firsts[p](t, index))
                accumulate(block, halves.at[to, i])
                whole_copy(h, p, to, index, block).start()

    def ready(h, p, t):
        b, i = seconds[p](t)
        wholes = sides[h]["wholes"][p]
        for to in range(2):
            whole_copy(h, p, to, i, wholes.at[to, i]).wait_recv()
        accumulate(part(h, p, b), wholes.at[0, i], wholes.at[1, i])
        return part(h, p, b)

    def second_copy(h, p, k, what):
        edge = CUTS[p]
        lower, upper = pl.ds(0, edge), pl.ds(edge, PARTS[p][1] - edge)
        rows, slot, by = ((lower, 0, 1), (upper, 0, 3), (upper, 1, 1), (lower, 2, 3), (lower, 1, 1), (upper, 2, 3))[k]
        sems = sides[h]["sems"]
        return remote(what.at[rows], sides[h]["later"][p].at[slot, rows], sems[6].at[p, k], sems[7].at[p, k],
                      shift(orders[p][1], by))

    def block2(h, p, by):
        return part(h, p, seconds[p](rem(place[orders[p][1]] + by, 4))[0])

    def second_sends(h):
        for p in range(3):
            opposite = ready(h, p, rem(place[orders[p][1]] + 2, 4))
            second_copy(h, p, 0, opposite).start()
            second_copy(h, p, 1, opposite).start()
        for p in range(3):
            second_copy(h, p, 2, ready(h, p, rem(place[orders[p][1]] + 1, 4))).start()
            second_copy(h, p, 3, ready(h, p, rem(place[orders[p][1]] + 3, 4))).start()

    def second_relays(h):
        for p in range(3):
            edge = CUTS[p]
            inbox = sides[h]["later"][p]
            for k, by, rows in ((0, 1, pl.ds(0, edge)), (1, 3, pl.ds(edge, PARTS[p][1] - edge))):
                what = block2(h, p, by)
                second_copy(h, p, k, what).wait_recv()
                accumulate(what.at[rows], inbox.at[0, rows])
                second_copy(h, p, 4 + k, what).start()
        for p in range(3):
            ready(h, p, place[orders[p][1]])

    chosen = c == rem(xh + y + z, 2)
    partner = device(2 * xh + 1 - xl, y, z, c)
    outward = device(rem(x + 3 + 2 * xl, 4), y, z, c)
    y_to = 2 * xl + rem(c + z + xh, 2)
    z_to = 2 * xl + rem(c + y + xh, 2)
    reach = ((1, 2, y_to, y, lambda: device(x, y_to, z, c)), (2, 5, z_to, z, lambda: device(x, y, z_to, c)))

    def third(h, src, dst, k, to):
        sems = sides[h]["sems"]
        return remote(src, dst, sems[8].at[k], sems[9].at[k], to)

    def mine(h, p):
        return block2(h, p, 0)

    def final(h, p):
        return sides[h]["F"].at[pl.ds(*PARTS[p]), :]

    def to_pair(h):
        return third(h, mine(h, 0), sides[h]["C"][0].at[0], 0, outward)

    def swap(h):
        return third(h, sides[h]["T1"], sides[h]["C"][0].at[1], 1, partner)

    def share(h, p):
        return third(h, final(h, p), final(h, p), 7 + p, partner)

    def hand(h):
        return third(h, sides[h]["F"], sides[h]["F"], 10, mate)

    def third_sends(h):
        for p in range(3):
            for k in range(2, 6):
                second_copy(h, p, k, mine(h, p)).wait_recv()
            accumulate(mine(h, p), sides[h]["later"][p].at[1], sides[h]["later"][p].at[2])
            if p == 0:
                @pl.when(jnp.logical_not(chosen))
                def _():
                    to_pair(h).start()
            else:
                _, base, to, at, where = reach[p - 1]
                for r in range(3):
                    @pl.when(rem(at - to + 4, 4) == r + 1)
                    def _():
                        third(h, mine(h, p), sides[h]["C"][p].at[r], base + r, where()).start()

    def third_sums(h):
        side = sides[h]

        @pl.when(chosen)
        def _():
            to_pair(h).wait_recv()
            side["T1"][...] = low(mine(h, 0)[...].astype(jnp.float32) + side["C"][0][0].astype(jnp.float32))
            swap(h).start()

        for p, base, to, at, where in reach:
            @pl.when(at == to)
            def _():
                total = mine(h, p)[...].astype(jnp.float32)
                for r in range(3):
                    third(h, mine(h, p), side["C"][p].at[r], base + r, mate).wait_recv()
                    total = total + side["C"][p][r].astype(jnp.float32)
                final(h, p)[...] = low(total)
                share(h, p).start()

    def finish(h):
        side = sides[h]

        @pl.when(chosen)
        def _():
            swap(h).wait_recv()
            final(h, 0)[...] = low(side["T1"][...].astype(jnp.float32) + side["C"][0][1].astype(jnp.float32))

        for p, base, to, at, where in reach:
            @pl.when(jnp.logical_and(chosen, at != to))
            def _():
                share(h, p).wait_recv()

        @pl.when(chosen)
        def _():
            hand(h).start()

    def write(h):
        @pl.when(jnp.logical_not(chosen))
        def _():
            hand(h).wait_recv()

        total = sides[h]["F"][...].astype(jnp.float32)
        qkv_out[:, spans[h][0] : spans[h][1]] = total[:Q_ROWS]
        out_out[:, spans[h][0] : spans[h][1]] = total[Q_ROWS:]

    def drain(h):
        for p in range(3):
            for to in range(2):
                for i in range(4):
                    whole_copy(h, p, to, i, sides[h]["wholes"][p].at[to, i]).wait_send()
                for i in range(2):
                    half_copy(h, p, to, i, sides[h]["halves"][p].at[to, i]).wait_send()
            for k in range(6):
                second_copy(h, p, k, mine(h, p)).wait_send()

        @pl.when(chosen)
        def _():
            swap(h).wait_send()
            hand(h).wait_send()

        @pl.when(jnp.logical_not(chosen))
        def _():
            to_pair(h).wait_send()

        for p, base, to, at, where in reach:
            @pl.when(at == to)
            def _():
                share(h, p).wait_send()

            for r in range(3):
                @pl.when(rem(at - to + 4, 4) == r + 1)
                def _():
                    third(h, mine(h, p), sides[h]["C"][p].at[r], base + r, where()).wait_send()

    weights(0, 0).start()
    produce(0)
    first_sends(0)
    produce(1)
    first_relays(0)
    first_sends(1)
    input_gradient()
    gain_start(0)
    second_sends(0)
    gain_end(0)
    gain_start(1)
    first_relays(1)
    gain_end(1)
    gain_start(2)
    second_relays(0)
    second_sends(1)
    third_sends(0)
    gain_end(2)
    gain_start(3)
    second_relays(1)
    third_sums(0)
    third_sends(1)
    finish(0)
    gain_end(3)
    third_sums(1)
    write(0)
    finish(1)
    write(1)
    drain(0)
    drain(1)


def reduce_call(gt, ct, lno, ao, x, cot, gain, w, factor):
    tok, cols = lno.shape
    dma = pltpu.SemaphoreType.DMA
    vm = pl.BlockSpec(memory_space=pltpu.VMEM)
    dim = gt.shape[1]
    scratch = [
        pltpu.VMEM((4, 4, 16, LANES), jnp.float32), dma((4, 3)), dma((4, 3)),
        pltpu.VMEM((2, 3, dim, cols), jnp.bfloat16), pltpu.VMEM((3 * LANES, cols), jnp.bfloat16),
        pltpu.VMEM((tok, cols), jnp.float32), pltpu.VMEM((1, cols), jnp.float32), dma((2,)),
    ]
    for lo, hi in column_halves(cols):
        bf = lambda *shape: pltpu.VMEM(shape + (hi - lo,), jnp.bfloat16)
        sizes = [size for _, size in PARTS]
        scratch += [bf(16, ROWS), bf(16, ROWS), bf(RING, ROWS)]
        scratch += [x for s in sizes for x in (bf(2, 2, s), bf(2, 4, s), bf(3, s))]
        scratch += [bf(2, sizes[0]), bf(3, sizes[1]), bf(3, sizes[2]), bf(sizes[0]), bf(ROWS)]
        scratch += [dma((16,))] * 2 + [dma((3, 2, 2))] * 2 + [dma((3, 2, 4))] * 2 + [dma((3, 6))] * 2 + [dma((11,))] * 2
    return pl.pallas_call(
        functools.partial(reduce_kernel, factor),
        out_shape=(
            jax.ShapeDtypeStruct((Q_ROWS, cols), jnp.float32),
            jax.ShapeDtypeStruct((ROWS - Q_ROWS, cols), jnp.float32),
            jax.ShapeDtypeStruct((1, cols), jnp.float32),
            jax.ShapeDtypeStruct((tok, cols), jnp.bfloat16),
        ),
        in_specs=[vm] * 7 + [pl.BlockSpec(memory_space=pl.ANY)],
        out_specs=[vm] * 4,
        scratch_shapes=scratch,
        compiler_params=pltpu.CompilerParams(collective_id=0, has_side_effects=True, vmem_limit_bytes=63 * 2**20),
        cost_estimate=pl.CostEstimate(flops=2 * BLOCKS * ROWS * tok * cols, bytes_accessed=2**24, transcendentals=0),
    )(gt, ct, lno, ao, x, cot, gain, w)


def local(tokens, cotangent, ln_gain, w_qkv, w_out):
    images = tokens.shape[0] * lax.axis_size("wide") * lax.axis_size("narrow")
    factor = 1.0 / images
    x, cot = tokens[0], cotangent[0]
    ln_out, attn_out, grad_t = front_call(x, cot, ln_gain, w_qkv, w_out)
    cot_t = cot.T.reshape(BLOCKS // 2, -1, cot.shape[0])
    grad_t = grad_t.reshape(BLOCKS * 3 // 2, -1, cot.shape[0])
    w = w_qkv.reshape(3, HEADS, -1, cot.shape[1])
    grad_qkv, grad_out, gain, grad_input = reduce_call(grad_t, cot_t, ln_out, attn_out, x, cot, ln_gain, w, factor)
    return (grad_input[None], grad_qkv, grad_out, gain.reshape(-1))


def solution(mesh):
    return jax.shard_map(
        local,
        mesh=mesh,
        in_specs=(
            P(("wide", "narrow"), None, None),
            P(("wide", "narrow"), None, None),
            P(),
            P(),
            P(),
        ),
        out_specs=(P(("wide", "narrow"), None, None), P("wide", None), P("wide", None), P()),
        check_vma=False,
    )
```

```python
import functools

import jax
import jax.numpy as jnp
from jax import lax
from jax.experimental import pallas as pl
from jax.experimental.pallas import tpu as pltpu
from jax.sharding import PartitionSpec as P

HEADS = 16


ln_epsilon = 1e-06


LANES = 128
WINDOW = 256
LOG2_E = 1.4426950408889634
TOGETHER = 4


def dot(a, b, over=((1,), (0,))):
    return lax.dot_general(a, b, (over, ((), ())), preferred_element_type=jnp.float32)


def low(a):
    return a.astype(jnp.bfloat16)


def normalise(x_ref):
    x = x_ref[...].astype(jnp.float32)
    centered = x - jnp.mean(x, axis=-1, keepdims=True)
    inv_sigma = lax.rsqrt(jnp.mean(centered * centered, axis=-1, keepdims=True) + ln_epsilon)
    return centered * inv_sigma, inv_sigma


def front_kernel(scale, x_ref, cot_ref, gain_ref, w_ref, wo_ref,
                 lno_ref, ao_ref, gt_ref, ct_ref, wpad):
    h = pl.program_id(0)
    dim = w_ref.shape[2]

    @pl.when(h == 0)
    def _():
        normed, _ = normalise(x_ref)
        lno_ref[...] = low(normed * gain_ref[...].reshape(1, -1))
        wpad[...] = jnp.zeros_like(wpad)

    pair = range(TOGETHER)
    for j in pair:
        for s in range(3):
            at = (3 * j + s) * LANES
            wpad[at : at + dim, :] = w_ref[s, j]
    qkv = low(dot(lno_ref[...], wpad[...], ((1,), (1,))))
    q, k, v = ([qkv[:, (3 * j + s) * LANES : (3 * j + s + 1) * LANES] for j in pair] for s in range(3))
    scores = [dot(q[j], k[j], ((1,), (1,))) for j in pair]

    lane = lax.broadcasted_iota(jnp.int32, (1, WINDOW), 1)
    starts = [jnp.minimum(lax.div((h * TOGETHER + j) * dim, LANES) * LANES, wo_ref.shape[1] - WINDOW) for j in pair]
    starts = [pl.multiple_of(start, LANES) for start in starts]
    offsets = [(h * TOGETHER + j) * dim - starts[j] for j in pair]
    grad = [dot(cot_ref[...], wo_ref[:, pl.ds(starts[j], WINDOW)]) for j in pair]
    back = [lax.rem(WINDOW - offsets[j], WINDOW) for j in pair]
    grad = [pltpu.roll(grad[j], back[j], 1)[:, :LANES] for j in pair]
    grad = [low(jnp.where(lane[:, :LANES] < dim, grad[j], 0.0)) for j in pair]
    grad_prob = [dot(grad[j], v[j], ((1,), (1,))) for j in pair]

    prob = []
    for j in pair:
        expo = jnp.exp2((scores[j] - jnp.max(scores[j], axis=-1, keepdims=True)) * (scale * LOG2_E))
        prob.append(expo * (1.0 / jnp.sum(expo, axis=-1, keepdims=True)))
    prob_low = [low(prob[j]) for j in pair]
    attn = [dot(prob_low[j], v[j]) for j in pair]
    for j in pair:
        gt_ref[2, j] = low(dot(grad[j], prob_low[j], ((0,), (0,)))[:dim])

    grad_score = []
    for j in pair:
        inner = jnp.sum(grad_prob[j] * prob[j], axis=-1, keepdims=True)
        grad_score.append(low(prob[j] * (grad_prob[j] - inner) * scale))
    for j in pair:
        gt_ref[1, j] = low(dot(q[j], grad_score[j], ((0,), (0,)))[:dim])
        gt_ref[0, j] = low(dot(grad_score[j], k[j]).T[:dim])

    for j in pair:
        part = cot_ref[:, pl.ds(starts[j], WINDOW)].astype(jnp.float32)
        ct_ref[j] = low(pltpu.roll(part, back[j], 1)[:, :LANES].T[:dim])
        wide = pltpu.roll(jnp.concatenate([attn[j], jnp.zeros_like(attn[j])], axis=1), offsets[j], 1)
        window = ao_ref[:, pl.ds(starts[j], WINDOW)].astype(jnp.float32)
        inside = jnp.logical_and(lane >= offsets[j], lane < offsets[j] + dim)
        ao_ref[:, pl.ds(starts[j], WINDOW)] = low(jnp.where(inside, wide, window))


def front_call(x, cot, gain, w_qkv, w_out):
    tok, width = x.shape
    dim = width // HEADS
    whole = lambda a: pl.BlockSpec(a.shape, lambda h: (0,) * len(a.shape))
    w = w_qkv.reshape(3, HEADS, dim, width)
    outs = (
        jax.ShapeDtypeStruct((tok, width), jnp.bfloat16),
        jax.ShapeDtypeStruct((tok, width), jnp.bfloat16),
        jax.ShapeDtypeStruct((3, HEADS, dim, tok), jnp.bfloat16),
        jax.ShapeDtypeStruct((HEADS, dim, tok), jnp.bfloat16),
    )
    return pl.pallas_call(
        functools.partial(front_kernel, dim**-0.5),
        grid=(HEADS // TOGETHER,),
        out_shape=outs,
        in_specs=[whole(x), whole(cot), whole(gain), pl.BlockSpec((3, TOGETHER, dim, width), lambda h: (0, h, 0, 0)), whole(w_out)],
        out_specs=[whole(outs[0]), whole(outs[1]), pl.BlockSpec((3, TOGETHER, dim, tok), lambda h: (0, h, 0, 0)),
                   pl.BlockSpec((TOGETHER, dim, tok), lambda h: (h, 0, 0))],
        scratch_shapes=[pltpu.VMEM((TOGETHER * 3 * LANES, width), jnp.bfloat16)],
        compiler_params=pltpu.CompilerParams(vmem_limit_bytes=56 * 2**20, dimension_semantics=("arbitrary",)),
        cost_estimate=pl.CostEstimate(flops=12 * 10**9, bytes_accessed=26 * 2**20, transcendentals=HEADS * tok * tok),
    )(x, cot, gain, w, w_out)


BLOCKS = 32
ROWS = 208
Q_ROWS = 156
PARTS = ((0, 80), (80, 64), (144, 64))
CUTS = (48, 32, 32)
RING = 4
LAG = 2
MESH = pl.DeviceIdType.MESH


def rem(a, b):
    return lax.rem(a, jnp.int32(b))


def div(a, b):
    return lax.div(a, jnp.int32(b))


def column_halves(cols):
    edge = (cols // LANES + 1) // 2 * LANES
    return ((0, edge), (edge, cols))


def reduce_kernel(factor, gt, ct, lno, ao, x_ref, cot_ref, gain_ref, w_hbm, qkv_out, out_out, gain_out, gx_ref,
                  G, sg, rg, wbuf, wpad, gln, row, wsem, *scratch):
    cols = lno.shape[1]
    spans = column_halves(cols)
    per = len(scratch) // 2
    sides = []
    for h in range(2):
        s = scratch[h * per : (h + 1) * per]
        sides.append(dict(S=s[0], R0=s[1], T0=s[2], halves=(s[3], s[6], s[9]), wholes=(s[4], s[7], s[10]),
                          later=(s[5], s[8], s[11]), C=s[12:15], T1=s[15], F=s[16], sems=s[17:27]))

    wide, narrow = lax.axis_index("wide"), lax.axis_index("narrow")
    xh, y, z = div(wide, 16), rem(div(wide, 4), 4), rem(wide, 4)
    xl, c = div(narrow, 2), rem(narrow, 2)
    x = 2 * xh + xl
    place = (x, y, z)

    def device(x_, y_, z_, c_):
        return (div(x_, 2) * 16 + y_ * 4 + z_, rem(x_, 2) * 2 + c_)

    def shift(dim, by):
        at = [x, y, z]
        at[dim] = rem(at[dim] + by, 4)
        return device(*at, c)

    mate = device(x, y, z, 1 - c)
    peers = [mate] + [shift(d, by) for d in range(3) for by in (1, 2, 3)]
    barrier = pltpu.get_barrier_semaphore()
    for peer in peers:
        pl.semaphore_signal(barrier, inc=1, device_id=peer, device_id_type=MESH)
    pl.semaphore_wait(barrier, len(peers))

    def remote(src, dst, ssem, rsem, to):
        return pltpu.make_async_remote_copy(src_ref=src, dst_ref=dst, send_sem=ssem, recv_sem=rsem,
                                            device_id=to, device_id_type=MESH)

    def accumulate(dst, *more):
        total = dst[...].astype(jnp.float32)
        for term in more:
            total = total + term[...].astype(jnp.float32)
        dst[...] = total.astype(jnp.bfloat16)

    rings = ((2, c, lambda r: mate), (4, x, lambda r: shift(0, r)), (4, y, lambda r: shift(1, r)), (4, z, lambda r: shift(2, r)))
    gain_copies = []

    def gain_start(k):
        n, m, to = rings[k]
        if k == 0:
            G[k, m] = jnp.zeros(G.shape[2:], jnp.float32)
            for i in range(cols // LANES):
                G[k, m, i : i + 1, :] = row[:, i * LANES : (i + 1) * LANES]
        else:
            G[k, m] = gain_total(k - 1)
        for r in range(n - 1):
            copy = remote(G.at[k, m], G.at[k, m], sg.at[k, r], rg.at[k, r], to(r + 1))
            copy.start()
            gain_copies.append(copy)

    def gain_total(k):
        total = G[k, 0]
        for other in range(1, rings[k][0]):
            total = total + G[k, other]
        return total

    def gain_end(k):
        while gain_copies:
            gain_copies.pop().wait()
        if k == 3:
            total = gain_total(k) * factor
            for i in range(cols // LANES):
                gain_out[i * LANES : (i + 1) * LANES] = total[i]

    def weights(h, slot):
        return pltpu.make_async_copy(w_hbm.at[:, h], wbuf.at[slot], wsem.at[slot])

    def input_gradient():
        dim = gt.shape[1]
        gln[...] = jnp.zeros_like(gln)
        wpad[...] = jnp.zeros_like(wpad)

        @pl.loop(0, HEADS)
        def _(h):
            slot = rem(h, 2)
            weights(h, slot).wait()

            @pl.when(h < HEADS - 1)
            def _():
                weights(h + 1, 1 - slot).start()

            pad = jnp.zeros((LANES - dim, gt.shape[2]), jnp.float32)
            stack = []
            for s in range(3):
                wpad[s * LANES : s * LANES + dim, :] = wbuf[slot, s]
                stack += [gt[s * HEADS + h].astype(jnp.float32), pad]
            gln[...] += dot(low(jnp.concatenate(stack, axis=0).T), wpad[...])

        normed, inv_sigma = normalise(x_ref)
        grad_ln = gln[...]
        row[...] = jnp.sum(grad_ln * normed, axis=0, keepdims=True)
        g = grad_ln * gain_ref[...].reshape(1, -1)
        grad_x = inv_sigma * (
            g - jnp.mean(g, axis=-1, keepdims=True) - normed * jnp.mean(g * normed, axis=-1, keepdims=True)
        )
        gx_ref[...] = low(cot_ref[...].astype(jnp.float32) + grad_x)

    def rows_of_pair(b):
        g = jnp.concatenate([gt[3 * b + i].astype(jnp.float32) for i in range(3)], axis=0)
        d = ct[b].astype(jnp.float32)
        out_rows = ROWS - Q_ROWS
        return tuple(
            jnp.concatenate([g[i * Q_ROWS : (i + 1) * Q_ROWS], d[i * out_rows : (i + 1) * out_rows]], axis=0)
            for i in range(2)
        )

    def product(left, right, lo, hi):
        full = right.shape[0] // 256 * 256
        total = dot(low(left[:, :full]), right[0:full, lo:hi])
        for k in range(full, right.shape[0]):
            total = total + left[:, k : k + 1] * right[k : k + 1, lo:hi].astype(jnp.float32)
        return total * factor

    def fill(side, span, b, slot):
        even, odd = rows_of_pair(b)
        mine_odd = rem(c + div(b, 8) + rem(div(b, 2), 4), 2) == 1
        give, keep = jnp.where(mine_odd, even, odd), jnp.where(mine_odd, odd, even)
        first = jnp.concatenate([give[0:160], keep[0:160]], axis=0)
        last = jnp.concatenate([give[144:208], keep[144:208]], axis=0)
        line = lax.broadcasted_iota(jnp.int32, (16, 1), 0)
        width = span[1] - span[0]
        for lo in range(0, width, 512):
            hi = min(width, lo + 512)
            p = product(first, lno, span[0] + lo, span[0] + hi)
            q = product(last, ao, span[0] + lo, span[0] + hi)
            for k, dst, at in ((0, side["T0"], slot), (1, side["S"], b)):
                u, v = p[160 * k : 160 * k + 160], q[64 * k : 64 * k + 64]
                dst[at, 0:144, lo:hi] = low(u[0:144])
                dst[at, 144:160, lo:hi] = low(jnp.where(line < Q_ROWS - 144, u[144:160], v[0:16]))
                dst[at, 160:208, lo:hi] = low(v[16:64])

    def core_copy(side, b, slot):
        return remote(side["T0"].at[slot], side["R0"].at[b], side["sems"][0].at[b], side["sems"][1].at[b], mate)

    def produce(h):
        side = sides[h]

        @pl.loop(0, 16 + LAG)
        def _(n):
            @pl.when(n < 16)
            def _():
                slot = rem(n, RING)

                @pl.when(n >= RING)
                def _():
                    core_copy(side, n - RING, slot).wait_send()

                fill(side, spans[h], n, slot)
                core_copy(side, n, slot).start()

            @pl.when(n >= LAG)
            def _():
                b = n - LAG
                core_copy(side, b, 0).wait_recv()
                accumulate(side["S"].at[b], side["R0"].at[b])

        for n in range(16 - RING, 16):
            core_copy(side, n, n % RING).wait_send()

    orders = ((1, 2, 0), (2, 0, 1), (0, 1, 2))
    firsts = (
        lambda t, i: (i // 2) * 8 + t * 2 + i % 2,
        lambda t, i: (i // 2) * 8 + (2 * (i % 2) + rem(c + t + i // 2, 2)) * 2 + div(t, 2),
        lambda t, i: div(t, 2) * 8 + i * 2 + rem(t, 2),
    )
    seconds = (
        lambda t: (rem(c + y + t, 2) * 8 + y * 2 + div(t, 2), rem(c + y + t, 2) * 2 + div(t, 2)),
        lambda t: (div(t, 2) * 8 + (2 * rem(t, 2) + rem(c + z + div(t, 2), 2)) * 2 + div(z, 2), t),
        lambda t: (div(x, 2) * 8 + t * 2 + rem(x, 2), t),
    )

    def part(h, p, b):
        return sides[h]["S"].at[b, pl.ds(*PARTS[p]), :]

    def half_copy(h, p, to, i, src):
        sems = sides[h]["sems"]
        return remote(src, sides[h]["halves"][p].at[to, i], sems[2].at[p, to, i], sems[3].at[p, to, i],
                      shift(orders[p][0], 1 + 2 * to))

    def whole_copy(h, p, to, i, src):
        sems = sides[h]["sems"]
        return remote(src, sides[h]["wholes"][p].at[to, i], sems[4].at[p, to, i], sems[5].at[p, to, i],
                      shift(orders[p][0], 1 + 2 * to))

    six = [(p, to) for to in range(2) for p in range(3)]

    def first_sends(h):
        for i in range(2):
            for p, to in six:
                t = rem(place[orders[p][0]] + 2, 4)
                half_copy(h, p, to, i, part(h, p, firsts[p](t, i + 2 * to))).start()
        for i in range(2):
            for p, to in six:
                t = rem(place[orders[p][0]] + 1 + 2 * to, 4)
                index = i + 2 - 2 * to
                whole_copy(h, p, to, index, part(h, p, firsts[p](t, index))).start()

    def first_relays(h):
        for i in range(2):
            for p, to in six:
                halves = sides[h]["halves"][p]
                half_copy(h, p, to, i, halves.at[to, i]).wait_recv()
                t = rem(place[orders[p][0]] + 1 + 2 * to, 4)
                index = i + 2 * to
                block = part(h, p, firsts[p](t, index))
                accumulate(block, halves.at[to, i])
                whole_copy(h, p, to, index, block).start()

    def ready(h, p, t):
        b, i = seconds[p](t)
        wholes = sides[h]["wholes"][p]
        for to in range(2):
            whole_copy(h, p, to, i, wholes.at[to, i]).wait_recv()
        accumulate(part(h, p, b), wholes.at[0, i], wholes.at[1, i])
        return part(h, p, b)

    def second_copy(h, p, k, what):
        edge = CUTS[p]
        lower, upper = pl.ds(0, edge), pl.ds(edge, PARTS[p][1] - edge)
        rows, slot, by = ((lower, 0, 1), (upper, 0, 3), (upper, 1, 1), (lower, 2, 3), (lower, 1, 1), (upper, 2, 3))[k]
        sems = sides[h]["sems"]
        return remote(what.at[rows], sides[h]["later"][p].at[slot, rows], sems[6].at[p, k], sems[7].at[p, k],
                      shift(orders[p][1], by))

    def block2(h, p, by):
        return part(h, p, seconds[p](rem(place[orders[p][1]] + by, 4))[0])

    def second_sends(h):
        for p in range(3):
            opposite = ready(h, p, rem(place[orders[p][1]] + 2, 4))
            second_copy(h, p, 0, opposite).start()
            second_copy(h, p, 1, opposite).start()
        for p in range(3):
            second_copy(h, p, 2, ready(h, p, rem(place[orders[p][1]] + 1, 4))).start()
            second_copy(h, p, 3, ready(h, p, rem(place[orders[p][1]] + 3, 4))).start()

    def second_relays(h):
        for p in range(3):
            edge = CUTS[p]
            inbox = sides[h]["later"][p]
            for k, by, rows in ((0, 1, pl.ds(0, edge)), (1, 3, pl.ds(edge, PARTS[p][1] - edge))):
                what = block2(h, p, by)
                second_copy(h, p, k, what).wait_recv()
                accumulate(what.at[rows], inbox.at[0, rows])
                second_copy(h, p, 4 + k, what).start()
        for p in range(3):
            ready(h, p, place[orders[p][1]])

    chosen = c == rem(xh + y + z, 2)
    partner = device(2 * xh + 1 - xl, y, z, c)
    outward = device(rem(x + 3 + 2 * xl, 4), y, z, c)
    y_to = 2 * xl + rem(c + z + xh, 2)
    z_to = 2 * xl + rem(c + y + xh, 2)
    reach = ((1, 2, y_to, y, lambda: device(x, y_to, z, c)), (2, 5, z_to, z, lambda: device(x, y, z_to, c)))

    def third(h, src, dst, k, to):
        sems = sides[h]["sems"]
        return remote(src, dst, sems[8].at[k], sems[9].at[k], to)

    def mine(h, p):
        return block2(h, p, 0)

    def final(h, p):
        return sides[h]["F"].at[pl.ds(*PARTS[p]), :]

    def to_pair(h):
        return third(h, mine(h, 0), sides[h]["C"][0].at[0], 0, outward)

    def swap(h):
        return third(h, sides[h]["T1"], sides[h]["C"][0].at[1], 1, partner)

    def share(h, p):
        return third(h, final(h, p), final(h, p), 7 + p, partner)

    def hand(h):
        return third(h, sides[h]["F"], sides[h]["F"], 10, mate)

    def third_sends(h):
        for p in range(3):
            for k in range(2, 6):
                second_copy(h, p, k, mine(h, p)).wait_recv()
            accumulate(mine(h, p), sides[h]["later"][p].at[1], sides[h]["later"][p].at[2])
            if p == 0:
                @pl.when(jnp.logical_not(chosen))
                def _():
                    to_pair(h).start()
            else:
                _, base, to, at, where = reach[p - 1]
                for r in range(3):
                    @pl.when(rem(at - to + 4, 4) == r + 1)
                    def _():
                        third(h, mine(h, p), sides[h]["C"][p].at[r], base + r, where()).start()

    def third_sums(h):
        side = sides[h]

        @pl.when(chosen)
        def _():
            to_pair(h).wait_recv()
            side["T1"][...] = low(mine(h, 0)[...].astype(jnp.float32) + side["C"][0][0].astype(jnp.float32))
            swap(h).start()

        for p, base, to, at, where in reach:
            @pl.when(at == to)
            def _():
                total = mine(h, p)[...].astype(jnp.float32)
                for r in range(3):
                    third(h, mine(h, p), side["C"][p].at[r], base + r, mate).wait_recv()
                    total = total + side["C"][p][r].astype(jnp.float32)
                final(h, p)[...] = low(total)
                share(h, p).start()

    def finish(h):
        side = sides[h]

        @pl.when(chosen)
        def _():
            swap(h).wait_recv()
            final(h, 0)[...] = low(side["T1"][...].astype(jnp.float32) + side["C"][0][1].astype(jnp.float32))

        for p, base, to, at, where in reach:
            @pl.when(jnp.logical_and(chosen, at != to))
            def _():
                share(h, p).wait_recv()

        @pl.when(chosen)
        def _():
            hand(h).start()

    def write(h):
        @pl.when(jnp.logical_not(chosen))
        def _():
            hand(h).wait_recv()

        total = sides[h]["F"][...].astype(jnp.float32)
        qkv_out[:, spans[h][0] : spans[h][1]] = total[:Q_ROWS]
        out_out[:, spans[h][0] : spans[h][1]] = total[Q_ROWS:]

    def drain(h):
        for p in range(3):
            for to in range(2):
                for i in range(4):
                    whole_copy(h, p, to, i, sides[h]["wholes"][p].at[to, i]).wait_send()
                for i in range(2):
                    half_copy(h, p, to, i, sides[h]["halves"][p].at[to, i]).wait_send()
            for k in range(6):
                second_copy(h, p, k, mine(h, p)).wait_send()

        @pl.when(chosen)
        def _():
            swap(h).wait_send()
            hand(h).wait_send()

        @pl.when(jnp.logical_not(chosen))
        def _():
            to_pair(h).wait_send()

        for p, base, to, at, where in reach:
            @pl.when(at == to)
            def _():
                share(h, p).wait_send()

            for r in range(3):
                @pl.when(rem(at - to + 4, 4) == r + 1)
                def _():
                    third(h, mine(h, p), sides[h]["C"][p].at[r], base + r, where()).wait_send()

    weights(0, 0).start()
    produce(0)
    first_sends(0)
    produce(1)
    first_relays(0)
    first_sends(1)
    input_gradient()
    gain_start(0)
    second_sends(0)
    gain_end(0)
    gain_start(1)
    first_relays(1)
    gain_end(1)
    gain_start(2)
    second_relays(0)
    second_sends(1)
    third_sends(0)
    gain_end(2)
    gain_start(3)
    second_relays(1)
    third_sums(0)
    third_sends(1)
    finish(0)
    gain_end(3)
    third_sums(1)
    write(0)
    finish(1)
    write(1)
    drain(0)
    drain(1)


def reduce_call(gt, ct, lno, ao, x, cot, gain, w, factor):
    tok, cols = lno.shape
    dma = pltpu.SemaphoreType.DMA
    vm = pl.BlockSpec(memory_space=pltpu.VMEM)
    dim = gt.shape[1]
    scratch = [
        pltpu.VMEM((4, 4, 16, LANES), jnp.float32), dma((4, 3)), dma((4, 3)),
        pltpu.VMEM((2, 3, dim, cols), jnp.bfloat16), pltpu.VMEM((3 * LANES, cols), jnp.bfloat16),
        pltpu.VMEM((tok, cols), jnp.float32), pltpu.VMEM((1, cols), jnp.float32), dma((2,)),
    ]
    for lo, hi in column_halves(cols):
        bf = lambda *shape: pltpu.VMEM(shape + (hi - lo,), jnp.bfloat16)
        sizes = [size for _, size in PARTS]
        scratch += [bf(16, ROWS), bf(16, ROWS), bf(RING, ROWS)]
        scratch += [x for s in sizes for x in (bf(2, 2, s), bf(2, 4, s), bf(3, s))]
        scratch += [bf(2, sizes[0]), bf(3, sizes[1]), bf(3, sizes[2]), bf(sizes[0]), bf(ROWS)]
        scratch += [dma((16,))] * 2 + [dma((3, 2, 2))] * 2 + [dma((3, 2, 4))] * 2 + [dma((3, 6))] * 2 + [dma((11,))] * 2
    return pl.pallas_call(
        functools.partial(reduce_kernel, factor),
        out_shape=(
            jax.ShapeDtypeStruct((Q_ROWS, cols), jnp.float32),
            jax.ShapeDtypeStruct((ROWS - Q_ROWS, cols), jnp.float32),
            jax.ShapeDtypeStruct((cols,), jnp.float32),
            jax.ShapeDtypeStruct((tok, cols), jnp.bfloat16),
        ),
        in_specs=[vm] * 7 + [pl.BlockSpec(memory_space=pl.ANY)],
        out_specs=[vm] * 4,
        scratch_shapes=scratch,
        compiler_params=pltpu.CompilerParams(collective_id=0, has_side_effects=True, vmem_limit_bytes=63 * 2**20),
        cost_estimate=pl.CostEstimate(flops=2 * BLOCKS * ROWS * tok * cols, bytes_accessed=2**24, transcendentals=0),
    )(gt, ct, lno, ao, x, cot, gain, w)


def local(tokens, cotangent, ln_gain, w_qkv, w_out):
    images = tokens.shape[0] * lax.axis_size("wide") * lax.axis_size("narrow")
    factor = 1.0 / images
    x, cot = tokens[0], cotangent[0]
    ln_out, attn_out, grad_t, cot_t = front_call(x, cot, ln_gain, w_qkv, w_out)
    grad_t = grad_t.reshape(BLOCKS * 3 // 2, -1, cot.shape[0])
    w = w_qkv.reshape(3, HEADS, -1, cot.shape[1])
    grad_qkv, grad_out, gain, grad_input = reduce_call(grad_t, cot_t, ln_out, attn_out, x, cot, ln_gain, w, factor)
    return (grad_input[None], grad_qkv, grad_out, gain)


def solution(mesh):
    return jax.shard_map(
        local,
        mesh=mesh,
        in_specs=(
            P(("wide", "narrow"), None, None),
            P(("wide", "narrow"), None, None),
            P(),
            P(),
            P(),
        ),
        out_specs=(P(("wide", "narrow"), None, None), P("wide", None), P("wide", None), P()),
        check_vma=False,
    )
```

```python
import functools

import jax
import jax.numpy as jnp
from jax import lax
from jax.experimental import pallas as pl
from jax.experimental.pallas import tpu as pltpu
from jax.sharding import PartitionSpec as P

HEADS = 16


ln_epsilon = 1e-06


LANES = 128
WINDOW = 256
LOG2_E = 1.4426950408889634
TOGETHER = 4


def dot(a, b, over=((1,), (0,))):
    return lax.dot_general(a, b, (over, ((), ())), preferred_element_type=jnp.float32)


def low(a):
    return a.astype(jnp.bfloat16)


def normalise(x_ref):
    x = x_ref[...].astype(jnp.float32)
    centered = x - jnp.mean(x, axis=-1, keepdims=True)
    inv_sigma = lax.rsqrt(jnp.mean(centered * centered, axis=-1, keepdims=True) + ln_epsilon)
    return centered * inv_sigma, inv_sigma


def front_kernel(scale, x_ref, cot_ref, gain_ref, w_ref, wo_ref,
                 lno_ref, ao_ref, gt_ref, ct_ref, wpad):
    h = pl.program_id(0)
    dim = w_ref.shape[2]

    @pl.when(h == 0)
    def _():
        normed, _ = normalise(x_ref)
        lno_ref[...] = low(normed * gain_ref[...].reshape(1, -1))
        wpad[...] = jnp.zeros_like(wpad)

    pair = range(TOGETHER)
    for j in pair:
        for s in range(3):
            at = (3 * j + s) * LANES
            wpad[at : at + dim, :] = w_ref[s, j]
    qkv = low(dot(lno_ref[...], wpad[...], ((1,), (1,))))
    q, k, v = ([qkv[:, (3 * j + s) * LANES : (3 * j + s + 1) * LANES] for j in pair] for s in range(3))
    scores = [dot(q[j], k[j], ((1,), (1,))) for j in pair]

    lane = lax.broadcasted_iota(jnp.int32, (1, WINDOW), 1)
    starts = [jnp.minimum(lax.div((h * TOGETHER + j) * dim, LANES) * LANES, wo_ref.shape[1] - WINDOW) for j in pair]
    starts = [pl.multiple_of(start, LANES) for start in starts]
    offsets = [(h * TOGETHER + j) * dim - starts[j] for j in pair]
    grad = [dot(cot_ref[...], wo_ref[:, pl.ds(starts[j], WINDOW)]) for j in pair]
    back = [lax.rem(WINDOW - offsets[j], WINDOW) for j in pair]
    grad = [pltpu.roll(grad[j], back[j], 1)[:, :LANES] for j in pair]
    grad = [low(jnp.where(lane[:, :LANES] < dim, grad[j], 0.0)) for j in pair]
    grad_prob = [dot(grad[j], v[j], ((1,), (1,))) for j in pair]

    prob = []
    for j in pair:
        expo = jnp.exp2((scores[j] - jnp.max(scores[j], axis=-1, keepdims=True)) * (scale * LOG2_E))
        prob.append(expo * (1.0 / jnp.sum(expo, axis=-1, keepdims=True)))
    prob_low = [low(prob[j]) for j in pair]
    attn = [dot(prob_low[j], v[j]) for j in pair]
    for j in pair:
        gt_ref[2, j] = low(dot(grad[j], prob_low[j], ((0,), (0,)))[:dim])

    grad_score = []
    for j in pair:
        inner = jnp.sum(grad_prob[j] * prob[j], axis=-1, keepdims=True)
        grad_score.append(low(prob[j] * (grad_prob[j] - inner) * scale))
    for j in pair:
        gt_ref[1, j] = low(dot(q[j], grad_score[j], ((0,), (0,)))[:dim])
        gt_ref[0, j] = low(dot(grad_score[j], k[j]).T[:dim])

    for j in pair:
        part = cot_ref[:, pl.ds(starts[j], WINDOW)].astype(jnp.float32)
        ct_ref[j] = low(pltpu.roll(part, back[j], 1)[:, :LANES].T[:dim])
        wide = pltpu.roll(jnp.concatenate([attn[j], jnp.zeros_like(attn[j])], axis=1), offsets[j], 1)
        window = ao_ref[:, pl.ds(starts[j], WINDOW)].astype(jnp.float32)
        inside = jnp.logical_and(lane >= offsets[j], lane < offsets[j] + dim)
        ao_ref[:, pl.ds(starts[j], WINDOW)] = low(jnp.where(inside, wide, window))


def front_call(x, cot, gain, w_qkv, w_out):
    tok, width = x.shape
    dim = width // HEADS
    whole = lambda a: pl.BlockSpec(a.shape, lambda h: (0,) * len(a.shape))
    w = w_qkv.reshape(3, HEADS, dim, width)
    outs = (
        jax.ShapeDtypeStruct((tok, width), jnp.bfloat16),
        jax.ShapeDtypeStruct((tok, width), jnp.bfloat16),
        jax.ShapeDtypeStruct((3, HEADS, dim, tok), jnp.bfloat16),
        jax.ShapeDtypeStruct((HEADS, dim, tok), jnp.bfloat16),
    )
    return pl.pallas_call(
        functools.partial(front_kernel, dim**-0.5),
        grid=(HEADS // TOGETHER,),
        out_shape=outs,
        in_specs=[whole(x), whole(cot), whole(gain), pl.BlockSpec((3, TOGETHER, dim, width), lambda h: (0, h, 0, 0)), whole(w_out)],
        out_specs=[whole(outs[0]), whole(outs[1]), pl.BlockSpec((3, TOGETHER, dim, tok), lambda h: (0, h, 0, 0)),
                   pl.BlockSpec((TOGETHER, dim, tok), lambda h: (h, 0, 0))],
        scratch_shapes=[pltpu.VMEM((TOGETHER * 3 * LANES, width), jnp.bfloat16)],
        compiler_params=pltpu.CompilerParams(vmem_limit_bytes=56 * 2**20, dimension_semantics=("arbitrary",)),
        cost_estimate=pl.CostEstimate(flops=12 * 10**9, bytes_accessed=26 * 2**20, transcendentals=HEADS * tok * tok),
    )(x, cot, gain, w, w_out)


BLOCKS = 32
ROWS = 208
Q_ROWS = 156
PARTS = ((0, 80), (80, 64), (144, 64))
CUTS = (48, 32, 32)
RING = 6
LAG = 4
MESH = pl.DeviceIdType.MESH


def rem(a, b):
    return lax.rem(a, jnp.int32(b))


def div(a, b):
    return lax.div(a, jnp.int32(b))


def column_halves(cols):
    edge = (cols // LANES + 1) // 2 * LANES
    return ((0, edge), (edge, cols))


def reduce_kernel(factor, gt, ct, lno, ao, x_ref, cot_ref, gain_ref, w_hbm, qkv_out, out_out, gain_out, gx_ref,
                  G, sg, rg, wbuf, wpad, gln, row, wsem, *scratch):
    cols = lno.shape[1]
    spans = column_halves(cols)
    per = len(scratch) // 2
    sides = []
    for h in range(2):
        s = scratch[h * per : (h + 1) * per]
        sides.append(dict(S=s[0], R0=s[1], T0=s[2], halves=(s[3], s[6], s[9]), wholes=(s[4], s[7], s[10]),
                          later=(s[5], s[8], s[11]), C=s[12:15], T1=s[15], F=s[16], sems=s[17:27]))

    wide, narrow = lax.axis_index("wide"), lax.axis_index("narrow")
    xh, y, z = div(wide, 16), rem(div(wide, 4), 4), rem(wide, 4)
    xl, c = div(narrow, 2), rem(narrow, 2)
    x = 2 * xh + xl
    place = (x, y, z)

    def device(x_, y_, z_, c_):
        return (div(x_, 2) * 16 + y_ * 4 + z_, rem(x_, 2) * 2 + c_)

    def shift(dim, by):
        at = [x, y, z]
        at[dim] = rem(at[dim] + by, 4)
        return device(*at, c)

    mate = device(x, y, z, 1 - c)
    peers = [mate] + [shift(d, by) for d in range(3) for by in (1, 2, 3)]
    barrier = pltpu.get_barrier_semaphore()
    for peer in peers:
        pl.semaphore_signal(barrier, inc=1, device_id=peer, device_id_type=MESH)
    pl.semaphore_wait(barrier, len(peers))

    def remote(src, dst, ssem, rsem, to):
        return pltpu.make_async_remote_copy(src_ref=src, dst_ref=dst, send_sem=ssem, recv_sem=rsem,
                                            device_id=to, device_id_type=MESH)

    def accumulate(dst, *more):
        total = dst[...].astype(jnp.float32)
        for term in more:
            total = total + term[...].astype(jnp.float32)
        dst[...] = total.astype(jnp.bfloat16)

    rings = ((2, c, lambda r: mate), (4, x, lambda r: shift(0, r)), (4, y, lambda r: shift(1, r)), (4, z, lambda r: shift(2, r)))
    gain_copies = []

    def gain_start(k):
        n, m, to = rings[k]
        if k == 0:
            G[k, m] = jnp.zeros(G.shape[2:], jnp.float32)
            for i in range(cols // LANES):
                G[k, m, i : i + 1, :] = row[:, i * LANES : (i + 1) * LANES]
        else:
            G[k, m] = gain_total(k - 1)
        for r in range(n - 1):
            copy = remote(G.at[k, m], G.at[k, m], sg.at[k, r], rg.at[k, r], to(r + 1))
            copy.start()
            gain_copies.append(copy)

    def gain_total(k):
        total = G[k, 0]
        for other in range(1, rings[k][0]):
            total = total + G[k, other]
        return total

    def gain_end(k):
        while gain_copies:
            gain_copies.pop().wait()
        if k == 3:
            total = gain_total(k) * factor
            for i in range(cols // LANES):
                gain_out[i * LANES : (i + 1) * LANES] = total[i]

    def weights(h, slot):
        return pltpu.make_async_copy(w_hbm.at[:, h], wbuf.at[slot], wsem.at[slot])

    def input_gradient():
        dim = gt.shape[1]
        gln[...] = jnp.zeros_like(gln)
        wpad[...] = jnp.zeros_like(wpad)

        @pl.loop(0, HEADS)
        def _(h):
            slot = rem(h, 2)
            weights(h, slot).wait()

            @pl.when(h < HEADS - 1)
            def _():
                weights(h + 1, 1 - slot).start()

            pad = jnp.zeros((LANES - dim, gt.shape[2]), jnp.float32)
            stack = []
            for s in range(3):
                wpad[s * LANES : s * LANES + dim, :] = wbuf[slot, s]
                stack += [gt[s * HEADS + h].astype(jnp.float32), pad]
            gln[...] += dot(low(jnp.concatenate(stack, axis=0).T), wpad[...])

        normed, inv_sigma = normalise(x_ref)
        grad_ln = gln[...]
        row[...] = jnp.sum(grad_ln * normed, axis=0, keepdims=True)
        g = grad_ln * gain_ref[...].reshape(1, -1)
        grad_x = inv_sigma * (
            g - jnp.mean(g, axis=-1, keepdims=True) - normed * jnp.mean(g * normed, axis=-1, keepdims=True)
        )
        gx_ref[...] = low(cot_ref[...].astype(jnp.float32) + grad_x)

    def rows_of_pair(b):
        g = jnp.concatenate([gt[3 * b + i].astype(jnp.float32) for i in range(3)], axis=0)
        d = ct[b].astype(jnp.float32)
        out_rows = ROWS - Q_ROWS
        return tuple(
            jnp.concatenate([g[i * Q_ROWS : (i + 1) * Q_ROWS], d[i * out_rows : (i + 1) * out_rows]], axis=0)
            for i in range(2)
        )

    def product(left, right, lo, hi):
        full = right.shape[0] // 256 * 256
        total = dot(low(left[:, :full]), right[0:full, lo:hi])
        for k in range(full, right.shape[0]):
            total = total + left[:, k : k + 1] * right[k : k + 1, lo:hi].astype(jnp.float32)
        return total * factor

    def fill(side, span, b, slot):
        even, odd = rows_of_pair(b)
        mine_odd = rem(c + div(b, 8) + rem(div(b, 2), 4), 2) == 1
        give, keep = jnp.where(mine_odd, even, odd), jnp.where(mine_odd, odd, even)
        first = jnp.concatenate([give[0:160], keep[0:160]], axis=0)
        last = jnp.concatenate([give[144:208], keep[144:208]], axis=0)
        line = lax.broadcasted_iota(jnp.int32, (16, 1), 0)
        width = span[1] - span[0]
        for lo in range(0, width, 512):
            hi = min(width, lo + 512)
            p = product(first, lno, span[0] + lo, span[0] + hi)
            q = product(last, ao, span[0] + lo, span[0] + hi)
            for k, dst, at in ((0, side["T0"], slot), (1, side["S"], b)):
                u, v = p[160 * k : 160 * k + 160], q[64 * k : 64 * k + 64]
                dst[at, 0:144, lo:hi] = low(u[0:144])
                dst[at, 144:160, lo:hi] = low(jnp.where(line < Q_ROWS - 144, u[144:160], v[0:16]))
                dst[at, 160:208, lo:hi] = low(v[16:64])

    def core_copy(side, b, slot):
        return remote(side["T0"].at[slot], side["R0"].at[b], side["sems"][0].at[b], side["sems"][1].at[b], mate)

    def produce(h):
        side = sides[h]

        @pl.loop(0, 16 + LAG)
        def _(n):
            @pl.when(n < 16)
            def _():
                slot = rem(n, RING)

                @pl.when(n >= RING)
                def _():
                    core_copy(side, n - RING, slot).wait_send()

                fill(side, spans[h], n, slot)
                core_copy(side, n, slot).start()

            @pl.when(n >= LAG)
            def _():
                b = n - LAG
                core_copy(side, b, 0).wait_recv()
                accumulate(side["S"].at[b], side["R0"].at[b])

        for n in range(16 - RING, 16):
            core_copy(side, n, n % RING).wait_send()

    orders = ((1, 2, 0), (2, 0, 1), (0, 1, 2))
    firsts = (
        lambda t, i: (i // 2) * 8 + t * 2 + i % 2,
        lambda t, i: (i // 2) * 8 + (2 * (i % 2) + rem(c + t + i // 2, 2)) * 2 + div(t, 2),
        lambda t, i: div(t, 2) * 8 + i * 2 + rem(t, 2),
    )
    seconds = (
        lambda t: (rem(c + y + t, 2) * 8 + y * 2 + div(t, 2), rem(c + y + t, 2) * 2 + div(t, 2)),
        lambda t: (div(t, 2) * 8 + (2 * rem(t, 2) + rem(c + z + div(t, 2), 2)) * 2 + div(z, 2), t),
        lambda t: (div(x, 2) * 8 + t * 2 + rem(x, 2), t),
    )

    def part(h, p, b):
        return sides[h]["S"].at[b, pl.ds(*PARTS[p]), :]

    def half_copy(h, p, to, i, src):
        sems = sides[h]["sems"]
        return remote(src, sides[h]["halves"][p].at[to, i], sems[2].at[p, to, i], sems[3].at[p, to, i],
                      shift(orders[p][0], 1 + 2 * to))

    def whole_copy(h, p, to, i, src):
        sems = sides[h]["sems"]
        return remote(src, sides[h]["wholes"][p].at[to, i], sems[4].at[p, to, i], sems[5].at[p, to, i],
                      shift(orders[p][0], 1 + 2 * to))

    six = [(p, to) for to in range(2) for p in range(3)]

    def first_sends(h):
        for i in range(2):
            for p, to in six:
                t = rem(place[orders[p][0]] + 2, 4)
                half_copy(h, p, to, i, part(h, p, firsts[p](t, i + 2 * to))).start()
        for i in range(2):
            for p, to in six:
                t = rem(place[orders[p][0]] + 1 + 2 * to, 4)
                index = i + 2 - 2 * to
                whole_copy(h, p, to, index, part(h, p, firsts[p](t, index))).start()

    def first_relays(h):
        for i in range(2):
            for p, to in six:
                halves = sides[h]["halves"][p]
                half_copy(h, p, to, i, halves.at[to, i]).wait_recv()
                t = rem(place[orders[p][0]] + 1 + 2 * to, 4)
                index = i + 2 * to
                block = part(h, p, firsts[p](t, index))
                accumulate(block, halves.at[to, i])
                whole_copy(h, p, to, index, block).start()

    def ready(h, p, t):
        b, i = seconds[p](t)
        wholes = sides[h]["wholes"][p]
        for to in range(2):
            whole_copy(h, p, to, i, wholes.at[to, i]).wait_recv()
        accumulate(part(h, p, b), wholes.at[0, i], wholes.at[1, i])
        return part(h, p, b)

    def second_copy(h, p, k, what):
        edge = CUTS[p]
        lower, upper = pl.ds(0, edge), pl.ds(edge, PARTS[p][1] - edge)
        rows, slot, by = ((lower, 0, 1), (upper, 0, 3), (upper, 1, 1), (lower, 2, 3), (lower, 1, 1), (upper, 2, 3))[k]
        sems = sides[h]["sems"]
        return remote(what.at[rows], sides[h]["later"][p].at[slot, rows], sems[6].at[p, k], sems[7].at[p, k],
                      shift(orders[p][1], by))

    def block2(h, p, by):
        return part(h, p, seconds[p](rem(place[orders[p][1]] + by, 4))[0])

    def second_sends(h):
        for p in range(3):
            opposite = ready(h, p, rem(place[orders[p][1]] + 2, 4))
            second_copy(h, p, 0, opposite).start()
            second_copy(h, p, 1, opposite).start()
        for p in range(3):
            second_copy(h, p, 2, ready(h, p, rem(place[orders[p][1]] + 1, 4))).start()
            second_copy(h, p, 3, ready(h, p, rem(place[orders[p][1]] + 3, 4))).start()

    def second_relays(h):
        for p in range(3):
            edge = CUTS[p]
            inbox = sides[h]["later"][p]
            for k, by, rows in ((0, 1, pl.ds(0, edge)), (1, 3, pl.ds(edge, PARTS[p][1] - edge))):
                what = block2(h, p, by)
                second_copy(h, p, k, what).wait_recv()
                accumulate(what.at[rows], inbox.at[0, rows])
                second_copy(h, p, 4 + k, what).start()
        for p in range(3):
            ready(h, p, place[orders[p][1]])

    chosen = c == rem(xh + y + z, 2)
    partner = device(2 * xh + 1 - xl, y, z, c)
    outward = device(rem(x + 3 + 2 * xl, 4), y, z, c)
    y_to = 2 * xl + rem(c + z + xh, 2)
    z_to = 2 * xl + rem(c + y + xh, 2)
    reach = ((1, 2, y_to, y, lambda: device(x, y_to, z, c)), (2, 5, z_to, z, lambda: device(x, y, z_to, c)))

    def third(h, src, dst, k, to):
        sems = sides[h]["sems"]
        return remote(src, dst, sems[8].at[k], sems[9].at[k], to)

    def mine(h, p):
        return block2(h, p, 0)

    def final(h, p):
        return sides[h]["F"].at[pl.ds(*PARTS[p]), :]

    def to_pair(h):
        return third(h, mine(h, 0), sides[h]["C"][0].at[0], 0, outward)

    def swap(h):
        return third(h, sides[h]["T1"], sides[h]["C"][0].at[1], 1, partner)

    def share(h, p):
        return third(h, final(h, p), final(h, p), 7 + p, partner)

    def hand(h):
        return third(h, sides[h]["F"], sides[h]["F"], 10, mate)

    def third_sends(h):
        for p in range(3):
            for k in range(2, 6):
                second_copy(h, p, k, mine(h, p)).wait_recv()
            accumulate(mine(h, p), sides[h]["later"][p].at[1], sides[h]["later"][p].at[2])
            if p == 0:
                @pl.when(jnp.logical_not(chosen))
                def _():
                    to_pair(h).start()
            else:
                _, base, to, at, where = reach[p - 1]
                for r in range(3):
                    @pl.when(rem(at - to + 4, 4) == r + 1)
                    def _():
                        third(h, mine(h, p), sides[h]["C"][p].at[r], base + r, where()).start()

    def third_sums(h):
        side = sides[h]

        @pl.when(chosen)
        def _():
            to_pair(h).wait_recv()
            side["T1"][...] = low(mine(h, 0)[...].astype(jnp.float32) + side["C"][0][0].astype(jnp.float32))
            swap(h).start()

        for p, base, to, at, where in reach:
            @pl.when(at == to)
            def _():
                total = mine(h, p)[...].astype(jnp.float32)
                for r in range(3):
                    third(h, mine(h, p), side["C"][p].at[r], base + r, mate).wait_recv()
                    total = total + side["C"][p][r].astype(jnp.float32)
                final(h, p)[...] = low(total)
                share(h, p).start()

    def finish(h):
        side = sides[h]

        @pl.when(chosen)
        def _():
            swap(h).wait_recv()
            final(h, 0)[...] = low(side["T1"][...].astype(jnp.float32) + side["C"][0][1].astype(jnp.float32))

        for p, base, to, at, where in reach:
            @pl.when(jnp.logical_and(chosen, at != to))
            def _():
                share(h, p).wait_recv()

        @pl.when(chosen)
        def _():
            hand(h).start()

    def write(h):
        @pl.when(jnp.logical_not(chosen))
        def _():
            hand(h).wait_recv()

        total = sides[h]["F"][...].astype(jnp.float32)
        qkv_out[:, spans[h][0] : spans[h][1]] = total[:Q_ROWS]
        out_out[:, spans[h][0] : spans[h][1]] = total[Q_ROWS:]

    def drain(h):
        for p in range(3):
            for to in range(2):
                for i in range(4):
                    whole_copy(h, p, to, i, sides[h]["wholes"][p].at[to, i]).wait_send()
                for i in range(2):
                    half_copy(h, p, to, i, sides[h]["halves"][p].at[to, i]).wait_send()
            for k in range(6):
                second_copy(h, p, k, mine(h, p)).wait_send()

        @pl.when(chosen)
        def _():
            swap(h).wait_send()
            hand(h).wait_send()

        @pl.when(jnp.logical_not(chosen))
        def _():
            to_pair(h).wait_send()

        for p, base, to, at, where in reach:
            @pl.when(at == to)
            def _():
                share(h, p).wait_send()

            for r in range(3):
                @pl.when(rem(at - to + 4, 4) == r + 1)
                def _():
                    third(h, mine(h, p), sides[h]["C"][p].at[r], base + r, where()).wait_send()

    weights(0, 0).start()
    produce(0)
    first_sends(0)
    produce(1)
    first_relays(0)
    first_sends(1)
    input_gradient()
    gain_start(0)
    second_sends(0)
    gain_end(0)
    gain_start(1)
    first_relays(1)
    gain_end(1)
    gain_start(2)
    second_relays(0)
    second_sends(1)
    third_sends(0)
    gain_end(2)
    gain_start(3)
    second_relays(1)
    third_sums(0)
    third_sends(1)
    finish(0)
    gain_end(3)
    third_sums(1)
    write(0)
    finish(1)
    write(1)
    drain(0)
    drain(1)


def reduce_call(gt, ct, lno, ao, x, cot, gain, w, factor):
    tok, cols = lno.shape
    dma = pltpu.SemaphoreType.DMA
    vm = pl.BlockSpec(memory_space=pltpu.VMEM)
    dim = gt.shape[1]
    scratch = [
        pltpu.VMEM((4, 4, 16, LANES), jnp.float32), dma((4, 3)), dma((4, 3)),
        pltpu.VMEM((2, 3, dim, cols), jnp.bfloat16), pltpu.VMEM((3 * LANES, cols), jnp.bfloat16),
        pltpu.VMEM((tok, cols), jnp.float32), pltpu.VMEM((1, cols), jnp.float32), dma((2,)),
    ]
    for lo, hi in column_halves(cols):
        bf = lambda *shape: pltpu.VMEM(shape + (hi - lo,), jnp.bfloat16)
        sizes = [size for _, size in PARTS]
        scratch += [bf(16, ROWS), bf(16, ROWS), bf(RING, ROWS)]
        scratch += [x for s in sizes for x in (bf(2, 2, s), bf(2, 4, s), bf(3, s))]
        scratch += [bf(2, sizes[0]), bf(3, sizes[1]), bf(3, sizes[2]), bf(sizes[0]), bf(ROWS)]
        scratch += [dma((16,))] * 2 + [dma((3, 2, 2))] * 2 + [dma((3, 2, 4))] * 2 + [dma((3, 6))] * 2 + [dma((11,))] * 2
    return pl.pallas_call(
        functools.partial(reduce_kernel, factor),
        out_shape=(
            jax.ShapeDtypeStruct((Q_ROWS, cols), jnp.float32),
            jax.ShapeDtypeStruct((ROWS - Q_ROWS, cols), jnp.float32),
            jax.ShapeDtypeStruct((cols,), jnp.float32),
            jax.ShapeDtypeStruct((tok, cols), jnp.bfloat16),
        ),
        in_specs=[vm] * 7 + [pl.BlockSpec(memory_space=pl.ANY)],
        out_specs=[vm] * 4,
        scratch_shapes=scratch,
        compiler_params=pltpu.CompilerParams(collective_id=0, has_side_effects=True, vmem_limit_bytes=63 * 2**20),
        cost_estimate=pl.CostEstimate(flops=2 * BLOCKS * ROWS * tok * cols, bytes_accessed=2**24, transcendentals=0),
    )(gt, ct, lno, ao, x, cot, gain, w)


def local(tokens, cotangent, ln_gain, w_qkv, w_out):
    images = tokens.shape[0] * lax.axis_size("wide") * lax.axis_size("narrow")
    factor = 1.0 / images
    x, cot = tokens[0], cotangent[0]
    ln_out, attn_out, grad_t, cot_t = front_call(x, cot, ln_gain, w_qkv, w_out)
    grad_t = grad_t.reshape(BLOCKS * 3 // 2, -1, cot.shape[0])
    w = w_qkv.reshape(3, HEADS, -1, cot.shape[1])
    grad_qkv, grad_out, gain, grad_input = reduce_call(grad_t, cot_t, ln_out, attn_out, x, cot, ln_gain, w, factor)
    return (grad_input[None], grad_qkv, grad_out, gain)


def solution(mesh):
    return jax.shard_map(
        local,
        mesh=mesh,
        in_specs=(
            P(("wide", "narrow"), None, None),
            P(("wide", "narrow"), None, None),
            P(),
            P(),
            P(),
        ),
        out_specs=(P(("wide", "narrow"), None, None), P("wide", None), P("wide", None), P()),
        check_vma=False,
    )
```

```python
import functools

import jax
import jax.numpy as jnp
from jax import lax
from jax.experimental import pallas as pl
from jax.experimental.pallas import tpu as pltpu
from jax.sharding import PartitionSpec as P

HEADS = 16


ln_epsilon = 1e-06


LANES = 128
WINDOW = 256
LOG2_E = 1.4426950408889634
TOGETHER = 4


def dot(a, b, over=((1,), (0,))):
    return lax.dot_general(a, b, (over, ((), ())), preferred_element_type=jnp.float32)


def low(a):
    return a.astype(jnp.bfloat16)


def normalise(x_ref):
    x = x_ref[...].astype(jnp.float32)
    centered = x - jnp.mean(x, axis=-1, keepdims=True)
    inv_sigma = lax.rsqrt(jnp.mean(centered * centered, axis=-1, keepdims=True) + ln_epsilon)
    return centered * inv_sigma, inv_sigma


def front_kernel(scale, x_ref, cot_ref, gain_ref, w_ref, wo_hbm,
                 lno_ref, ao_ref, gt_ref, ct_ref, wpad, wo_ref, wo_sem):
    h = pl.program_id(0)
    dim = w_ref.shape[2]
    fetch = pltpu.make_async_copy(wo_hbm, wo_ref, wo_sem)

    @pl.when(h == 0)
    def _():
        fetch.start()
        normed, _ = normalise(x_ref)
        lno_ref[...] = low(normed * gain_ref[...].reshape(1, -1))
        wpad[...] = jnp.zeros_like(wpad)

    pair = range(TOGETHER)
    for j in pair:
        for s in range(3):
            at = (3 * j + s) * LANES
            wpad[at : at + dim, :] = w_ref[s, j]
    qkv = low(dot(lno_ref[...], wpad[...], ((1,), (1,))))
    q, k, v = ([qkv[:, (3 * j + s) * LANES : (3 * j + s + 1) * LANES] for j in pair] for s in range(3))
    scores = [dot(q[j], k[j], ((1,), (1,))) for j in pair]

    lane = lax.broadcasted_iota(jnp.int32, (1, WINDOW), 1)
    starts = [jnp.minimum(lax.div((h * TOGETHER + j) * dim, LANES) * LANES, wo_ref.shape[1] - WINDOW) for j in pair]
    starts = [pl.multiple_of(start, LANES) for start in starts]
    offsets = [(h * TOGETHER + j) * dim - starts[j] for j in pair]
    @pl.when(h == 0)
    def _():
        fetch.wait()

    grad = [dot(cot_ref[...], wo_ref[:, pl.ds(starts[j], WINDOW)]) for j in pair]
    back = [lax.rem(WINDOW - offsets[j], WINDOW) for j in pair]
    grad = [pltpu.roll(grad[j], back[j], 1)[:, :LANES] for j in pair]
    grad = [low(jnp.where(lane[:, :LANES] < dim, grad[j], 0.0)) for j in pair]
    grad_prob = [dot(grad[j], v[j], ((1,), (1,))) for j in pair]

    prob = []
    for j in pair:
        expo = jnp.exp2((scores[j] - jnp.max(scores[j], axis=-1, keepdims=True)) * (scale * LOG2_E))
        prob.append(expo * (1.0 / jnp.sum(expo, axis=-1, keepdims=True)))
    prob_low = [low(prob[j]) for j in pair]
    attn = [dot(prob_low[j], v[j]) for j in pair]
    for j in pair:
        gt_ref[2, j] = low(dot(grad[j], prob_low[j], ((0,), (0,)))[:dim])

    grad_score = []
    for j in pair:
        inner = jnp.sum(grad_prob[j] * prob[j], axis=-1, keepdims=True)
        grad_score.append(low(prob[j] * (grad_prob[j] - inner) * scale))
    for j in pair:
        gt_ref[1, j] = low(dot(q[j], grad_score[j], ((0,), (0,)))[:dim])
        gt_ref[0, j] = low(dot(grad_score[j], k[j]).T[:dim])

    for j in pair:
        part = cot_ref[:, pl.ds(starts[j], WINDOW)].astype(jnp.float32)
        ct_ref[j] = low(pltpu.roll(part, back[j], 1)[:, :LANES].T[:dim])
        wide = pltpu.roll(jnp.concatenate([attn[j], jnp.zeros_like(attn[j])], axis=1), offsets[j], 1)
        window = ao_ref[:, pl.ds(starts[j], WINDOW)].astype(jnp.float32)
        inside = jnp.logical_and(lane >= offsets[j], lane < offsets[j] + dim)
        ao_ref[:, pl.ds(starts[j], WINDOW)] = low(jnp.where(inside, wide, window))


def front_call(x, cot, gain, w_qkv, w_out):
    tok, width = x.shape
    dim = width // HEADS
    whole = lambda a: pl.BlockSpec(a.shape, lambda h: (0,) * len(a.shape))
    w = w_qkv.reshape(3, HEADS, dim, width)
    outs = (
        jax.ShapeDtypeStruct((tok, width), jnp.bfloat16),
        jax.ShapeDtypeStruct((tok, width), jnp.bfloat16),
        jax.ShapeDtypeStruct((3, HEADS, dim, tok), jnp.bfloat16),
        jax.ShapeDtypeStruct((HEADS, dim, tok), jnp.bfloat16),
    )
    return pl.pallas_call(
        functools.partial(front_kernel, dim**-0.5),
        grid=(HEADS // TOGETHER,),
        out_shape=outs,
        in_specs=[whole(x), whole(cot), whole(gain), pl.BlockSpec((3, TOGETHER, dim, width), lambda h: (0, h, 0, 0)), pl.BlockSpec(memory_space=pl.ANY)],
        out_specs=[whole(outs[0]), whole(outs[1]), pl.BlockSpec((3, TOGETHER, dim, tok), lambda h: (0, h, 0, 0)),
                   pl.BlockSpec((TOGETHER, dim, tok), lambda h: (h, 0, 0))],
        scratch_shapes=[pltpu.VMEM((TOGETHER * 3 * LANES, width), jnp.bfloat16), pltpu.VMEM(w_out.shape, jnp.bfloat16), pltpu.SemaphoreType.DMA],
        compiler_params=pltpu.CompilerParams(vmem_limit_bytes=56 * 2**20, dimension_semantics=("arbitrary",)),
        cost_estimate=pl.CostEstimate(flops=12 * 10**9, bytes_accessed=26 * 2**20, transcendentals=HEADS * tok * tok),
    )(x, cot, gain, w, w_out)


BLOCKS = 32
ROWS = 208
Q_ROWS = 156
PARTS = ((0, 80), (80, 64), (144, 64))
CUTS = (48, 32, 32)
RING = 6
LAG = 4
MESH = pl.DeviceIdType.MESH


def rem(a, b):
    return lax.rem(a, jnp.int32(b))


def div(a, b):
    return lax.div(a, jnp.int32(b))


def column_halves(cols):
    edge = (cols // LANES + 1) // 2 * LANES
    return ((0, edge), (edge, cols))


def reduce_kernel(factor, gt, ct, lno, ao, x_ref, cot_ref, gain_ref, w_hbm, qkv_out, out_out, gain_out, gx_ref,
                  G, sg, rg, wbuf, wpad, gln, row, wsem, *scratch):
    cols = lno.shape[1]
    spans = column_halves(cols)
    per = len(scratch) // 2
    sides = []
    for h in range(2):
        s = scratch[h * per : (h + 1) * per]
        sides.append(dict(S=s[0], R0=s[1], T0=s[2], halves=(s[3], s[6], s[9]), wholes=(s[4], s[7], s[10]),
                          later=(s[5], s[8], s[11]), C=s[12:15], T1=s[15], F=s[16], sems=s[17:27]))

    wide, narrow = lax.axis_index("wide"), lax.axis_index("narrow")
    xh, y, z = div(wide, 16), rem(div(wide, 4), 4), rem(wide, 4)
    xl, c = div(narrow, 2), rem(narrow, 2)
    x = 2 * xh + xl
    place = (x, y, z)

    def device(x_, y_, z_, c_):
        return (div(x_, 2) * 16 + y_ * 4 + z_, rem(x_, 2) * 2 + c_)

    def shift(dim, by):
        at = [x, y, z]
        at[dim] = rem(at[dim] + by, 4)
        return device(*at, c)

    mate = device(x, y, z, 1 - c)
    peers = [mate] + [shift(d, by) for d in range(3) for by in (1, 2, 3)]
    barrier = pltpu.get_barrier_semaphore()
    for peer in peers:
        pl.semaphore_signal(barrier, inc=1, device_id=peer, device_id_type=MESH)
    pl.semaphore_wait(barrier, len(peers))

    def remote(src, dst, ssem, rsem, to):
        return pltpu.make_async_remote_copy(src_ref=src, dst_ref=dst, send_sem=ssem, recv_sem=rsem,
                                            device_id=to, device_id_type=MESH)

    def accumulate(dst, *more):
        total = dst[...].astype(jnp.float32)
        for term in more:
            total = total + term[...].astype(jnp.float32)
        dst[...] = total.astype(jnp.bfloat16)

    rings = ((2, c, lambda r: mate), (4, x, lambda r: shift(0, r)), (4, y, lambda r: shift(1, r)), (4, z, lambda r: shift(2, r)))
    gain_copies = []

    def gain_start(k):
        n, m, to = rings[k]
        if k == 0:
            G[k, m] = jnp.zeros(G.shape[2:], jnp.float32)
            for i in range(cols // LANES):
                G[k, m, i : i + 1, :] = row[:, i * LANES : (i + 1) * LANES]
        else:
            G[k, m] = gain_total(k - 1)
        for r in range(n - 1):
            copy = remote(G.at[k, m], G.at[k, m], sg.at[k, r], rg.at[k, r], to(r + 1))
            copy.start()
            gain_copies.append(copy)

    def gain_total(k):
        total = G[k, 0]
        for other in range(1, rings[k][0]):
            total = total + G[k, other]
        return total

    def gain_end(k):
        while gain_copies:
            gain_copies.pop().wait()
        if k == 3:
            total = gain_total(k) * factor
            for i in range(cols // LANES):
                gain_out[i * LANES : (i + 1) * LANES] = total[i]

    def weights(h, slot):
        return pltpu.make_async_copy(w_hbm.at[:, h], wbuf.at[slot], wsem.at[slot])

    def input_gradient():
        dim = gt.shape[1]
        gln[...] = jnp.zeros_like(gln)
        wpad[...] = jnp.zeros_like(wpad)

        @pl.loop(0, HEADS)
        def _(h):
            slot = rem(h, 2)
            weights(h, slot).wait()

            @pl.when(h < HEADS - 1)
            def _():
                weights(h + 1, 1 - slot).start()

            pad = jnp.zeros((LANES - dim, gt.shape[2]), jnp.float32)
            stack = []
            for s in range(3):
                wpad[s * LANES : s * LANES + dim, :] = wbuf[slot, s]
                stack += [gt[s * HEADS + h].astype(jnp.float32), pad]
            gln[...] += dot(low(jnp.concatenate(stack, axis=0).T), wpad[...])

        normed, inv_sigma = normalise(x_ref)
        grad_ln = gln[...]
        row[...] = jnp.sum(grad_ln * normed, axis=0, keepdims=True)
        g = grad_ln * gain_ref[...].reshape(1, -1)
        grad_x = inv_sigma * (
            g - jnp.mean(g, axis=-1, keepdims=True) - normed * jnp.mean(g * normed, axis=-1, keepdims=True)
        )
        gx_ref[...] = low(cot_ref[...].astype(jnp.float32) + grad_x)

    def rows_of_pair(b):
        g = jnp.concatenate([gt[3 * b + i].astype(jnp.float32) for i in range(3)], axis=0)
        d = ct[b].astype(jnp.float32)
        out_rows = ROWS - Q_ROWS
        return tuple(
            jnp.concatenate([g[i * Q_ROWS : (i + 1) * Q_ROWS], d[i * out_rows : (i + 1) * out_rows]], axis=0)
            for i in range(2)
        )

    def product(left, right, lo, hi):
        full = right.shape[0] // 256 * 256
        total = dot(low(left[:, :full]), right[0:full, lo:hi])
        for k in range(full, right.shape[0]):
            total = total + left[:, k : k + 1] * right[k : k + 1, lo:hi].astype(jnp.float32)
        return total * factor

    def fill(side, span, b, slot):
        even, odd = rows_of_pair(b)
        mine_odd = rem(c + div(b, 8) + rem(div(b, 2), 4), 2) == 1
        give, keep = jnp.where(mine_odd, even, odd), jnp.where(mine_odd, odd, even)
        first = jnp.concatenate([give[0:160], keep[0:160]], axis=0)
        last = jnp.concatenate([give[144:208], keep[144:208]], axis=0)
        line = lax.broadcasted_iota(jnp.int32, (16, 1), 0)
        width = span[1] - span[0]
        for lo in range(0, width, 512):
            hi = min(width, lo + 512)
            p = product(first, lno, span[0] + lo, span[0] + hi)
            q = product(last, ao, span[0] + lo, span[0] + hi)
            for k, dst, at in ((0, side["T0"], slot), (1, side["S"], b)):
                u, v = p[160 * k : 160 * k + 160], q[64 * k : 64 * k + 64]
                dst[at, 0:144, lo:hi] = low(u[0:144])
                dst[at, 144:160, lo:hi] = low(jnp.where(line < Q_ROWS - 144, u[144:160], v[0:16]))
                dst[at, 160:208, lo:hi] = low(v[16:64])

    def core_copy(side, b, slot):
        return remote(side["T0"].at[slot], side["R0"].at[b], side["sems"][0].at[b], side["sems"][1].at[b], mate)

    def produce(h):
        side = sides[h]

        @pl.loop(0, 16 + LAG)
        def _(n):
            @pl.when(n < 16)
            def _():
                slot = rem(n, RING)

                @pl.when(n >= RING)
                def _():
                    core_copy(side, n - RING, slot).wait_send()

                fill(side, spans[h], n, slot)
                core_copy(side, n, slot).start()

            @pl.when(n >= LAG)
            def _():
                b = n - LAG
                core_copy(side, b, 0).wait_recv()
                accumulate(side["S"].at[b], side["R0"].at[b])

        for n in range(16 - RING, 16):
            core_copy(side, n, n % RING).wait_send()

    orders = ((1, 2, 0), (2, 0, 1), (0, 1, 2))
    firsts = (
        lambda t, i: (i // 2) * 8 + t * 2 + i % 2,
        lambda t, i: (i // 2) * 8 + (2 * (i % 2) + rem(c + t + i // 2, 2)) * 2 + div(t, 2),
        lambda t, i: div(t, 2) * 8 + i * 2 + rem(t, 2),
    )
    seconds = (
        lambda t: (rem(c + y + t, 2) * 8 + y * 2 + div(t, 2), rem(c + y + t, 2) * 2 + div(t, 2)),
        lambda t: (div(t, 2) * 8 + (2 * rem(t, 2) + rem(c + z + div(t, 2), 2)) * 2 + div(z, 2), t),
        lambda t: (div(x, 2) * 8 + t * 2 + rem(x, 2), t),
    )

    def part(h, p, b):
        return sides[h]["S"].at[b, pl.ds(*PARTS[p]), :]

    def half_copy(h, p, to, i, src):
        sems = sides[h]["sems"]
        return remote(src, sides[h]["halves"][p].at[to, i], sems[2].at[p, to, i], sems[3].at[p, to, i],
                      shift(orders[p][0], 1 + 2 * to))

    def whole_copy(h, p, to, i, src):
        sems = sides[h]["sems"]
        return remote(src, sides[h]["wholes"][p].at[to, i], sems[4].at[p, to, i], sems[5].at[p, to, i],
                      shift(orders[p][0], 1 + 2 * to))

    six = [(p, to) for to in range(2) for p in range(3)]

    def first_sends(h):
        for i in range(2):
            for p, to in six:
                t = rem(place[orders[p][0]] + 2, 4)
                half_copy(h, p, to, i, part(h, p, firsts[p](t, i + 2 * to))).start()
        for i in range(2):
            for p, to in six:
                t = rem(place[orders[p][0]] + 1 + 2 * to, 4)
                index = i + 2 - 2 * to
                whole_copy(h, p, to, index, part(h, p, firsts[p](t, index))).start()

    def first_relays(h):
        for i in range(2):
            for p, to in six:
                halves = sides[h]["halves"][p]
                half_copy(h, p, to, i, halves.at[to, i]).wait_recv()
                t = rem(place[orders[p][0]] + 1 + 2 * to, 4)
                index = i + 2 * to
                block = part(h, p, firsts[p](t, index))
                accumulate(block, halves.at[to, i])
                whole_copy(h, p, to, index, block).start()

    def ready(h, p, t):
        b, i = seconds[p](t)
        wholes = sides[h]["wholes"][p]
        for to in range(2):
            whole_copy(h, p, to, i, wholes.at[to, i]).wait_recv()
        accumulate(part(h, p, b), wholes.at[0, i], wholes.at[1, i])
        return part(h, p, b)

    def second_copy(h, p, k, what):
        edge = CUTS[p]
        lower, upper = pl.ds(0, edge), pl.ds(edge, PARTS[p][1] - edge)
        rows, slot, by = ((lower, 0, 1), (upper, 0, 3), (upper, 1, 1), (lower, 2, 3), (lower, 1, 1), (upper, 2, 3))[k]
        sems = sides[h]["sems"]
        return remote(what.at[rows], sides[h]["later"][p].at[slot, rows], sems[6].at[p, k], sems[7].at[p, k],
                      shift(orders[p][1], by))

    def block2(h, p, by):
        return part(h, p, seconds[p](rem(place[orders[p][1]] + by, 4))[0])

    def second_sends(h):
        for p in range(3):
            opposite = ready(h, p, rem(place[orders[p][1]] + 2, 4))
            second_copy(h, p, 0, opposite).start()
            second_copy(h, p, 1, opposite).start()
        for p in range(3):
            second_copy(h, p, 2, ready(h, p, rem(place[orders[p][1]] + 1, 4))).start()
            second_copy(h, p, 3, ready(h, p, rem(place[orders[p][1]] + 3, 4))).start()

    def second_relays(h):
        for p in range(3):
            edge = CUTS[p]
            inbox = sides[h]["later"][p]
            for k, by, rows in ((0, 1, pl.ds(0, edge)), (1, 3, pl.ds(edge, PARTS[p][1] - edge))):
                what = block2(h, p, by)
                second_copy(h, p, k, what).wait_recv()
                accumulate(what.at[rows], inbox.at[0, rows])
                second_copy(h, p, 4 + k, what).start()
        for p in range(3):
            ready(h, p, place[orders[p][1]])

    chosen = c == rem(xh + y + z, 2)
    partner = device(2 * xh + 1 - xl, y, z, c)
    outward = device(rem(x + 3 + 2 * xl, 4), y, z, c)
    y_to = 2 * xl + rem(c + z + xh, 2)
    z_to = 2 * xl + rem(c + y + xh, 2)
    reach = ((1, 2, y_to, y, lambda: device(x, y_to, z, c)), (2, 5, z_to, z, lambda: device(x, y, z_to, c)))

    def third(h, src, dst, k, to):
        sems = sides[h]["sems"]
        return remote(src, dst, sems[8].at[k], sems[9].at[k], to)

    def mine(h, p):
        return block2(h, p, 0)

    def final(h, p):
        return sides[h]["F"].at[pl.ds(*PARTS[p]), :]

    def to_pair(h):
        return third(h, mine(h, 0), sides[h]["C"][0].at[0], 0, outward)

    def swap(h):
        return third(h, sides[h]["T1"], sides[h]["C"][0].at[1], 1, partner)

    def share(h, p):
        return third(h, final(h, p), final(h, p), 7 + p, partner)

    def hand(h):
        return third(h, sides[h]["F"], sides[h]["F"], 10, mate)

    def third_sends(h):
        for p in range(3):
            for k in range(2, 6):
                second_copy(h, p, k, mine(h, p)).wait_recv()
            accumulate(mine(h, p), sides[h]["later"][p].at[1], sides[h]["later"][p].at[2])
            if p == 0:
                @pl.when(jnp.logical_not(chosen))
                def _():
                    to_pair(h).start()
            else:
                _, base, to, at, where = reach[p - 1]
                for r in range(3):
                    @pl.when(rem(at - to + 4, 4) == r + 1)
                    def _():
                        third(h, mine(h, p), sides[h]["C"][p].at[r], base + r, where()).start()

    def third_sums(h):
        side = sides[h]

        @pl.when(chosen)
        def _():
            to_pair(h).wait_recv()
            side["T1"][...] = low(mine(h, 0)[...].astype(jnp.float32) + side["C"][0][0].astype(jnp.float32))
            swap(h).start()

        for p, base, to, at, where in reach:
            @pl.when(at == to)
            def _():
                total = mine(h, p)[...].astype(jnp.float32)
                for r in range(3):
                    third(h, mine(h, p), side["C"][p].at[r], base + r, mate).wait_recv()
                    total = total + side["C"][p][r].astype(jnp.float32)
                final(h, p)[...] = low(total)
                share(h, p).start()

    def finish(h):
        side = sides[h]

        @pl.when(chosen)
        def _():
            swap(h).wait_recv()
            final(h, 0)[...] = low(side["T1"][...].astype(jnp.float32) + side["C"][0][1].astype(jnp.float32))

        for p, base, to, at, where in reach:
            @pl.when(jnp.logical_and(chosen, at != to))
            def _():
                share(h, p).wait_recv()

        @pl.when(chosen)
        def _():
            hand(h).start()

    def write(h):
        @pl.when(jnp.logical_not(chosen))
        def _():
            hand(h).wait_recv()

        total = sides[h]["F"][...].astype(jnp.float32)
        qkv_out[:, spans[h][0] : spans[h][1]] = total[:Q_ROWS]
        out_out[:, spans[h][0] : spans[h][1]] = total[Q_ROWS:]

    def drain(h):
        for p in range(3):
            for to in range(2):
                for i in range(4):
                    whole_copy(h, p, to, i, sides[h]["wholes"][p].at[to, i]).wait_send()
                for i in range(2):
                    half_copy(h, p, to, i, sides[h]["halves"][p].at[to, i]).wait_send()
            for k in range(6):
                second_copy(h, p, k, mine(h, p)).wait_send()

        @pl.when(chosen)
        def _():
            swap(h).wait_send()
            hand(h).wait_send()

        @pl.when(jnp.logical_not(chosen))
        def _():
            to_pair(h).wait_send()

        for p, base, to, at, where in reach:
            @pl.when(at == to)
            def _():
                share(h, p).wait_send()

            for r in range(3):
                @pl.when(rem(at - to + 4, 4) == r + 1)
                def _():
                    third(h, mine(h, p), sides[h]["C"][p].at[r], base + r, where()).wait_send()

    weights(0, 0).start()
    produce(0)
    first_sends(0)
    produce(1)
    first_relays(0)
    first_sends(1)
    input_gradient()
    gain_start(0)
    second_sends(0)
    gain_end(0)
    gain_start(1)
    first_relays(1)
    gain_end(1)
    gain_start(2)
    second_relays(0)
    second_sends(1)
    third_sends(0)
    gain_end(2)
    gain_start(3)
    second_relays(1)
    third_sums(0)
    third_sends(1)
    finish(0)
    gain_end(3)
    third_sums(1)
    write(0)
    finish(1)
    write(1)
    drain(0)
    drain(1)


def reduce_call(gt, ct, lno, ao, x, cot, gain, w, factor):
    tok, cols = lno.shape
    dma = pltpu.SemaphoreType.DMA
    vm = pl.BlockSpec(memory_space=pltpu.VMEM)
    dim = gt.shape[1]
    scratch = [
        pltpu.VMEM((4, 4, 16, LANES), jnp.float32), dma((4, 3)), dma((4, 3)),
        pltpu.VMEM((2, 3, dim, cols), jnp.bfloat16), pltpu.VMEM((3 * LANES, cols), jnp.bfloat16),
        pltpu.VMEM((tok, cols), jnp.float32), pltpu.VMEM((1, cols), jnp.float32), dma((2,)),
    ]
    for lo, hi in column_halves(cols):
        bf = lambda *shape: pltpu.VMEM(shape + (hi - lo,), jnp.bfloat16)
        sizes = [size for _, size in PARTS]
        scratch += [bf(16, ROWS), bf(16, ROWS), bf(RING, ROWS)]
        scratch += [x for s in sizes for x in (bf(2, 2, s), bf(2, 4, s), bf(3, s))]
        scratch += [bf(2, sizes[0]), bf(3, sizes[1]), bf(3, sizes[2]), bf(sizes[0]), bf(ROWS)]
        scratch += [dma((16,))] * 2 + [dma((3, 2, 2))] * 2 + [dma((3, 2, 4))] * 2 + [dma((3, 6))] * 2 + [dma((11,))] * 2
    return pl.pallas_call(
        functools.partial(reduce_kernel, factor),
        out_shape=(
            jax.ShapeDtypeStruct((Q_ROWS, cols), jnp.float32),
            jax.ShapeDtypeStruct((ROWS - Q_ROWS, cols), jnp.float32),
            jax.ShapeDtypeStruct((cols,), jnp.float32),
            jax.ShapeDtypeStruct((tok, cols), jnp.bfloat16),
        ),
        in_specs=[vm] * 7 + [pl.BlockSpec(memory_space=pl.ANY)],
        out_specs=[vm] * 4,
        scratch_shapes=scratch,
        compiler_params=pltpu.CompilerParams(collective_id=0, has_side_effects=True, vmem_limit_bytes=63 * 2**20),
        cost_estimate=pl.CostEstimate(flops=2 * BLOCKS * ROWS * tok * cols, bytes_accessed=2**24, transcendentals=0),
    )(gt, ct, lno, ao, x, cot, gain, w)


def local(tokens, cotangent, ln_gain, w_qkv, w_out):
    images = tokens.shape[0] * lax.axis_size("wide") * lax.axis_size("narrow")
    factor = 1.0 / images
    x, cot = tokens[0], cotangent[0]
    ln_out, attn_out, grad_t, cot_t = front_call(x, cot, ln_gain, w_qkv, w_out)
    grad_t = grad_t.reshape(BLOCKS * 3 // 2, -1, cot.shape[0])
    w = w_qkv.reshape(3, HEADS, -1, cot.shape[1])
    grad_qkv, grad_out, gain, grad_input = reduce_call(grad_t, cot_t, ln_out, attn_out, x, cot, ln_gain, w, factor)
    return (grad_input[None], grad_qkv, grad_out, gain)


def solution(mesh):
    return jax.shard_map(
        local,
        mesh=mesh,
        in_specs=(
            P(("wide", "narrow"), None, None),
            P(("wide", "narrow"), None, None),
            P(),
            P(),
            P(),
        ),
        out_specs=(P(("wide", "narrow"), None, None), P("wide", None), P("wide", None), P()),
        check_vma=False,
    )
```

```python
import functools

import jax
import jax.numpy as jnp
from jax import lax
from jax.experimental import pallas as pl
from jax.experimental.pallas import tpu as pltpu
from jax.sharding import PartitionSpec as P

HEADS = 16


ln_epsilon = 1e-06


LANES = 128
WINDOW = 256
LOG2_E = 1.4426950408889634
TOGETHER = 4


def dot(a, b, over=((1,), (0,))):
    return lax.dot_general(a, b, (over, ((), ())), preferred_element_type=jnp.float32)


def low(a):
    return a.astype(jnp.bfloat16)


def normalise(x_ref):
    x = x_ref[...].astype(jnp.float32)
    centered = x - jnp.mean(x, axis=-1, keepdims=True)
    inv_sigma = lax.rsqrt(jnp.mean(centered * centered, axis=-1, keepdims=True) + ln_epsilon)
    return centered * inv_sigma, inv_sigma


def front_kernel(scale, x_ref, cot_ref, gain_ref, w_ref, wo_hbm,
                 lno_ref, ao_ref, gt_ref, ct_ref, wpad, wo_ref, wo_sem):
    h = pl.program_id(0)
    dim = w_ref.shape[2]
    fetch = pltpu.make_async_copy(wo_hbm, wo_ref, wo_sem)

    @pl.when(h == 0)
    def _():
        fetch.start()
        normed, _ = normalise(x_ref)
        lno_ref[...] = low(normed * gain_ref[...].reshape(1, -1))
        wpad[...] = jnp.zeros_like(wpad)

    pair = range(TOGETHER)
    for j in pair:
        for s in range(3):
            at = (3 * j + s) * LANES
            wpad[at : at + dim, :] = w_ref[s, j]
    qkv = low(dot(lno_ref[...], wpad[...], ((1,), (1,))))
    q, k, v = ([qkv[:, (3 * j + s) * LANES : (3 * j + s + 1) * LANES] for j in pair] for s in range(3))
    scores = [dot(q[j], k[j], ((1,), (1,))) for j in pair]

    lane = lax.broadcasted_iota(jnp.int32, (1, WINDOW), 1)
    starts = [jnp.minimum(lax.div((h * TOGETHER + j) * dim, LANES) * LANES, wo_ref.shape[1] - WINDOW) for j in pair]
    starts = [pl.multiple_of(start, LANES) for start in starts]
    offsets = [(h * TOGETHER + j) * dim - starts[j] for j in pair]
    @pl.when(h == 0)
    def _():
        fetch.wait()

    grad = [dot(cot_ref[...], wo_ref[:, pl.ds(starts[j], WINDOW)]) for j in pair]
    back = [lax.rem(WINDOW - offsets[j], WINDOW) for j in pair]
    grad = [pltpu.roll(grad[j], back[j], 1)[:, :LANES] for j in pair]
    grad = [low(jnp.where(lane[:, :LANES] < dim, grad[j], 0.0)) for j in pair]
    grad_prob = [dot(grad[j], v[j], ((1,), (1,))) for j in pair]

    prob = []
    for j in pair:
        expo = jnp.exp2((scores[j] - jnp.max(scores[j], axis=-1, keepdims=True)) * (scale * LOG2_E))
        prob.append(expo * (1.0 / jnp.sum(expo, axis=-1, keepdims=True)))
    prob_low = [low(prob[j]) for j in pair]
    attn = [dot(prob_low[j], v[j]) for j in pair]
    for j in pair:
        gt_ref[2, j] = low(dot(grad[j], prob_low[j], ((0,), (0,)))[:dim])

    grad_score = []
    for j in pair:
        inner = jnp.sum(grad_prob[j] * prob[j], axis=-1, keepdims=True)
        grad_score.append(low(prob[j] * (grad_prob[j] - inner) * scale))
    for j in pair:
        gt_ref[1, j] = low(dot(q[j], grad_score[j], ((0,), (0,)))[:dim])
        gt_ref[0, j] = low(dot(grad_score[j], k[j]).T[:dim])

    for j in pair:
        part = cot_ref[:, pl.ds(starts[j], WINDOW)].astype(jnp.float32)
        ct_ref[j] = low(pltpu.roll(part, back[j], 1)[:, :LANES].T[:dim])
        wide = pltpu.roll(jnp.concatenate([attn[j], jnp.zeros_like(attn[j])], axis=1), offsets[j], 1)
        window = ao_ref[:, pl.ds(starts[j], WINDOW)].astype(jnp.float32)
        inside = jnp.logical_and(lane >= offsets[j], lane < offsets[j] + dim)
        ao_ref[:, pl.ds(starts[j], WINDOW)] = low(jnp.where(inside, wide, window))


def front_call(x, cot, gain, w_qkv, w_out):
    tok, width = x.shape
    dim = width // HEADS
    whole = lambda a: pl.BlockSpec(a.shape, lambda h: (0,) * len(a.shape))
    w = w_qkv.reshape(3, HEADS, dim, width)
    outs = (
        jax.ShapeDtypeStruct((tok, width), jnp.bfloat16),
        jax.ShapeDtypeStruct((tok, width), jnp.bfloat16),
        jax.ShapeDtypeStruct((3, HEADS, dim, tok), jnp.bfloat16),
        jax.ShapeDtypeStruct((HEADS, dim, tok), jnp.bfloat16),
    )
    return pl.pallas_call(
        functools.partial(front_kernel, dim**-0.5),
        grid=(HEADS // TOGETHER,),
        out_shape=outs,
        in_specs=[whole(x), whole(cot), whole(gain), pl.BlockSpec((3, TOGETHER, dim, width), lambda h: (0, h, 0, 0)), pl.BlockSpec(memory_space=pl.ANY)],
        out_specs=[whole(outs[0]), whole(outs[1]), pl.BlockSpec((3, TOGETHER, dim, tok), lambda h: (0, h, 0, 0)),
                   pl.BlockSpec((TOGETHER, dim, tok), lambda h: (h, 0, 0))],
        scratch_shapes=[pltpu.VMEM((TOGETHER * 3 * LANES, width), jnp.bfloat16), pltpu.VMEM(w_out.shape, jnp.bfloat16), pltpu.SemaphoreType.DMA],
        compiler_params=pltpu.CompilerParams(vmem_limit_bytes=56 * 2**20, dimension_semantics=("arbitrary",)),
        cost_estimate=pl.CostEstimate(flops=12 * 10**9, bytes_accessed=26 * 2**20, transcendentals=HEADS * tok * tok),
    )(x, cot, gain, w, w_out)


BLOCKS = 32
ROWS = 208
Q_ROWS = 156
PARTS = ((0, 80), (80, 64), (144, 64))
CUTS = (48, 32, 32)
RING = 6
LAG = 4
MESH = pl.DeviceIdType.MESH


def rem(a, b):
    return lax.rem(a, jnp.int32(b))


def div(a, b):
    return lax.div(a, jnp.int32(b))


def column_halves(cols):
    edge = (cols // LANES + 1) // 2 * LANES
    return ((0, edge), (edge, cols))


def reduce_kernel(factor, gt, ct, lno, ao, x_ref, cot_ref, gain_ref, w_hbm, qkv_out, out_out, gain_out, gx_ref,
                  G, sg, rg, wbuf, wpad, gln, row, wsem, *scratch):
    cols = lno.shape[1]
    spans = column_halves(cols)
    per = len(scratch) // 2
    sides = []
    for h in range(2):
        s = scratch[h * per : (h + 1) * per]
        sides.append(dict(S=s[0], R0=s[1], T0=s[2], halves=(s[3], s[6], s[9]), wholes=(s[4], s[7], s[10]),
                          later=(s[5], s[8], s[11]), C=s[12:15], T1=s[15], F=s[16], sems=s[17:27]))

    wide, narrow = lax.axis_index("wide"), lax.axis_index("narrow")
    xh, y, z = div(wide, 16), rem(div(wide, 4), 4), rem(wide, 4)
    xl, c = div(narrow, 2), rem(narrow, 2)
    x = 2 * xh + xl
    place = (x, y, z)

    def device(x_, y_, z_, c_):
        return (div(x_, 2) * 16 + y_ * 4 + z_, rem(x_, 2) * 2 + c_)

    def shift(dim, by):
        at = [x, y, z]
        at[dim] = rem(at[dim] + by, 4)
        return device(*at, c)

    mate = device(x, y, z, 1 - c)
    peers = [mate] + [shift(d, by) for d in range(3) for by in (1, 2, 3)]
    barrier = pltpu.get_barrier_semaphore()
    for peer in peers:
        pl.semaphore_signal(barrier, inc=1, device_id=peer, device_id_type=MESH)
    pl.semaphore_wait(barrier, len(peers))

    def remote(src, dst, ssem, rsem, to):
        return pltpu.make_async_remote_copy(src_ref=src, dst_ref=dst, send_sem=ssem, recv_sem=rsem,
                                            device_id=to, device_id_type=MESH)

    def accumulate(dst, *more):
        total = dst[...].astype(jnp.float32)
        for term in more:
            total = total + term[...].astype(jnp.float32)
        dst[...] = total.astype(jnp.bfloat16)

    rings = ((2, c, lambda r: mate), (4, x, lambda r: shift(0, r)), (4, y, lambda r: shift(1, r)), (4, z, lambda r: shift(2, r)))
    gain_copies = []

    def gain_start(k):
        n, m, to = rings[k]
        if k == 0:
            G[k, m] = jnp.zeros(G.shape[2:], jnp.float32)
            for i in range(cols // LANES):
                G[k, m, i : i + 1, :] = row[:, i * LANES : (i + 1) * LANES]
        else:
            G[k, m] = gain_total(k - 1)
        for r in range(n - 1):
            copy = remote(G.at[k, m], G.at[k, m], sg.at[k, r], rg.at[k, r], to(r + 1))
            copy.start()
            gain_copies.append(copy)

    def gain_total(k):
        total = G[k, 0]
        for other in range(1, rings[k][0]):
            total = total + G[k, other]
        return total

    def gain_end(k):
        while gain_copies:
            gain_copies.pop().wait()
        if k == 3:
            total = gain_total(k) * factor
            for i in range(cols // LANES):
                gain_out[i * LANES : (i + 1) * LANES] = total[i]

    def weights(h, slot):
        return pltpu.make_async_copy(w_hbm.at[:, h], wbuf.at[slot], wsem.at[slot])

    def input_gradient():
        dim = gt.shape[1]
        gln[...] = jnp.zeros_like(gln)
        wpad[...] = jnp.zeros_like(wpad)

        @pl.loop(0, HEADS // 2)
        def _(n):
            pad = jnp.zeros((LANES - dim, gt.shape[2]), jnp.float32)
            stack = []
            for slot in range(2):
                weights(2 * n + slot, slot).wait()
                for s in range(3):
                    at = (3 * slot + s) * LANES
                    wpad[at : at + dim, :] = wbuf[slot, s]
                    stack += [gt[s * HEADS + 2 * n + slot].astype(jnp.float32), pad]

                @pl.when(n < HEADS // 2 - 1)
                def _():
                    weights(2 * n + 2 + slot, slot).start()

            gln[...] += dot(low(jnp.concatenate(stack, axis=0).T), wpad[...])

        normed, inv_sigma = normalise(x_ref)
        grad_ln = gln[...]
        row[...] = jnp.sum(grad_ln * normed, axis=0, keepdims=True)
        g = grad_ln * gain_ref[...].reshape(1, -1)
        grad_x = inv_sigma * (
            g - jnp.mean(g, axis=-1, keepdims=True) - normed * jnp.mean(g * normed, axis=-1, keepdims=True)
        )
        gx_ref[...] = low(cot_ref[...].astype(jnp.float32) + grad_x)

    def rows_of_pair(b):
        g = jnp.concatenate([gt[3 * b + i].astype(jnp.float32) for i in range(3)], axis=0)
        d = ct[b].astype(jnp.float32)
        out_rows = ROWS - Q_ROWS
        return tuple(
            jnp.concatenate([g[i * Q_ROWS : (i + 1) * Q_ROWS], d[i * out_rows : (i + 1) * out_rows]], axis=0)
            for i in range(2)
        )

    def product(left, right, lo, hi):
        full = right.shape[0] // 256 * 256
        total = dot(low(left[:, :full]), right[0:full, lo:hi])
        for k in range(full, right.shape[0]):
            total = total + left[:, k : k + 1] * right[k : k + 1, lo:hi].astype(jnp.float32)
        return total * factor

    def block_at(side, b):
        return side["S"].at[div(b, 8), rem(div(b, 4), 2), rem(div(b, 2), 2), rem(b, 2)]

    def fill(side, span, b, slot):
        even, odd = rows_of_pair(b)
        mine_odd = rem(c + div(b, 8) + rem(div(b, 2), 4), 2) == 1
        give, keep = jnp.where(mine_odd, even, odd), jnp.where(mine_odd, odd, even)
        first = jnp.concatenate([give[0:160], keep[0:160]], axis=0)
        last = jnp.concatenate([give[144:208], keep[144:208]], axis=0)
        line = lax.broadcasted_iota(jnp.int32, (16, 1), 0)
        width = span[1] - span[0]
        for lo in range(0, width, 512):
            hi = min(width, lo + 512)
            p = product(first, lno, span[0] + lo, span[0] + hi)
            q = product(last, ao, span[0] + lo, span[0] + hi)
            for k, dst in ((0, side["T0"].at[slot]), (1, block_at(side, b))):
                u, v = p[160 * k : 160 * k + 160], q[64 * k : 64 * k + 64]
                dst[0:144, lo:hi] = low(u[0:144])
                dst[144:160, lo:hi] = low(jnp.where(line < Q_ROWS - 144, u[144:160], v[0:16]))
                dst[160:208, lo:hi] = low(v[16:64])

    def core_copy(side, b, slot):
        return remote(side["T0"].at[slot], side["R0"].at[b], side["sems"][0].at[b], side["sems"][1].at[b], mate)

    def produce(h):
        side = sides[h]

        @pl.loop(0, 16 + LAG)
        def _(n):
            @pl.when(n < 16)
            def _():
                slot = rem(n, RING)

                @pl.when(n >= RING)
                def _():
                    core_copy(side, n - RING, slot).wait_send()

                fill(side, spans[h], n, slot)
                core_copy(side, n, slot).start()

            @pl.when(n >= LAG)
            def _():
                b = n - LAG
                core_copy(side, b, 0).wait_recv()
                accumulate(block_at(side, b), side["R0"].at[b])

        for n in range(16 - RING, 16):
            core_copy(side, n, n % RING).wait_send()

    orders = ((1, 2, 0), (2, 0, 1), (0, 1, 2))
    firsts = (
        lambda t, i: (i // 2) * 8 + t * 2 + i % 2,
        lambda t, i: (i // 2) * 8 + (2 * (i % 2) + rem(c + t + i // 2, 2)) * 2 + div(t, 2),
        lambda t, i: div(t, 2) * 8 + i * 2 + rem(t, 2),
    )
    seconds = (
        lambda t: (rem(c + y + t, 2) * 8 + y * 2 + div(t, 2), rem(c + y + t, 2) * 2 + div(t, 2)),
        lambda t: (div(t, 2) * 8 + (2 * rem(t, 2) + rem(c + z + div(t, 2), 2)) * 2 + div(z, 2), t),
        lambda t: (div(x, 2) * 8 + t * 2 + rem(x, 2), t),
    )

    def part(h, p, b):
        return block_at(sides[h], b).at[pl.ds(*PARTS[p]), :]

    def two(h, p, t, g):
        rows = pl.ds(*PARTS[p])
        t_hi, t_lo = div(t, 2), rem(t, 2)
        if p == 0:
            return sides[h]["S"].at[g, t_hi, t_lo, :, rows, :]
        if p == 1:
            return sides[h]["S"].at[g, :, rem(c + t + g, 2), t_hi, rows, :]
        return sides[h]["S"].at[t_hi, g, :, t_lo, rows, :]

    def half_copy(h, p, to, src):
        sems = sides[h]["sems"]
        return remote(src, sides[h]["halves"][p].at[to], sems[2].at[p, to], sems[3].at[p, to],
                      shift(orders[p][0], 1 + 2 * to))

    def whole_copy(h, p, to, g, src):
        sems = sides[h]["sems"]
        return remote(src, sides[h]["wholes"][p].at[to, pl.ds(2 * g, 2)], sems[4].at[p, to, g], sems[5].at[p, to, g],
                      shift(orders[p][0], 1 + 2 * to))

    def any_whole(h, p, to, g):
        return whole_copy(h, p, to, g, sides[h]["wholes"][p].at[to, pl.ds(2 * g, 2)])

    six = [(p, to) for to in range(2) for p in range(3)]

    def first_sends(h):
        for p, to in six:
            half_copy(h, p, to, two(h, p, rem(place[orders[p][0]] + 2, 4), to)).start()
        for p, to in six:
            t = rem(place[orders[p][0]] + 1 + 2 * to, 4)
            whole_copy(h, p, to, 1 - to, two(h, p, t, 1 - to)).start()

    def first_relays(h):
        for p, to in six:
            halves = sides[h]["halves"][p]
            half_copy(h, p, to, halves.at[to]).wait_recv()
            t = rem(place[orders[p][0]] + 1 + 2 * to, 4)
            for i in range(2):
                accumulate(part(h, p, firsts[p](t, i + 2 * to)), halves.at[to, i])
            whole_copy(h, p, to, to, two(h, p, t, to)).start()

    def ready(h, p, t):
        b, i = seconds[p](t)
        wholes = sides[h]["wholes"][p]
        accumulate(part(h, p, b), wholes.at[0, i], wholes.at[1, i])
        return part(h, p, b)

    def second_copy(h, p, k, what):
        edge = CUTS[p]
        lower, upper = pl.ds(0, edge), pl.ds(edge, PARTS[p][1] - edge)
        rows, slot, by = ((lower, 0, 1), (upper, 0, 3), (upper, 1, 1), (lower, 2, 3), (lower, 1, 1), (upper, 2, 3))[k]
        sems = sides[h]["sems"]
        return remote(what.at[rows], sides[h]["later"][p].at[slot, rows], sems[6].at[p, k], sems[7].at[p, k],
                      shift(orders[p][1], by))

    def block2(h, p, by):
        return part(h, p, seconds[p](rem(place[orders[p][1]] + by, 4))[0])

    def second_sends(h):
        for p in range(3):
            for to in range(2):
                for g in range(2):
                    any_whole(h, p, to, g).wait_recv()
            opposite = ready(h, p, rem(place[orders[p][1]] + 2, 4))
            second_copy(h, p, 0, opposite).start()
            second_copy(h, p, 1, opposite).start()
        for p in range(3):
            second_copy(h, p, 2, ready(h, p, rem(place[orders[p][1]] + 1, 4))).start()
            second_copy(h, p, 3, ready(h, p, rem(place[orders[p][1]] + 3, 4))).start()

    def second_relays(h):
        for p in range(3):
            edge = CUTS[p]
            inbox = sides[h]["later"][p]
            for k, by, rows in ((0, 1, pl.ds(0, edge)), (1, 3, pl.ds(edge, PARTS[p][1] - edge))):
                what = block2(h, p, by)
                second_copy(h, p, k, what).wait_recv()
                accumulate(what.at[rows], inbox.at[0, rows])
                second_copy(h, p, 4 + k, what).start()
        for p in range(3):
            ready(h, p, place[orders[p][1]])

    chosen = c == rem(xh + y + z, 2)
    partner = device(2 * xh + 1 - xl, y, z, c)
    outward = device(rem(x + 3 + 2 * xl, 4), y, z, c)
    y_to = 2 * xl + rem(c + z + xh, 2)
    z_to = 2 * xl + rem(c + y + xh, 2)
    reach = ((1, 2, y_to, y, lambda: device(x, y_to, z, c)), (2, 5, z_to, z, lambda: device(x, y, z_to, c)))

    def third(h, src, dst, k, to):
        sems = sides[h]["sems"]
        return remote(src, dst, sems[8].at[k], sems[9].at[k], to)

    def mine(h, p):
        return block2(h, p, 0)

    def final(h, p):
        return sides[h]["F"].at[pl.ds(*PARTS[p]), :]

    def to_pair(h):
        return third(h, mine(h, 0), sides[h]["C"][0].at[0], 0, outward)

    def swap(h):
        return third(h, sides[h]["T1"], sides[h]["C"][0].at[1], 1, partner)

    def share(h, p):
        return third(h, final(h, p), final(h, p), 7 + p, partner)

    def hand(h):
        return third(h, sides[h]["F"], sides[h]["F"], 10, mate)

    def third_sends(h):
        for p in range(3):
            for k in range(2, 6):
                second_copy(h, p, k, mine(h, p)).wait_recv()
            accumulate(mine(h, p), sides[h]["later"][p].at[1], sides[h]["later"][p].at[2])
            if p == 0:
                @pl.when(jnp.logical_not(chosen))
                def _():
                    to_pair(h).start()
            else:
                _, base, to, at, where = reach[p - 1]
                for r in range(3):
                    @pl.when(rem(at - to + 4, 4) == r + 1)
                    def _():
                        third(h, mine(h, p), sides[h]["C"][p].at[r], base + r, where()).start()

    def third_sums(h):
        side = sides[h]

        @pl.when(chosen)
        def _():
            to_pair(h).wait_recv()
            side["T1"][...] = low(mine(h, 0)[...].astype(jnp.float32) + side["C"][0][0].astype(jnp.float32))
            swap(h).start()

        for p, base, to, at, where in reach:
            @pl.when(at == to)
            def _():
                total = mine(h, p)[...].astype(jnp.float32)
                for r in range(3):
                    third(h, mine(h, p), side["C"][p].at[r], base + r, mate).wait_recv()
                    total = total + side["C"][p][r].astype(jnp.float32)
                final(h, p)[...] = low(total)
                share(h, p).start()

    def finish(h):
        side = sides[h]

        @pl.when(chosen)
        def _():
            swap(h).wait_recv()
            final(h, 0)[...] = low(side["T1"][...].astype(jnp.float32) + side["C"][0][1].astype(jnp.float32))

        for p, base, to, at, where in reach:
            @pl.when(jnp.logical_and(chosen, at != to))
            def _():
                share(h, p).wait_recv()

        @pl.when(chosen)
        def _():
            hand(h).start()

    def write(h):
        @pl.when(jnp.logical_not(chosen))
        def _():
            hand(h).wait_recv()

        total = sides[h]["F"][...].astype(jnp.float32)
        qkv_out[:, spans[h][0] : spans[h][1]] = total[:Q_ROWS]
        out_out[:, spans[h][0] : spans[h][1]] = total[Q_ROWS:]

    def drain(h):
        for p in range(3):
            for to in range(2):
                for g in range(2):
                    any_whole(h, p, to, g).wait_send()
                half_copy(h, p, to, sides[h]["halves"][p].at[to]).wait_send()
            for k in range(6):
                second_copy(h, p, k, mine(h, p)).wait_send()

        @pl.when(chosen)
        def _():
            swap(h).wait_send()
            hand(h).wait_send()

        @pl.when(jnp.logical_not(chosen))
        def _():
            to_pair(h).wait_send()

        for p, base, to, at, where in reach:
            @pl.when(at == to)
            def _():
                share(h, p).wait_send()

            for r in range(3):
                @pl.when(rem(at - to + 4, 4) == r + 1)
                def _():
                    third(h, mine(h, p), sides[h]["C"][p].at[r], base + r, where()).wait_send()

    weights(0, 0).start()
    weights(1, 1).start()
    produce(0)
    first_sends(0)
    produce(1)
    first_relays(0)
    first_sends(1)
    input_gradient()
    gain_start(0)
    second_sends(0)
    gain_end(0)
    gain_start(1)
    first_relays(1)
    gain_end(1)
    gain_start(2)
    second_relays(0)
    second_sends(1)
    third_sends(0)
    gain_end(2)
    gain_start(3)
    second_relays(1)
    third_sums(0)
    third_sends(1)
    finish(0)
    gain_end(3)
    third_sums(1)
    write(0)
    finish(1)
    write(1)
    drain(0)
    drain(1)


def reduce_call(gt, ct, lno, ao, x, cot, gain, w, factor):
    tok, cols = lno.shape
    dma = pltpu.SemaphoreType.DMA
    vm = pl.BlockSpec(memory_space=pltpu.VMEM)
    dim = gt.shape[1]
    scratch = [
        pltpu.VMEM((4, 4, 16, LANES), jnp.float32), dma((4, 3)), dma((4, 3)),
        pltpu.VMEM((2, 3, dim, cols), jnp.bfloat16), pltpu.VMEM((6 * LANES, cols), jnp.bfloat16),
        pltpu.VMEM((tok, cols), jnp.float32), pltpu.VMEM((1, cols), jnp.float32), dma((2,)),
    ]
    for lo, hi in column_halves(cols):
        bf = lambda *shape: pltpu.VMEM(shape + (hi - lo,), jnp.bfloat16)
        sizes = [size for _, size in PARTS]
        scratch += [bf(2, 2, 2, 2, ROWS), bf(16, ROWS), bf(RING, ROWS)]
        scratch += [x for s in sizes for x in (bf(2, 2, s), bf(2, 4, s), bf(3, s))]
        scratch += [bf(2, sizes[0]), bf(3, sizes[1]), bf(3, sizes[2]), bf(sizes[0]), bf(ROWS)]
        scratch += [dma((16,))] * 2 + [dma((3, 2))] * 2 + [dma((3, 2, 2))] * 2 + [dma((3, 6))] * 2 + [dma((11,))] * 2
    return pl.pallas_call(
        functools.partial(reduce_kernel, factor),
        out_shape=(
            jax.ShapeDtypeStruct((Q_ROWS, cols), jnp.float32),
            jax.ShapeDtypeStruct((ROWS - Q_ROWS, cols), jnp.float32),
            jax.ShapeDtypeStruct((cols,), jnp.float32),
            jax.ShapeDtypeStruct((tok, cols), jnp.bfloat16),
        ),
        in_specs=[vm] * 7 + [pl.BlockSpec(memory_space=pl.ANY)],
        out_specs=[vm] * 4,
        scratch_shapes=scratch,
        compiler_params=pltpu.CompilerParams(collective_id=0, has_side_effects=True, vmem_limit_bytes=63 * 2**20),
        cost_estimate=pl.CostEstimate(flops=2 * BLOCKS * ROWS * tok * cols, bytes_accessed=2**24, transcendentals=0),
    )(gt, ct, lno, ao, x, cot, gain, w)


def local(tokens, cotangent, ln_gain, w_qkv, w_out):
    images = tokens.shape[0] * lax.axis_size("wide") * lax.axis_size("narrow")
    factor = 1.0 / images
    x, cot = tokens[0], cotangent[0]
    ln_out, attn_out, grad_t, cot_t = front_call(x, cot, ln_gain, w_qkv, w_out)
    grad_t = grad_t.reshape(BLOCKS * 3 // 2, -1, cot.shape[0])
    w = w_qkv.reshape(3, HEADS, -1, cot.shape[1])
    grad_qkv, grad_out, gain, grad_input = reduce_call(grad_t, cot_t, ln_out, attn_out, x, cot, ln_gain, w, factor)
    return (grad_input[None], grad_qkv, grad_out, gain)


def solution(mesh):
    return jax.shard_map(
        local,
        mesh=mesh,
        in_specs=(
            P(("wide", "narrow"), None, None),
            P(("wide", "narrow"), None, None),
            P(),
            P(),
            P(),
        ),
        out_specs=(P(("wide", "narrow"), None, None), P("wide", None), P("wide", None), P()),
        check_vma=False,
    )
```
